32 devices in a mesh: wide: 8 (over z, x), narrow: 4 (over y, core).
Axes of the slice: x: 2, y: 2, z: 4, core: 2. Of those that a mesh axis runs over, the one named last changes fastest.
Arguments:
- latents: bfloat16 [8, 3840, 384], P('wide', 'narrow'), may hold values from -6 to 6
- cotangent: bfloat16 [8, 3840, 384], P('wide', 'narrow'), may hold values from -8 to 8
- bucket: int32 [8], P('wide'), may hold values from 0 to 1, as said below
- pixel_mask: int32 [8, 3840], P('wide'), may hold values from 0 to 1, as said below
- labels: int32 [8], P('wide'), may hold values from 0 to 999
- timesteps: int32 [8], P('wide'), may hold values from 0 to 999
- gain_first: bfloat16 [384], replicated, may hold values from 0.25 to 1.75
- conv_first: bfloat16 [3456, 384], replicated, may hold values from -0.109375 to 0.109375
- time_proj: bfloat16 [768, 384], replicated, may hold values from -0.21875 to 0.21875
- gain_second: bfloat16 [384], replicated, may hold values from 0.25 to 1.75
- conv_second: bfloat16 [3456, 384], replicated, may hold values from -0.109375 to 0.109375
- gain_spatial: bfloat16 [384], replicated, may hold values from 0.25 to 1.75
- proj_in: bfloat16 [384, 384], replicated, may hold values from -0.3125 to 0.3125
- gain_attn: bfloat16 [384], replicated, may hold values from 0.25 to 1.75
- attn_qkv: bfloat16 [384, 1152], replicated, may hold values from -0.3125 to 0.3125
- attn_out: bfloat16 [384, 384], replicated, may hold values from -8 to 8
- class_table: bfloat16 [1000, 512], replicated, may hold values from -6 to 6
- cross_value: bfloat16 [512, 384], replicated, may hold values from -0.25 to 0.25
- cross_out: bfloat16 [384, 384], replicated, may hold values from -0.3125 to 0.3125
- gain_ff: bfloat16 [384], replicated, may hold values from 0.25 to 1.75
- geglu_in: bfloat16 [384, 3072], replicated, may hold values from -0.3125 to 0.3125
- geglu_out: bfloat16 [1536, 384], replicated, may hold values from -0.15625 to 0.15625
- proj_out: bfloat16 [384, 384], replicated, may hold values from -0.3125 to 0.3125
Outputs:
- output: bfloat16 [8, 3840, 384], P('wide', 'narrow')
- grad_latents: bfloat16 [8, 3840, 384], P('wide', 'narrow')
- grad_gain_first: float32 [384], P('wide')
- grad_conv_first: float32 [3456, 384], P(None, 'wide')
- grad_time_proj: float32 [768, 384], P(None, 'wide')
- grad_gain_second: float32 [384], P('wide')
- grad_conv_second: float32 [3456, 384], P(None, 'wide')
- grad_gain_spatial: float32 [384], P('wide')
- grad_proj_in: float32 [384, 384], P(None, 'wide')
- grad_gain_attn: float32 [384], P('wide')
- grad_attn_qkv: float32 [384, 768], P(None, 'wide')
- grad_attn_value: float32 [384, 384], P(None, 'wide')
- grad_attn_out: float32 [384, 384], P(None, 'wide')
- grad_class_table: float32 [1000, 512], P(None, 'wide')
- grad_cross_value: float32 [512, 384], P(None, 'wide')
- grad_cross_out: float32 [384, 384], P(None, 'wide')
- grad_gain_ff: float32 [384], P('wide')
- grad_geglu_in: float32 [384, 3072], P(None, 'wide')
- grad_geglu_out: float32 [1536, 384], P(None, 'wide')
- grad_proj_out: float32 [384, 384], P(None, 'wide')
The draws below stay inside these ranges and needn't reach their ends.
Inputs may be any that keep to these rules, and one draw needn't show every extreme that they name: `bucket`: 0: the image's grid is 48 rows of 80 pixels; 1: 80 rows of 48 pixels. `pixel_mask`: an image's real pixels are the first r rows and first c columns of its grid, every image has all rows of its grid; its real columns are the first c, c at least half of the grid's columns.
All inputs are finite; a program needn't handle non-finite values.
Results may differ from the reference program's by a relative error of at most 0.014.
Values may be sent and summed in bfloat16 or wider, within the bound.
No kernel may reach another device: no remote copies, remote signals or barrier semaphores. Data moves between devices by JAX's collectives and lax.ppermute only.
A program may use at most 256 MiB of HBM per device.

```python
import math
import jax
import jax.numpy as jnp
from jax import lax

C = 384
HEADS = 12
HEAD_DIM = 32
GROUPS = 32
FF = 1536
CTX = 512
TEMB = 768
NCLASS = 1000
SHORT = 48
LONG = 80
QBLOCK = 768
IMG_DEV = 1
PIX = 3840
IMAGES = 8


def shape_draw(key):
    bucket_key, rows_key, cols_key, pick_key = jax.random.split(key, 4)
    bucket_ids = jax.random.randint(bucket_key, (IMAGES,), 0, 2).astype(jnp.int32)
    grid_rows = jnp.where(bucket_ids == 0, SHORT, LONG).astype(jnp.int32)
    grid_cols = jnp.where(bucket_ids == 0, LONG, SHORT).astype(jnp.int32)
    least_rows = (grid_rows + 1) // 2
    least_cols = (grid_cols + 1) // 2
    rows_draw = jax.random.randint(rows_key, (IMAGES,), 0, 1 << 20).astype(jnp.int32)
    cols_draw = jax.random.randint(cols_key, (IMAGES,), 0, 1 << 20).astype(jnp.int32)
    real_rows = least_rows + rows_draw % (grid_rows - least_rows + 1)
    real_cols = least_cols + cols_draw % (grid_cols - least_cols + 1)
    chosen = jax.random.randint(pick_key, (IMAGES // IMG_DEV,), 0, IMG_DEV).astype(jnp.int32)
    image_index = jnp.arange(IMAGES, dtype=jnp.int32)
    whole_rows = image_index % IMG_DEV == chosen[image_index // IMG_DEV]
    real_rows = jnp.where(whole_rows, grid_rows, real_rows)
    pixels = jnp.arange(PIX, dtype=jnp.int32)[None, :]
    row_of = pixels // grid_cols[:, None]
    col_of = pixels % grid_cols[:, None]
    pixel_keep = ((row_of < real_rows[:, None]) & (col_of < real_cols[:, None])).astype(jnp.int32)
    return (bucket_ids, pixel_keep)


def draw_bucket(key, part):
    return shape_draw(key)[0]


def draw_pixel_mask(key, part):
    return shape_draw(key)[1]


def draw_cotangent(key, part):
    key = jax.random.fold_in(key, 11)
    noise_key, common_key, image_key = jax.random.split(key, 3)
    position = jnp.arange(PIX, dtype=jnp.float32) / PIX
    rise = 4.0 ** position
    noise = jax.random.normal(noise_key, (IMAGES, PIX, C), jnp.float32)
    common = jax.random.normal(common_key, (IMAGES, 1, C), jnp.float32)
    image_scale = jnp.exp(jax.random.uniform(image_key, (IMAGES, 1, 1), jnp.float32, -0.5, 0.5))
    values = 0.6 * image_scale * rise[None, :, None] * (noise + common)
    return jnp.clip(values, -8.0, 8.0).astype(jnp.bfloat16)


def set_ends(array, stream_key, least, top_value):
    index_at = [jax.random.randint(jax.random.fold_in(stream_key, axis), (), 0, length) for axis, length in enumerate(array.shape)]
    longest = array.shape.index(max(array.shape))
    beside = index_at[:longest] + [(index_at[longest] + 1) % array.shape[longest]] + index_at[longest + 1:]
    return array.at[tuple(index_at)].set(least).at[tuple(beside)].set(top_value)


def block_scale(key, extent, cuts, low, high):
    loudness = 1.0
    for dim, shards_of in cuts:
        draws = jax.random.uniform(jax.random.fold_in(jax.random.fold_in(key, 6), dim), (shards_of,), jnp.float32, low / len(cuts), high / len(cuts))
        loudness = loudness * jnp.repeat(jnp.exp(draws), extent[dim] // shards_of).reshape((-1,) + (1,) * (len(extent) - 1 - dim))
    return loudness


def scatter_about(stream_key, shape, width, reach, cuts=(), held_as=jnp.bfloat16):
    loudness = block_scale(stream_key, shape, cuts, -0.22, 0.18) if cuts else 1.0
    values = jax.random.normal(stream_key, shape, jnp.float32) * width * loudness
    return jnp.minimum(jnp.maximum(values, -reach), reach).astype(held_as)


def setup_inputs(seed: int = 0) -> dict:
    arg_keys = jax.random.split(jax.random.key(seed), 24)
    return {
        "latents": scatter_about(arg_keys[0], (IMAGES, PIX, C), 1.0, 6.0, ((0, 8), (1, 4))),
        "cotangent": draw_cotangent(jax.random.fold_in(arg_keys[23], 71), 0),
        "bucket": draw_bucket(jax.random.fold_in(arg_keys[23], 71), 0),
        "pixel_mask": draw_pixel_mask(jax.random.fold_in(arg_keys[23], 71), 0),
        "labels": set_ends(jax.random.randint(arg_keys[4], (IMAGES,), 0, NCLASS), jax.random.fold_in(arg_keys[4], 1), 0, NCLASS - 1).astype(jnp.int32),
        "timesteps": set_ends(jax.random.randint(arg_keys[5], (IMAGES,), 0, 1000), jax.random.fold_in(arg_keys[5], 1), 0, 999).astype(jnp.int32),
        "gain_first": jnp.clip(1.0 + 0.15 * jax.random.normal(arg_keys[6], (C,), jnp.float32), 0.25, 1.75).astype(jnp.bfloat16),
        "conv_first": scatter_about(arg_keys[7], (9 * C, C), (9 * C) ** -0.5, 0.109375),
        "time_proj": scatter_about(arg_keys[8], (TEMB, C), TEMB ** -0.5, 0.21875),
        "gain_second": jnp.clip(1.0 + 0.15 * jax.random.normal(arg_keys[9], (C,), jnp.float32), 0.25, 1.75).astype(jnp.bfloat16),
        "conv_second": scatter_about(arg_keys[10], (9 * C, C), (9 * C) ** -0.5, 0.109375),
        "gain_spatial": jnp.clip(1.0 + 0.15 * jax.random.normal(arg_keys[11], (C,), jnp.float32), 0.25, 1.75).astype(jnp.bfloat16),
        "proj_in": scatter_about(arg_keys[12], (C, C), C ** -0.5, 0.3125),
        "gain_attn": jnp.clip(1.0 + 0.15 * jax.random.normal(arg_keys[13], (C,), jnp.float32), 0.25, 1.75).astype(jnp.bfloat16),
        "attn_qkv": scatter_about(arg_keys[14], (C, 3 * C), C ** -0.5, 0.3125),
        "attn_out": scatter_about(arg_keys[15], (C, C), ((PIX / (6.0 * C)) ** 0.5), 8.0),
        "class_table": scatter_about(arg_keys[16], (NCLASS, CTX), 1.0, 6.0),
        "cross_value": scatter_about(arg_keys[17], (CTX, C), CTX ** -0.5, 0.25),
        "cross_out": scatter_about(arg_keys[18], (C, C), C ** -0.5, 0.3125),
        "gain_ff": jnp.clip(1.0 + 0.15 * jax.random.normal(arg_keys[19], (C,), jnp.float32), 0.25, 1.75).astype(jnp.bfloat16),
        "geglu_in": scatter_about(arg_keys[20], (C, 2 * FF), C ** -0.5, 0.3125),
        "geglu_out": scatter_about(arg_keys[21], (FF, C), FF ** -0.5, 0.15625),
        "proj_out": scatter_about(arg_keys[22], (C, C), C ** -0.5, 0.3125),
    }


HIGH = lax.Precision.HIGHEST
EPS_GROUP = 1e-06
EPS_LAYER = 1e-05
MASKED = -1e+30

@jax.custom_vjp
def low(v):
    return lax.optimization_barrier(v.astype(jnp.bfloat16)).astype(jnp.float32)

@jax.custom_vjp
def low_back(v):
    return v

def low_keep(v):
    return (low(v), None)

def low_pass(kept, grad):
    return (grad,)

def back_keep(v):
    return (v, None)

def back_low(kept, grad):
    return (low(grad),)
low.defvjp(low_keep, low_pass)
low_back.defvjp(back_keep, back_low)

def matmul(left, right):
    return jnp.dot(left, right, precision=HIGH, preferred_element_type=jnp.float32)

def tap_stack(padded, wide_rows, column, row_width, pix_count):
    pieces = []
    offset = LONG + 1
    for shift_y in (-1, 0, 1):
        for shift_x in (-1, 0, 1):
            long_start = offset + shift_y * LONG + shift_x
            short_start = offset + shift_y * SHORT + shift_x
            long_piece = lax.slice_in_dim(padded, long_start, long_start + pix_count, axis=0)
            short_piece = lax.slice_in_dim(padded, short_start, short_start + pix_count, axis=0)
            chosen = jnp.where(wide_rows, long_piece, short_piece)
            inside = (column + shift_x >= 0) & (column + shift_x < row_width)
            pieces.append(jnp.where(inside, chosen, jnp.zeros_like(chosen)))
    return jnp.concatenate(pieces, axis=1)

def convolve(field_in, weight, wide_rows, column, row_width):
    padded = jnp.pad(field_in, ((LONG + 1, LONG + 1), (0, 0)))
    return matmul(tap_stack(padded, wide_rows, column, row_width, PIX), weight)

def group_norm(field_in, gain, keep_col, counts):
    group_size = C // GROUPS
    masked = field_in * keep_col
    sum_first = lax.optimization_barrier(jnp.sum(masked.reshape(PIX, GROUPS, group_size), axis=(0, 2)))
    sum_second = lax.optimization_barrier(jnp.sum((masked * field_in).reshape(PIX, GROUPS, group_size), axis=(0, 2)))
    center = sum_first / counts
    spread = sum_second / counts - center * center
    inv_std = lax.rsqrt(spread + EPS_GROUP)
    center = jnp.repeat(center, group_size)
    inv_std = jnp.repeat(inv_std, group_size)
    return keep_col * (field_in - center) * inv_std * gain

def layer_norm(field_in, gain):
    center = lax.optimization_barrier(jnp.mean(field_in, axis=-1, keepdims=True))
    spread = lax.optimization_barrier(jnp.mean(jnp.square(field_in - center), axis=-1, keepdims=True))
    return (field_in - center) * lax.rsqrt(spread + EPS_LAYER) * gain

def attention(query_all, key_all, value_all, key_keep):
    factor = 1.0 / math.sqrt(HEAD_DIM)
    blocks = query_all.reshape(PIX // QBLOCK, QBLOCK, HEADS, HEAD_DIM)

    def one_block(query_b):
        raw_scores = jnp.einsum('qhd,khd->hqk', query_b, key_all, precision=HIGH) * factor
        scores = low_back(raw_scores)
        scores = jnp.where(key_keep[None, None, :] > 0, scores, MASKED)
        row_peak = lax.optimization_barrier(jnp.max(scores, axis=2, keepdims=True))
        denom_sum = lax.optimization_barrier(jnp.sum(jnp.exp(scores - row_peak), axis=2, keepdims=True))
        prob_rows = low(jnp.exp(scores - (row_peak + jnp.log(denom_sum))))
        return jnp.einsum('hqk,khd->qhd', prob_rows, value_all, precision=HIGH)
    out_blocks = lax.map(jax.checkpoint(one_block), blocks)
    return out_blocks.reshape(PIX, HEADS * HEAD_DIM)

def forward_one(weight_set, image_in, keep_vec, wide_rows, label_hot, time_feat):
    gain_first, conv_first, time_proj, gain_second, conv_second, gain_spatial, proj_in, gain_attn, attn_qkv, attn_out, class_table, cross_value, cross_out, gain_ff, geglu_in, geglu_out, proj_out = weight_set
    keep_col = keep_vec[:, None]
    counts = jnp.sum(keep_vec) * (C // GROUPS)
    row_width = jnp.where(wide_rows, LONG, SHORT).astype(jnp.int32)
    column = (jnp.arange(PIX, dtype=jnp.int32) % row_width)[:, None]
    act_first = low(jax.nn.silu(group_norm(image_in, gain_first, keep_col, counts)))
    hidden = low_back(convolve(act_first, conv_first, wide_rows, column, row_width))
    hidden = hidden + matmul(jax.nn.silu(time_feat)[None, :], time_proj)
    act_second = low(jax.nn.silu(group_norm(hidden, gain_second, keep_col, counts)))
    residual = image_in + low_back(convolve(act_second, conv_second, wide_rows, column, row_width))
    spatial = low(group_norm(residual, gain_spatial, keep_col, counts))
    stream = low_back(matmul(spatial, proj_in))
    normed_attn = low(layer_norm(stream, gain_attn))
    packed = low_back(low(matmul(normed_attn, attn_qkv)))
    query_all = packed[:, :C].reshape(PIX, HEADS, HEAD_DIM)
    key_all = packed[:, C:2 * C].reshape(PIX, HEADS, HEAD_DIM)
    value_all = packed[:, 2 * C:].reshape(PIX, HEADS, HEAD_DIM)
    heads = low_back(low(attention(query_all, key_all, value_all, keep_vec)))
    stream = stream + low_back(matmul(heads, attn_out))
    context = matmul(label_hot[None, :], class_table)
    stream = stream + matmul(matmul(context, cross_value), cross_out)
    normed_ff = low(layer_norm(stream, gain_ff))
    gates = low_back(matmul(normed_ff, geglu_in))
    mixed = low(gates[:, :FF] * jax.nn.gelu(gates[:, FF:], approximate=False))
    stream = stream + low_back(matmul(mixed, geglu_out))
    return residual + low_back(matmul(low(stream), proj_out))

def add_pair(left, right):
    return left + right

def reference(latents, cotangent, bucket, pixel_mask, labels, timesteps, gain_first, conv_first, time_proj, gain_second, conv_second, gain_spatial, proj_in, gain_attn, attn_qkv, attn_out, class_table, cross_value, cross_out, gain_ff, geglu_in, geglu_out, proj_out):
    weight_set = tuple((weight.astype(jnp.float32) for weight in (gain_first, conv_first, time_proj, gain_second, conv_second, gain_spatial, proj_in, gain_attn, attn_qkv, attn_out, class_table, cross_value, cross_out, gain_ff, geglu_in, geglu_out, proj_out)))
    half_dim = TEMB // 2
    frequency = jnp.exp(-math.log(10000.0) * jnp.arange(half_dim, dtype=jnp.float32) / half_dim)

    def step(totals, item_in):
        image_in, grad_in, bucket_id, keep_int, label_id, stamp = item_in
        angles = stamp.astype(jnp.float32) * frequency
        time_feat = jnp.concatenate([jnp.cos(angles), jnp.sin(angles)])
        label_hot = (jnp.arange(NCLASS, dtype=jnp.int32) == label_id).astype(jnp.float32)
        wide_rows = bucket_id == 0
        keep_vec = keep_int.astype(jnp.float32)

        def local_forward(weights_in, image_f):
            return forward_one(weights_in, image_f, keep_vec, wide_rows, label_hot, time_feat)
        result, pullback = jax.vjp(local_forward, weight_set, image_in.astype(jnp.float32))
        grad_weights, grad_image = pullback(grad_in.astype(jnp.float32))
        totals = jax.tree.map(add_pair, totals, grad_weights)
        return (totals, (result.astype(jnp.bfloat16), grad_image.astype(jnp.bfloat16)))
    zero_init = jax.tree.map(jnp.zeros_like, weight_set)
    totals, (results, grad_images) = lax.scan(step, zero_init, (latents, cotangent, bucket, pixel_mask, labels, timesteps))
    return (results, grad_images, totals[0], totals[1], totals[2], totals[3], totals[4], totals[5], totals[6], totals[7], totals[8][:, :2 * C], totals[8][:, 2 * C:], totals[9], totals[10], totals[11], totals[12], totals[13], totals[14], totals[15], totals[16])
```

```python
import functools
import math

import jax
import jax.numpy as jnp
from jax import lax
from jax.experimental import pallas as pl
from jax.experimental.pallas import tpu as pltpu
from jax.sharding import PartitionSpec as P

HEAD_DIM = 32
GROUPS = 32
SHORT = 48
LONG = 80


HIGH = lax.Precision.HIGHEST
EPS_GROUP = 1e-06
EPS_LAYER = 1e-05
MASKED = -1e30


TILE = 128
PER_TILE = TILE // HEAD_DIM
QB = 256
ONES = 16
LN2 = math.log(2.0)
bf16 = jnp.bfloat16
f32 = jnp.float32


def padded_2(block, sides, width):
    for axis, dim in sides:
        count = lax.axis_size(axis)
        forward = [(i, i + 1) for i in range(count - 1)]
        backward = [(target, source) for source, target in forward]
        low = lax.ppermute(
            lax.slice_in_dim(block, block.shape[dim] - width, None, axis=dim), axis, forward
        )
        high = lax.ppermute(lax.slice_in_dim(block, 0, width, axis=dim), axis, backward)
        block = jnp.concatenate([low, block, high], axis=dim)
    return block


def tap_stack(padded, wide_rows, column, row_width, pix_count):
    pieces = []
    offset = LONG + 1
    for shift_y in (-1, 0, 1):
        for shift_x in (-1, 0, 1):
            long_start = offset + shift_y * LONG + shift_x
            short_start = offset + shift_y * SHORT + shift_x
            long_piece = lax.slice_in_dim(padded, long_start, long_start + pix_count, axis=1)
            short_piece = lax.slice_in_dim(padded, short_start, short_start + pix_count, axis=1)
            chosen = jnp.where(wide_rows, long_piece, short_piece)
            inside = (column + shift_x >= 0) & (column + shift_x < row_width)
            pieces.append(jnp.where(inside, chosen, jnp.zeros_like(chosen)))
    return lax.optimization_barrier(jnp.concatenate(pieces, axis=2)).astype(bf16)


def conv_stack(act_in, wide_rows, column, row_width):
    rimmed = padded_2(act_in, (("narrow", 1),), LONG)
    padded = lax.optimization_barrier(jnp.pad(rimmed.astype(f32), ((0, 0), (1, 1), (0, 0))))
    return tap_stack(padded, wide_rows, column, row_width, act_in.shape[1])


def conv_transpose(grad_in, weight, wide_rows, column, row_width):
    rimmed = padded_2(grad_in, (("narrow", 1),), LONG)
    padded = lax.optimization_barrier(jnp.pad(rimmed.astype(f32), ((0, 0), (1, 1), (0, 0))))
    tap_rows = tap_stack(padded, wide_rows, column, row_width, grad_in.shape[1])
    channels = weight.shape[1]
    taps_count = weight.shape[0] // channels
    flipped = jnp.transpose(
        weight.reshape(taps_count, channels, channels)[::-1], (0, 2, 1)
    ).reshape(weight.shape)
    return jnp.einsum("npk,kc->npc", tap_rows, flipped, preferred_element_type=jnp.float32)


def group_moments(field_in, pixel_keep, counts):
    images, local_pix, channels = field_in.shape
    group_size = channels // GROUPS
    shaped = (images, local_pix, GROUPS, group_size)
    masked = field_in * pixel_keep
    sum_first = jnp.sum(masked.reshape(shaped), axis=(1, 3))
    sum_second = jnp.sum((masked * field_in).reshape(shaped), axis=(1, 3))
    sum_first, sum_second = lax.psum((sum_first, sum_second), "narrow")
    center = sum_first / counts[:, None]
    spread = sum_second / counts[:, None] - center * center
    inv_std = lax.rsqrt(spread + EPS_GROUP)
    return (
        jnp.repeat(center, group_size, axis=1)[:, None, :],
        jnp.repeat(inv_std, group_size, axis=1)[:, None, :],
    )


def group_back(grad_out, field_in, center, inv_std, gain, pixel_keep, counts):
    images, local_pix, channels = field_in.shape
    group_size = channels // GROUPS
    shaped = (images, local_pix, GROUPS, group_size)
    normed = (field_in - center) * inv_std
    grad_gain = jnp.sum(grad_out * normed * pixel_keep, axis=(0, 1))
    grad_hat = grad_out * gain * pixel_keep
    sum_first = jnp.sum(grad_hat.reshape(shaped), axis=(1, 3))
    sum_second = jnp.sum((grad_hat * normed).reshape(shaped), axis=(1, 3))
    sum_first, sum_second = lax.psum((sum_first, sum_second), "narrow")
    mean_first = jnp.repeat(sum_first / counts[:, None], group_size, axis=1)[:, None, :]
    mean_second = jnp.repeat(sum_second / counts[:, None], group_size, axis=1)[:, None, :]
    grad_field = pixel_keep * inv_std * (grad_hat - mean_first - normed * mean_second)
    return (grad_field, grad_gain)


def layer_norm(field_in, gain):
    center = jnp.mean(field_in, axis=-1, keepdims=True)
    spread = jnp.mean(jnp.square(field_in - center), axis=-1, keepdims=True)
    return (field_in - center) * lax.rsqrt(spread + EPS_LAYER) * gain


def geglu_mix(gates):
    half_width = gates.shape[-1] // 2
    return gates[..., :half_width] * jax.nn.gelu(gates[..., half_width:], approximate=False)


def head_rows(block, head):
    row = lax.broadcasted_iota(jnp.int32, block.shape, 0)
    inside = (row >= head * HEAD_DIM) & (row < (head + 1) * HEAD_DIM)
    return jnp.where(inside, block, jnp.zeros_like(block))


def head_lanes(block, head):
    lane = lax.broadcasted_iota(jnp.int32, block.shape, 1)
    inside = (lane >= head * HEAD_DIM) & (lane < (head + 1) * HEAD_DIM)
    return jnp.where(inside, block, jnp.zeros_like(block))


def mask_rows():
    row = lax.broadcasted_iota(jnp.int32, (TILE, QB), 0)
    return jnp.where(row == 0, 1.0, 0.0).astype(bf16)


def attend_kernel(first, last, *refs):
    qt_ref, k0_ref, k1_ref, v0_ref, v1_ref, aug_ref = refs[:6]
    rest = refs[6:]
    if not first:
        peak_in, acc_in = rest[:2]
        rest = rest[2:]
    if last:
        heads_ref, log_ref = rest
    else:
        peak_ref, acc_ref = rest
    keys = jnp.concatenate([k0_ref[...].astype(bf16), k1_ref[...].astype(bf16)], axis=0)
    keys = jnp.concatenate([keys, aug_ref[...].astype(bf16)], axis=1)
    values = jnp.concatenate([v0_ref[...].astype(bf16), v1_ref[...].astype(bf16)], axis=0)
    value_t = jnp.transpose(values, (1, 0))
    ones = jnp.ones((ONES, value_t.shape[1]), bf16)
    low_rows = mask_rows()

    def block_step(step, carry):
        cols = pl.ds(pl.multiple_of(step * QB, QB), QB)
        qt = qt_ref[:, cols].astype(bf16)
        for head in range(PER_TILE):
            rows = slice(head * HEAD_DIM, (head + 1) * HEAD_DIM)
            query = jnp.concatenate([head_rows(qt, head), low_rows], axis=0)
            scores = jnp.dot(keys, query, preferred_element_type=f32)
            peak = jnp.max(scores, axis=0, keepdims=True)
            if not first:
                peak_old = peak_in[head, 0:1, cols]
                peak = jnp.maximum(peak, peak_old)
            probs = jnp.exp2(scores - peak).astype(bf16)
            value_h = jnp.concatenate([value_t[rows], ones], axis=0)
            acc = jnp.dot(value_h, probs, preferred_element_type=f32)
            if not first:
                acc = acc + acc_in[head, :, cols] * jnp.exp2(peak_old - peak)
            if last:
                total = acc[HEAD_DIM : HEAD_DIM + 1]
                heads_ref[rows, cols] = acc[:HEAD_DIM] / total
                log_ref[head, :, cols] = jnp.broadcast_to(peak + jnp.log2(total), (8, QB))
            else:
                acc_ref[head, :, cols] = acc
                peak_ref[head, :, cols] = jnp.broadcast_to(peak, (8, QB))
        return carry

    lax.fori_loop(0, qt_ref.shape[1] // QB, block_step, 0)


def chunk_specs(count, tiles):
    key_spec = pl.BlockSpec((count, TILE), lambda t: (0, t))
    value_spec = pl.BlockSpec((count, TILE), lambda t: (0, tiles + t))
    aug_spec = pl.BlockSpec((2 * count, TILE), lambda t: (0, 0))
    return [key_spec, key_spec, value_spec, value_spec, aug_spec]


def attend_pair(first, last, query_t, pair, aug, state):
    channels, queries = query_t.shape
    count = pair[0].shape[0]
    heads = channels // HEAD_DIM
    tiles = channels // TILE
    t_spec = pl.BlockSpec((TILE, queries), lambda t: (t, 0))
    cube = lambda t: (t, 0, 0)
    row_spec = pl.BlockSpec((PER_TILE, 8, queries), cube)
    acc_spec = pl.BlockSpec((PER_TILE, HEAD_DIM + ONES, queries), cube)
    in_specs = [t_spec] + chunk_specs(count, tiles)
    if not first:
        in_specs += [row_spec, acc_spec]
    row_shape = jax.ShapeDtypeStruct((heads, 8, queries), f32)
    if last:
        out_shape = (jax.ShapeDtypeStruct((channels, queries), f32), row_shape)
        out_specs = (t_spec, row_spec)
    else:
        out_shape = (
            row_shape,
            jax.ShapeDtypeStruct((heads, HEAD_DIM + ONES, queries), f32),
        )
        out_specs = (row_spec, acc_spec)
    return pl.pallas_call(
        functools.partial(attend_kernel, first, last),
        grid=(tiles,),
        in_specs=in_specs,
        out_specs=out_specs,
        out_shape=out_shape,
        compiler_params=pltpu.CompilerParams(vmem_limit_bytes=40 << 20),
        cost_estimate=pl.CostEstimate(
            flops=64 * channels * queries * count,
            bytes_accessed=8 * channels * (queries + count),
            transcendentals=2 * heads * queries * count,
        ),
        name="attend",
    )(query_t, pair[0], pair[1], pair[0], pair[1], aug, *state)


def attend_back_kernel(first, *refs):
    qt_ref, q_ref, dt_ref, d_ref, log_ref, heads_ref = refs[:6]
    k0_ref, k1_ref, v0_ref, v1_ref, aug_ref = refs[6:11]
    refs = refs[11:]
    if not first:
        dq_in = refs[0]
        refs = refs[1:]
    dq_ref, low_ref, high_ref, dk_acc, dv_acc = refs
    count = k0_ref.shape[0]
    k_tile = jnp.concatenate([k0_ref[...].astype(bf16), k1_ref[...].astype(bf16)], axis=0)
    keys = jnp.concatenate([k_tile, aug_ref[...].astype(bf16)], axis=1)
    values = jnp.concatenate([v0_ref[...].astype(bf16), v1_ref[...].astype(bf16)], axis=0)
    key_t = jnp.transpose(k_tile, (1, 0))
    low_rows = mask_rows()
    dk_acc[...] = jnp.zeros_like(dk_acc)
    dv_acc[...] = jnp.zeros_like(dv_acc)
    factor = 1.0 / math.sqrt(HEAD_DIM)

    def block_step(step, carry):
        cols = pl.ds(pl.multiple_of(step * QB, QB), QB)
        qt = qt_ref[:, cols].astype(bf16)
        dt = dt_ref[:, cols].astype(bf16)
        q_blk = q_ref[cols, :].astype(bf16)
        d_blk = d_ref[cols, :].astype(bf16)
        probs_all, grads_all, q_all, d_all = [], [], [], []
        for head in range(PER_TILE):
            rows = slice(head * HEAD_DIM, (head + 1) * HEAD_DIM)
            query = jnp.concatenate([head_rows(qt, head), low_rows], axis=0)
            scores = jnp.dot(keys, query, preferred_element_type=f32)
            probs = jnp.exp2(scores - log_ref[head, 0:1, cols])
            weighted = jnp.sum(
                heads_ref[rows, cols] * dt_ref[rows, cols], axis=0, keepdims=True
            )
            grad_p = jnp.dot(values, head_rows(dt, head), preferred_element_type=f32)
            grad_s = (probs * (grad_p - weighted)).astype(bf16)
            probs_all.append(probs.astype(bf16))
            grads_all.append(grad_s)
            q_all.append(head_lanes(q_blk, head))
            d_all.append(head_lanes(d_blk, head))
            dq = jnp.dot(key_t[rows], grad_s, preferred_element_type=f32) * factor
            if not first:
                dq = dq + dq_in[rows, cols]
            dq_ref[rows, cols] = dq
        dv_acc[...] += jnp.dot(
            jnp.concatenate(probs_all, axis=1),
            jnp.concatenate(d_all, axis=0),
            preferred_element_type=f32,
        )
        dk_acc[...] += jnp.dot(
            jnp.concatenate(grads_all, axis=1),
            jnp.concatenate(q_all, axis=0),
            preferred_element_type=f32,
        )
        return carry

    lax.fori_loop(0, qt_ref.shape[1] // QB, block_step, 0)
    low_ref[0] = dk_acc[:count] * LN2
    low_ref[1] = dv_acc[:count]
    high_ref[0] = dk_acc[count:] * LN2
    high_ref[1] = dv_acc[count:]


def attend_back_pair(first, query_t, query, grad_t, grad, logs, heads_t, pair, aug, dq):
    channels, queries = query_t.shape
    count = pair[0].shape[0]
    tiles = channels // TILE
    t_spec = pl.BlockSpec((TILE, queries), lambda t: (t, 0))
    n_spec = pl.BlockSpec((queries, TILE), lambda t: (0, t))
    row_spec = pl.BlockSpec((PER_TILE, 8, queries), lambda t: (t, 0, 0))
    out_spec = pl.BlockSpec((2, count, TILE), lambda t: (0, 0, t))
    in_specs = [t_spec, n_spec, t_spec, n_spec, row_spec, t_spec] + chunk_specs(count, tiles)
    state = ()
    if not first:
        in_specs.append(t_spec)
        state = (dq,)
    return pl.pallas_call(
        functools.partial(attend_back_kernel, first),
        grid=(tiles,),
        in_specs=in_specs,
        out_specs=(t_spec, out_spec, out_spec),
        out_shape=(
            jax.ShapeDtypeStruct((channels, queries), f32),
            jax.ShapeDtypeStruct((2, count, channels), f32),
            jax.ShapeDtypeStruct((2, count, channels), f32),
        ),
        scratch_shapes=[pltpu.VMEM((2 * count, TILE), f32), pltpu.VMEM((2 * count, TILE), f32)],
        compiler_params=pltpu.CompilerParams(vmem_limit_bytes=48 << 20),
        cost_estimate=pl.CostEstimate(
            flops=160 * channels * queries * count,
            bytes_accessed=12 * channels * (queries + count),
            transcendentals=2 * channels // HEAD_DIM * queries * count,
        ),
        name="attend_back",
    )(query_t, query, grad_t, grad, logs, heads_t, pair[0], pair[1], pair[0], pair[1], aug, *state)


def swap(value, bit):
    count = lax.axis_size("narrow")
    return lax.ppermute(value, "narrow", [(i, i ^ bit) for i in range(count)])


def low_bit(index):
    return index & -index


def key_aug(keep_chunk):
    lane = lax.broadcasted_iota(jnp.int32, (keep_chunk.shape[0], TILE), 1)
    bias = jnp.where(keep_chunk[:, None] > 0, 0.0, MASKED)
    return jnp.where(lane == 0, bias, 0.0)


def narrow_bits():
    count = lax.axis_size("narrow")
    return [1 << level for level in range(count.bit_length() - 1)]


def my_bit(bit):
    return (lax.axis_index("narrow") // bit) % 2


def narrow_share(grad):
    count = lax.axis_size("narrow")
    rows = grad.shape[0] // count
    held = grad.reshape(count, rows, grad.shape[1])
    for bit in narrow_bits():
        halves = held.reshape(held.shape[0] // 2, 2, rows, grad.shape[1])
        mine = my_bit(bit)
        kept = lax.dynamic_index_in_dim(halves, mine, 1, keepdims=False)
        sent = lax.dynamic_index_in_dim(halves, 1 - mine, 1, keepdims=False)
        held = kept.astype(f32) + swap(sent.astype(bf16), bit).astype(f32)
    return held[0]


def narrow_whole(share):
    whole = share.astype(bf16)[None]
    for bit in reversed(narrow_bits()):
        other = swap(whole, bit)
        pair = jnp.where(
            my_bit(bit) == 0,
            jnp.stack([whole, other], axis=1),
            jnp.stack([other, whole], axis=1),
        )
        whole = pair.reshape((-1,) + share.shape)
    return whole.reshape(-1, share.shape[1]).astype(f32)


def reduce_weight(grad):
    share = narrow_share(grad)
    share = lax.psum_scatter(share, "wide", scatter_dimension=1, tiled=True)
    return narrow_whole(share)


def gather_images(values, once):
    spot = lax.axis_index("wide")
    first = (lax.axis_index("narrow") == 0).astype(f32)
    rows = jnp.concatenate([values, once * first], axis=0)[None]
    placed = jnp.zeros((lax.axis_size("wide"),) + rows.shape[1:], f32)
    placed = lax.dynamic_update_slice_in_dim(placed, rows, spot, 0)
    return lax.psum(placed, ("wide", "narrow"))


def own_columns(value):
    width = value.shape[-1] // lax.axis_size("wide")
    start = lax.axis_index("wide") * width
    return lax.dynamic_slice_in_dim(value, start, width, value.ndim - 1)


def per_device(
    latents,
    cotangent,
    bucket,
    pixel_mask,
    labels,
    timesteps,
    gain_first,
    conv_first,
    time_proj,
    gain_second,
    conv_second,
    gain_spatial,
    proj_in,
    gain_attn,
    attn_qkv,
    attn_out,
    class_table,
    cross_value,
    cross_out,
    gain_ff,
    geglu_in,
    geglu_out,
    proj_out,
):
    images, local_pix, channels = latents.shape
    row_start = lax.axis_index("narrow") * local_pix
    keep_all = pixel_mask.astype(jnp.float32)
    pixel_keep = lax.dynamic_slice_in_dim(keep_all, row_start, local_pix, 1)[:, :, None]
    counts = jnp.sum(keep_all, axis=1) * (channels // GROUPS)
    wide_rows = (bucket == 0)[:, None, None]
    row_width = jnp.where(wide_rows, LONG, SHORT).astype(jnp.int32)
    column = jnp.arange(local_pix, dtype=jnp.int32)[None, :, None] % row_width
    half_dim = time_proj.shape[0] // 2
    frequency = jnp.exp(-math.log(10000.0) * jnp.arange(half_dim, dtype=jnp.float32) / half_dim)
    angles = timesteps.astype(jnp.float32)[:, None] * frequency[None, :]
    time_act = jax.nn.silu(jnp.concatenate([jnp.cos(angles), jnp.sin(angles)], axis=1))
    time_term = jnp.dot(time_act, time_proj.astype(jnp.float32), precision=HIGH)
    label_hot = (
        labels[:, None] == jnp.arange(class_table.shape[0], dtype=jnp.int32)[None, :]
    ).astype(jnp.float32)
    context = jnp.dot(label_hot, class_table.astype(jnp.float32), precision=HIGH)
    value_weight = cross_value.astype(jnp.float32)
    cross_weight = cross_out.astype(jnp.float32)
    value_term = jnp.dot(context, value_weight, precision=HIGH)
    cross_term = jnp.dot(value_term, cross_weight, precision=HIGH)
    gain_one = gain_first.astype(jnp.float32)
    gain_two = gain_second.astype(jnp.float32)
    gain_three = gain_spatial.astype(jnp.float32)
    image_in = latents.astype(jnp.float32)
    center_one, scale_one = group_moments(image_in, pixel_keep, counts)
    act_first, silu_pull_one = jax.vjp(
        jax.nn.silu, pixel_keep * (image_in - center_one) * scale_one * gain_one
    )
    stack_first = conv_stack(act_first.astype(jnp.bfloat16), wide_rows, column, row_width)
    hidden = (
        jnp.einsum("npk,kc->npc", stack_first, conv_first, preferred_element_type=jnp.float32)
        + time_term[:, None, :]
    )
    center_two, scale_two = group_moments(hidden, pixel_keep, counts)
    act_second, silu_pull_two = jax.vjp(
        jax.nn.silu, pixel_keep * (hidden - center_two) * scale_two * gain_two
    )
    stack_second = conv_stack(act_second.astype(jnp.bfloat16), wide_rows, column, row_width)
    residual = image_in + jnp.einsum(
        "npk,kc->npc", stack_second, conv_second, preferred_element_type=jnp.float32
    )
    center_three, scale_three = group_moments(residual, pixel_keep, counts)
    spatial = (pixel_keep * (residual - center_three) * scale_three * gain_three).astype(
        jnp.bfloat16
    )
    stream = jnp.einsum("npc,cd->npd", spatial, proj_in, preferred_element_type=jnp.float32)
    normed_attn, attn_pull = jax.vjp(layer_norm, stream, gain_attn.astype(jnp.float32))
    normed_attn = normed_attn.astype(jnp.bfloat16)
    packed_f = jnp.einsum("npc,cd->npd", normed_attn, attn_qkv, preferred_element_type=jnp.float32)
    query_pix = (packed_f[0, :, :channels] * (1.0 / (math.sqrt(HEAD_DIM) * LN2))).astype(bf16)
    pad_pix = -local_pix % QB
    query_pix = jnp.pad(query_pix, ((0, pad_pix), (0, 0))).astype(f32)
    query_t = query_pix.T
    key_value = packed_f[0, :, channels:].astype(bf16)
    count = lax.axis_size("narrow")
    position = lax.axis_index("narrow")
    chunks = [key_value]
    for index in range(1, count):
        bit = low_bit(index)
        chunks.append(swap(chunks[index ^ bit], bit))
    chunks = [chunk.astype(f32) for chunk in chunks]
    pairs = [chunks[index : index + 2] for index in range(0, count, 2)]
    keep_chunk = lambda index: lax.dynamic_slice_in_dim(
        keep_all[0], (position ^ index) * local_pix, local_pix, 0
    )
    augs = [
        key_aug(jnp.concatenate([keep_chunk(index), keep_chunk(index + 1)]))
        for index in range(0, count, 2)
    ]
    state = ()
    for index, pair in enumerate(pairs):
        state = attend_pair(
            index == 0, index == len(pairs) - 1, query_t, pair, augs[index], state
        )
    heads_t, log_rows = state
    heads_rows = heads_t.T[None, :local_pix].astype(bf16)
    stream_mid = (
        stream
        + jnp.einsum("npc,cd->npd", heads_rows, attn_out, preferred_element_type=jnp.float32)
        + cross_term[:, None, :]
    )
    normed_ff, ff_pull = jax.vjp(layer_norm, stream_mid, gain_ff.astype(jnp.float32))
    normed_ff = normed_ff.astype(jnp.bfloat16)
    gates = jnp.einsum("npc,cf->npf", normed_ff, geglu_in, preferred_element_type=jnp.float32)
    mixed, gate_pull = jax.vjp(geglu_mix, gates)
    mixed = mixed.astype(jnp.bfloat16)
    stream_end = stream_mid + jnp.einsum(
        "npf,fc->npc", mixed, geglu_out, preferred_element_type=jnp.float32
    )
    top_in = stream_end.astype(jnp.bfloat16)
    output = (
        residual + jnp.einsum("npc,cd->npd", top_in, proj_out, preferred_element_type=jnp.float32)
    ).astype(jnp.bfloat16)
    grad_proj_out = jnp.einsum("npc,npd->cd", top_in, cotangent, preferred_element_type=jnp.float32)
    grad_end = jnp.einsum("npd,cd->npc", cotangent, proj_out, preferred_element_type=jnp.float32)
    grad_ffo = grad_end.astype(jnp.bfloat16)
    grad_geglu_out = jnp.einsum("npf,npc->fc", mixed, grad_ffo, preferred_element_type=jnp.float32)
    grad_mixed = jnp.einsum("npc,fc->npf", grad_ffo, geglu_out, preferred_element_type=jnp.float32)
    grad_gates = gate_pull(grad_mixed)[0].astype(jnp.bfloat16)
    grad_geglu_in = jnp.einsum(
        "npc,npf->cf", normed_ff, grad_gates, preferred_element_type=jnp.float32
    )
    grad_normed = jnp.einsum(
        "npf,cf->npc", grad_gates, geglu_in, preferred_element_type=jnp.float32
    )
    grad_from_ff, grad_gain_ff = ff_pull(grad_normed)
    grad_mid = grad_end + grad_from_ff
    grad_cross = jnp.sum(grad_mid, axis=1)
    grad_attn_in = grad_mid.astype(jnp.bfloat16)
    grad_attn_out = jnp.einsum(
        "npc,npd->cd", heads_rows, grad_attn_in, preferred_element_type=jnp.float32
    )
    grad_heads_rows = jnp.einsum(
        "npd,cd->npc", grad_attn_in, attn_out, preferred_element_type=jnp.float32
    ).astype(jnp.bfloat16)
    grad_rows = jnp.pad(grad_heads_rows[0], ((0, pad_pix), (0, 0))).astype(f32)
    grad_t = grad_rows.T
    grad_query_t = None
    arrived = [None] * count
    for index in reversed(range(len(pairs))):
        grad_query_t, grad_low, grad_high = attend_back_pair(
            index == len(pairs) - 1,
            query_t,
            query_pix,
            grad_t,
            grad_rows,
            log_rows,
            heads_t,
            pairs[index],
            augs[index],
            grad_query_t,
        )
        total = grad_low + swap(grad_high.astype(bf16), 1).astype(f32)
        for source in range(index + 1, len(pairs)):
            bit = low_bit(2 * source)
            if (2 * source) ^ bit == 2 * index:
                total = total + arrived[source].astype(f32)
        if index:
            arrived[index] = swap(total.astype(bf16), low_bit(2 * index))
    grad_packed = jnp.concatenate(
        [
            grad_query_t.T[:local_pix].astype(bf16),
            total[0].astype(bf16),
            total[1].astype(bf16),
        ],
        axis=1,
    )[None]
    grad_attn_whole = jnp.einsum(
        "npc,npd->cd", normed_attn, grad_packed, preferred_element_type=jnp.float32
    )
    grad_attn_qkv = grad_attn_whole[:, : 2 * channels]
    grad_attn_value = grad_attn_whole[:, 2 * channels :]
    grad_normed_attn = jnp.einsum(
        "npd,cd->npc", grad_packed, attn_qkv, preferred_element_type=jnp.float32
    )
    grad_from_attn, grad_gain_attn = attn_pull(grad_normed_attn)
    grad_stream = (grad_mid + grad_from_attn).astype(jnp.bfloat16)
    grad_proj_in = jnp.einsum(
        "npc,npd->cd", spatial, grad_stream, preferred_element_type=jnp.float32
    )
    grad_spatial = jnp.einsum(
        "npd,cd->npc", grad_stream, proj_in, preferred_element_type=jnp.float32
    )
    grad_from_norm, grad_gain_spatial = group_back(
        grad_spatial, residual, center_three, scale_three, gain_three, pixel_keep, counts
    )
    grad_res = cotangent.astype(jnp.float32) + grad_from_norm
    grad_res_low = grad_res.astype(jnp.bfloat16)
    grad_conv_second = jnp.einsum(
        "npk,npc->kc", stack_second, grad_res_low, preferred_element_type=jnp.float32
    )
    grad_act_second = conv_transpose(grad_res_low, conv_second, wide_rows, column, row_width)
    grad_pre_second = silu_pull_two(grad_act_second)[0]
    grad_hidden, grad_gain_second = group_back(
        grad_pre_second, hidden, center_two, scale_two, gain_two, pixel_keep, counts
    )
    grad_hidden_low = grad_hidden.astype(jnp.bfloat16)
    grad_conv_first = jnp.einsum(
        "npk,npc->kc", stack_first, grad_hidden_low, preferred_element_type=jnp.float32
    )
    grad_act_first = conv_transpose(grad_hidden_low, conv_first, wide_rows, column, row_width)
    grad_pre_first = silu_pull_one(grad_act_first)[0]
    grad_image_norm, grad_gain_first = group_back(
        grad_pre_first, image_in, center_one, scale_one, gain_one, pixel_keep, counts
    )
    grad_latents = (grad_res + grad_image_norm).astype(jnp.bfloat16)
    stack_rows = lambda *parts: reduce_weight(jnp.concatenate(parts, axis=0))
    top = stack_rows(grad_proj_out, grad_attn_out, grad_geglu_out)
    sum_geglu_in = reduce_weight(grad_geglu_in)
    sum_qk = reduce_weight(grad_attn_qkv)
    low_part = stack_rows(grad_proj_in, grad_attn_value)
    sum_conv_second = reduce_weight(grad_conv_second)
    sum_conv_first = reduce_weight(grad_conv_first)
    stamp_row = jnp.pad(
        jnp.concatenate([labels, timesteps]).astype(f32), (0, channels - 2 * images)
    )
    spread = gather_images(
        jnp.stack(
            [
                grad_cross[0],
                jnp.sum(grad_hidden, axis=1)[0],
                grad_gain_ff,
                grad_gain_attn,
                grad_gain_spatial,
                grad_gain_second,
            ]
        ),
        stamp_row[None],
    )
    labels_all = spread[:, 6, 0].astype(jnp.int32)
    steps_all = spread[:, 6, 1].astype(jnp.int32)
    angles_all = steps_all.astype(jnp.float32)[:, None] * frequency[None, :]
    time_all = jax.nn.silu(jnp.concatenate([jnp.cos(angles_all), jnp.sin(angles_all)], axis=1))
    hot_all = (
        labels_all[:, None] == jnp.arange(class_table.shape[0], dtype=jnp.int32)[None, :]
    ).astype(jnp.float32)
    context_all = jnp.dot(hot_all, class_table.astype(jnp.float32), precision=HIGH)
    value_all = jnp.dot(context_all, value_weight, precision=HIGH)
    cross_all = spread[:, 0]
    grad_value_all = jnp.dot(cross_all, cross_weight.T, precision=HIGH)
    grad_context_all = jnp.dot(grad_value_all, value_weight.T, precision=HIGH)
    sum_cross_out = jnp.dot(value_all.T, own_columns(cross_all), precision=HIGH)
    sum_cross_value = jnp.dot(context_all.T, own_columns(grad_value_all), precision=HIGH)
    sum_class_table = jnp.dot(hot_all.T, own_columns(grad_context_all), precision=HIGH)
    sum_time_proj = jnp.dot(time_all.T, own_columns(spread[:, 1]), precision=HIGH)
    gain_sums = own_columns(jnp.sum(spread[:, 2:6], axis=0))
    sum_gain_first = own_columns(lax.psum(grad_gain_first, ("wide", "narrow")))
    return (
        output,
        grad_latents,
        sum_gain_first,
        sum_conv_first,
        sum_time_proj,
        gain_sums[3],
        sum_conv_second,
        gain_sums[2],
        low_part[:channels],
        gain_sums[1],
        sum_qk,
        low_part[channels:],
        top[channels : 2 * channels],
        sum_class_table,
        sum_cross_value,
        sum_cross_out,
        gain_sums[0],
        sum_geglu_in,
        top[2 * channels :],
        top[:channels],
    )


def solution(mesh):
    placed = (
        P("wide", "narrow", None),
        P("wide", "narrow", None),
        P("wide"),
        P("wide", None),
        P("wide"),
        P("wide"),
        P(),
        P(),
        P(),
        P(),
        P(),
        P(),
        P(),
        P(),
        P(),
        P(),
        P(),
        P(),
        P(),
        P(),
        P(),
        P(),
        P(),
    )
    return jax.shard_map(
        per_device,
        mesh=mesh,
        in_specs=placed,
        out_specs=(
            P("wide", "narrow", None),
            P("wide", "narrow", None),
            P("wide"),
            P(None, "wide"),
            P(None, "wide"),
            P("wide"),
            P(None, "wide"),
            P("wide"),
            P(None, "wide"),
            P("wide"),
            P(None, "wide"),
            P(None, "wide"),
            P(None, "wide"),
            P(None, "wide"),
            P(None, "wide"),
            P(None, "wide"),
            P("wide"),
            P(None, "wide"),
            P(None, "wide"),
            P(None, "wide"),
        ),
        check_vma=False,
    )
```

```python
import functools
import math

import jax
import jax.numpy as jnp
from jax import lax
from jax.experimental import pallas as pl
from jax.experimental.pallas import tpu as pltpu
from jax.sharding import PartitionSpec as P

HEAD_DIM = 32
GROUPS = 32
SHORT = 48
LONG = 80


HIGH = lax.Precision.HIGHEST
EPS_GROUP = 1e-06
EPS_LAYER = 1e-05
MASKED = -1e30


TILE = 128
PER_TILE = TILE // HEAD_DIM
QB = 256
ONES = 16
SAFE_REACH = 90.0
LN2 = math.log(2.0)
bf16 = jnp.bfloat16
f32 = jnp.float32


def padded_2(block, sides, width):
    for axis, dim in sides:
        count = lax.axis_size(axis)
        forward = [(i, i + 1) for i in range(count - 1)]
        backward = [(target, source) for source, target in forward]
        low = lax.ppermute(
            lax.slice_in_dim(block, block.shape[dim] - width, None, axis=dim), axis, forward
        )
        high = lax.ppermute(lax.slice_in_dim(block, 0, width, axis=dim), axis, backward)
        block = jnp.concatenate([low, block, high], axis=dim)
    return block


def tap_stack(padded, wide_rows, column, row_width, pix_count):
    pieces = []
    offset = LONG + 1
    for shift_y in (-1, 0, 1):
        for shift_x in (-1, 0, 1):
            long_start = offset + shift_y * LONG + shift_x
            short_start = offset + shift_y * SHORT + shift_x
            long_piece = lax.slice_in_dim(padded, long_start, long_start + pix_count, axis=1)
            short_piece = lax.slice_in_dim(padded, short_start, short_start + pix_count, axis=1)
            chosen = jnp.where(wide_rows, long_piece, short_piece)
            inside = (column + shift_x >= 0) & (column + shift_x < row_width)
            pieces.append(jnp.where(inside, chosen, jnp.zeros_like(chosen)))
    return lax.optimization_barrier(jnp.concatenate(pieces, axis=2)).astype(bf16)


def conv_stack(act_in, wide_rows, column, row_width):
    rimmed = padded_2(act_in, (("narrow", 1),), LONG)
    padded = lax.optimization_barrier(jnp.pad(rimmed.astype(f32), ((0, 0), (1, 1), (0, 0))))
    return tap_stack(padded, wide_rows, column, row_width, act_in.shape[1])


def conv_transpose(grad_in, weight, wide_rows, column, row_width):
    rimmed = padded_2(grad_in, (("narrow", 1),), LONG)
    padded = lax.optimization_barrier(jnp.pad(rimmed.astype(f32), ((0, 0), (1, 1), (0, 0))))
    tap_rows = tap_stack(padded, wide_rows, column, row_width, grad_in.shape[1])
    channels = weight.shape[1]
    taps_count = weight.shape[0] // channels
    flipped = jnp.transpose(
        weight.reshape(taps_count, channels, channels)[::-1], (0, 2, 1)
    ).reshape(weight.shape)
    return jnp.einsum("npk,kc->npc", tap_rows, flipped, preferred_element_type=jnp.float32)


def group_sum(value):
    grouped = value.reshape(value.shape[0], GROUPS, -1)
    summed = jnp.sum(grouped, axis=2, keepdims=True)
    return jnp.broadcast_to(summed, grouped.shape).reshape(value.shape)


def group_moments(field_in, pixel_keep, counts):
    masked = field_in * pixel_keep
    sums = jnp.concatenate([jnp.sum(masked, axis=1), jnp.sum(masked * field_in, axis=1)], axis=0)
    sums = group_sum(narrow_sum(sums)) / counts[0]
    center = sums[0]
    spread = sums[1] - center * center
    return center[None, None, :], lax.rsqrt(spread + EPS_GROUP)[None, None, :]


def group_back(grad_out, field_in, center, inv_std, gain, pixel_keep, counts, extras):
    normed = (field_in - center) * inv_std
    kept = grad_out * pixel_keep
    rows = [jnp.sum(kept, axis=1)[0], jnp.sum(kept * normed, axis=1)[0]] + extras
    sums = narrow_sum(jnp.stack(rows))
    means = group_sum(sums[:2] * gain) / counts[0]
    grad_field = pixel_keep * inv_std * (kept * gain - means[0] - normed * means[1])
    return grad_field, sums[1], sums[2:]


def layer_norm(field_in, gain):
    center = jnp.mean(field_in, axis=-1, keepdims=True)
    spread = jnp.mean(jnp.square(field_in - center), axis=-1, keepdims=True)
    return (field_in - center) * lax.rsqrt(spread + EPS_LAYER) * gain


def geglu_mix(gates):
    half_width = gates.shape[-1] // 2
    return gates[..., :half_width] * jax.nn.gelu(gates[..., half_width:], approximate=False)


def head_rows(block, head):
    row = lax.broadcasted_iota(jnp.int32, block.shape, 0)
    inside = (row >= head * HEAD_DIM) & (row < (head + 1) * HEAD_DIM)
    return jnp.where(inside, block, jnp.zeros_like(block))


def head_lanes(block, head):
    lane = lax.broadcasted_iota(jnp.int32, block.shape, 1)
    inside = (lane >= head * HEAD_DIM) & (lane < (head + 1) * HEAD_DIM)
    return jnp.where(inside, block, jnp.zeros_like(block))


def mask_rows():
    row = lax.broadcasted_iota(jnp.int32, (TILE, QB), 0)
    return jnp.where(row == 0, 1.0, 0.0).astype(bf16)


def attend_kernel(first, last, *refs):
    qt_ref, k0_ref, k1_ref, v0_ref, v1_ref, aug_ref = refs[:6]
    rest = refs[6:]
    if not first:
        peak_in, acc_in = rest[:2]
        rest = rest[2:]
    if last:
        heads_ref, log_ref = rest
    else:
        peak_ref, acc_ref = rest
    keys = jnp.concatenate([k0_ref[...], k1_ref[...]], axis=0)
    keys = jnp.concatenate([keys, aug_ref[...]], axis=1)
    values = jnp.concatenate([v0_ref[...], v1_ref[...]], axis=0)
    value_t = jnp.transpose(values, (1, 0))
    ones = jnp.ones((ONES, value_t.shape[1]), bf16)
    low_rows = mask_rows()

    head_of = lambda shape, axis: lax.broadcasted_iota(jnp.int32, shape, axis) // HEAD_DIM
    pick = jnp.where(head_of((TILE, TILE), 0) == head_of((TILE, TILE), 1), 1.0, 0.0).astype(bf16)
    all_keys = keys[:, :TILE]
    key_norms = jnp.dot(all_keys * all_keys, pick, preferred_element_type=f32)
    all_queries = qt_ref[...]
    query_norms = jnp.dot(pick, all_queries * all_queries, preferred_element_type=f32)
    reach = jnp.float32(0.0)
    for head in range(PER_TILE):
        rows = slice(head * HEAD_DIM, head * HEAD_DIM + 8)
        mine = head_of(key_norms.shape, 1) == head
        key_peak = jnp.max(jnp.where(mine, key_norms, 0.0))
        reach = jnp.maximum(reach, key_peak * jnp.max(query_norms[rows]))

    def make_step(shifted):
        def block_step(step, carry):
            cols = pl.ds(pl.multiple_of(step * QB, QB), QB)
            qt = qt_ref[:, cols]
            for head in range(PER_TILE):
                rows = slice(head * HEAD_DIM, (head + 1) * HEAD_DIM)
                query = jnp.concatenate([head_rows(qt, head), low_rows], axis=0)
                scores = jnp.dot(keys, query, preferred_element_type=f32)
                if shifted:
                    peak = jnp.max(scores, axis=0, keepdims=True)
                    probs = jnp.exp2(scores - peak).astype(bf16)
                else:
                    peak = jnp.zeros((1, QB), f32)
                    probs = jnp.exp2(scores).astype(bf16)
                value_h = jnp.concatenate([value_t[rows], ones], axis=0)
                acc = jnp.dot(value_h, probs, preferred_element_type=f32)
                if not first:
                    peak_old = peak_in[head, 0:1, cols]
                    peak_new = jnp.maximum(peak, peak_old)
                    acc = acc * jnp.exp2(peak - peak_new)
                    acc = acc + acc_in[head, :, cols] * jnp.exp2(peak_old - peak_new)
                    peak = peak_new
                if last:
                    total = acc[HEAD_DIM : HEAD_DIM + 1]
                    heads_ref[rows, cols] = acc[:HEAD_DIM] / total
                    log_ref[head, :, cols] = jnp.broadcast_to(peak + jnp.log2(total), (8, QB))
                else:
                    acc_ref[head, :, cols] = acc
                    peak_ref[head, :, cols] = jnp.broadcast_to(peak, (8, QB))
            return carry

        return block_step

    steps = qt_ref.shape[1] // QB

    @pl.when(reach < SAFE_REACH * SAFE_REACH)
    def _():
        lax.fori_loop(0, steps, make_step(False), 0)

    @pl.when(jnp.logical_not(reach < SAFE_REACH * SAFE_REACH))
    def _():
        lax.fori_loop(0, steps, make_step(True), 0)


def chunk_specs(count, tiles):
    key_spec = pl.BlockSpec((count, TILE), lambda t: (0, t))
    value_spec = pl.BlockSpec((count, TILE), lambda t: (0, tiles + t))
    aug_spec = pl.BlockSpec((2 * count, TILE), lambda t: (0, 0))
    return [key_spec, key_spec, value_spec, value_spec, aug_spec]


def attend_pair(first, last, query_t, pair, aug, state):
    channels, queries = query_t.shape
    count = pair[0].shape[0]
    heads = channels // HEAD_DIM
    tiles = channels // TILE
    t_spec = pl.BlockSpec((TILE, queries), lambda t: (t, 0))
    cube = lambda t: (t, 0, 0)
    row_spec = pl.BlockSpec((PER_TILE, 8, queries), cube)
    acc_spec = pl.BlockSpec((PER_TILE, HEAD_DIM + ONES, queries), cube)
    in_specs = [t_spec] + chunk_specs(count, tiles)
    if not first:
        in_specs += [row_spec, acc_spec]
    row_shape = jax.ShapeDtypeStruct((heads, 8, queries), f32)
    if last:
        out_shape = (jax.ShapeDtypeStruct((channels, queries), f32), row_shape)
        out_specs = (t_spec, row_spec)
    else:
        out_shape = (
            row_shape,
            jax.ShapeDtypeStruct((heads, HEAD_DIM + ONES, queries), f32),
        )
        out_specs = (row_spec, acc_spec)
    return pl.pallas_call(
        functools.partial(attend_kernel, first, last),
        grid=(tiles,),
        in_specs=in_specs,
        out_specs=out_specs,
        out_shape=out_shape,
        compiler_params=pltpu.CompilerParams(vmem_limit_bytes=40 << 20),
        cost_estimate=pl.CostEstimate(
            flops=64 * channels * queries * count,
            bytes_accessed=8 * channels * (queries + count),
            transcendentals=2 * heads * queries * count,
        ),
        name="attend",
    )(query_t, pair[0], pair[1], pair[0], pair[1], aug, *state)


def attend_back_kernel(first, *refs):
    qt_ref, q_ref, dt_ref, d_ref, log_ref, heads_ref = refs[:6]
    k0_ref, k1_ref, v0_ref, v1_ref, aug_ref = refs[6:11]
    refs = refs[11:]
    if not first:
        dq_in = refs[0]
        refs = refs[1:]
    dq_ref, low_ref, high_ref, dk_acc, dv_acc = refs
    count = k0_ref.shape[0]
    k_tile = jnp.concatenate([k0_ref[...], k1_ref[...]], axis=0)
    keys = jnp.concatenate([k_tile, aug_ref[...]], axis=1)
    values = jnp.concatenate([v0_ref[...], v1_ref[...]], axis=0)
    key_t = jnp.transpose(k_tile, (1, 0))
    low_rows = mask_rows()
    dk_acc[...] = jnp.zeros_like(dk_acc)
    dv_acc[...] = jnp.zeros_like(dv_acc)
    factor = 1.0 / math.sqrt(HEAD_DIM)

    def block_step(step, carry):
        cols = pl.ds(pl.multiple_of(step * QB, QB), QB)
        qt = qt_ref[:, cols]
        dt = dt_ref[:, cols]
        q_blk = q_ref[cols, :]
        d_blk = d_ref[cols, :]
        probs_all, grads_all, q_all, d_all = [], [], [], []
        for head in range(PER_TILE):
            rows = slice(head * HEAD_DIM, (head + 1) * HEAD_DIM)
            query = jnp.concatenate([head_rows(qt, head), low_rows], axis=0)
            scores = jnp.dot(keys, query, preferred_element_type=f32)
            probs = jnp.exp2(scores - log_ref[head, 0:1, cols])
            weighted = jnp.sum(
                heads_ref[rows, cols] * dt[rows].astype(f32), axis=0, keepdims=True
            )
            grad_p = jnp.dot(values, head_rows(dt, head), preferred_element_type=f32)
            grad_s = (probs * (grad_p - weighted)).astype(bf16)
            probs_all.append(probs.astype(bf16))
            grads_all.append(grad_s)
            q_all.append(head_lanes(q_blk, head))
            d_all.append(head_lanes(d_blk, head))
            dq = jnp.dot(key_t[rows], grad_s, preferred_element_type=f32) * factor
            if not first:
                dq = dq + dq_in[rows, cols]
            dq_ref[rows, cols] = dq
        dv_acc[...] += jnp.dot(
            jnp.concatenate(probs_all, axis=1),
            jnp.concatenate(d_all, axis=0),
            preferred_element_type=f32,
        )
        dk_acc[...] += jnp.dot(
            jnp.concatenate(grads_all, axis=1),
            jnp.concatenate(q_all, axis=0),
            preferred_element_type=f32,
        )
        return carry

    lax.fori_loop(0, qt_ref.shape[1] // QB, block_step, 0)
    low_ref[0] = dk_acc[:count] * LN2
    low_ref[1] = dv_acc[:count]
    high_ref[0] = (dk_acc[count:] * LN2).astype(bf16)
    high_ref[1] = dv_acc[count:].astype(bf16)


def attend_back_pair(first, query_t, query, grad_t, grad, logs, heads_t, pair, aug, dq):
    channels, queries = query_t.shape
    count = pair[0].shape[0]
    tiles = channels // TILE
    t_spec = pl.BlockSpec((TILE, queries), lambda t: (t, 0))
    n_spec = pl.BlockSpec((queries, TILE), lambda t: (0, t))
    row_spec = pl.BlockSpec((PER_TILE, 8, queries), lambda t: (t, 0, 0))
    out_spec = pl.BlockSpec((2, count, TILE), lambda t: (0, 0, t))
    in_specs = [t_spec, n_spec, t_spec, n_spec, row_spec, t_spec] + chunk_specs(count, tiles)
    state = ()
    if not first:
        in_specs.append(t_spec)
        state = (dq,)
    return pl.pallas_call(
        functools.partial(attend_back_kernel, first),
        grid=(tiles,),
        in_specs=in_specs,
        out_specs=(t_spec, out_spec, out_spec),
        out_shape=(
            jax.ShapeDtypeStruct((channels, queries), f32),
            jax.ShapeDtypeStruct((2, count, channels), f32),
            jax.ShapeDtypeStruct((2, count, channels), bf16),
        ),
        scratch_shapes=[pltpu.VMEM((2 * count, TILE), f32), pltpu.VMEM((2 * count, TILE), f32)],
        compiler_params=pltpu.CompilerParams(vmem_limit_bytes=48 << 20),
        cost_estimate=pl.CostEstimate(
            flops=160 * channels * queries * count,
            bytes_accessed=12 * channels * (queries + count),
            transcendentals=2 * channels // HEAD_DIM * queries * count,
        ),
        name="attend_back",
    )(query_t, query, grad_t, grad, logs, heads_t, pair[0], pair[1], pair[0], pair[1], aug, *state)


def swap(value, bit, axis="narrow"):
    count = lax.axis_size(axis)
    return lax.ppermute(value, axis, [(i, i ^ bit) for i in range(count)])


def low_bit(index):
    return index & -index


def axis_bits(axis):
    return [1 << level for level in range(lax.axis_size(axis).bit_length() - 1)]


def my_bit(bit, axis="narrow"):
    return (lax.axis_index(axis) // bit) % 2


def narrow_sum(value):
    for bit in axis_bits("narrow"):
        value = value + swap(value, bit)
    return value


def key_aug(keep_chunk):
    lane = lax.broadcasted_iota(jnp.int32, (keep_chunk.shape[0], TILE), 1)
    bias = jnp.where(keep_chunk[:, None] > 0, 0.0, MASKED)
    return jnp.where(lane == 0, bias, 0.0).astype(bf16)


def halve(held, axis):
    for bit in axis_bits(axis):
        halves = held.reshape((held.shape[0] // 2, 2) + held.shape[1:])
        mine = my_bit(bit, axis)
        kept = lax.dynamic_index_in_dim(halves, mine, 1, keepdims=False)
        sent = lax.dynamic_index_in_dim(halves, 1 - mine, 1, keepdims=False)
        held = (kept.astype(f32) + swap(sent, bit, axis).astype(f32)).astype(bf16)
    return held[0]


def double(value, axis):
    whole = value[None]
    for bit in reversed(axis_bits(axis)):
        other = swap(whole, bit, axis)
        pair = jnp.where(
            my_bit(bit, axis) == 0,
            jnp.stack([whole, other], axis=1),
            jnp.stack([other, whole], axis=1),
        )
        whole = pair.reshape((-1,) + value.shape)
    return whole


def conv_share(grad_t):
    count = lax.axis_size("narrow")
    channels, rows = grad_t.shape
    padded = rows + (-rows % (count * TILE))
    held = jnp.pad(grad_t.astype(bf16), ((0, 0), (0, padded - rows)))
    held = jnp.transpose(held.reshape(channels, count, padded // count), (1, 0, 2))
    return halve(held, "narrow")


def conv_finish(share, rows):
    wide = lax.axis_size("wide")
    share = halve(share.reshape(wide, share.shape[0] // wide, share.shape[1]), "wide")
    whole = double(share, "narrow")
    return jnp.transpose(whole, (0, 2, 1)).reshape(-1, whole.shape[1])[:rows].astype(f32)


def by_owner(grad_t, width):
    wide = lax.axis_size("wide")
    groups = grad_t.shape[0] // wide // width
    split = grad_t.reshape(wide, groups, width, grad_t.shape[1])
    return jnp.transpose(split, (0, 2, 1, 3)).reshape(wide * width, -1)


def packed_sum(parts):
    share = lax.psum_scatter(
        jnp.concatenate(parts, axis=1), "wide", scatter_dimension=0, tiled=True
    ).astype(bf16)
    for bit in axis_bits("narrow"):
        share = (share.astype(f32) + swap(share, bit).astype(f32)).astype(bf16)
    return share.astype(f32)


def from_owner(share, rows):
    width = share.shape[0]
    split = share.reshape(width, -1, rows)
    return jnp.transpose(split, (2, 1, 0)).reshape(rows, -1)


def own_columns(value):
    width = value.shape[-1] // lax.axis_size("wide")
    start = lax.axis_index("wide") * width
    return lax.dynamic_slice_in_dim(value, start, width, value.ndim - 1)


def per_device(
    latents,
    cotangent,
    bucket,
    pixel_mask,
    labels,
    timesteps,
    gain_first,
    conv_first,
    time_proj,
    gain_second,
    conv_second,
    gain_spatial,
    proj_in,
    gain_attn,
    attn_qkv,
    attn_out,
    class_table,
    cross_value,
    cross_out,
    gain_ff,
    geglu_in,
    geglu_out,
    proj_out,
):
    images, local_pix, channels = latents.shape
    row_start = lax.axis_index("narrow") * local_pix
    keep_all = pixel_mask.astype(jnp.float32)
    pixel_keep = lax.dynamic_slice_in_dim(keep_all, row_start, local_pix, 1)[:, :, None]
    counts = jnp.sum(keep_all, axis=1) * (channels // GROUPS)
    wide_rows = (bucket == 0)[:, None, None]
    row_width = jnp.where(wide_rows, LONG, SHORT).astype(jnp.int32)
    column = jnp.arange(local_pix, dtype=jnp.int32)[None, :, None] % row_width
    half_dim = time_proj.shape[0] // 2
    frequency = jnp.exp(-math.log(10000.0) * jnp.arange(half_dim, dtype=jnp.float32) / half_dim)
    angles = timesteps.astype(jnp.float32)[:, None] * frequency[None, :]
    time_act = jax.nn.silu(jnp.concatenate([jnp.cos(angles), jnp.sin(angles)], axis=1))
    time_term = jnp.dot(time_act, time_proj.astype(jnp.float32), precision=HIGH)
    label_hot = (
        labels[:, None] == jnp.arange(class_table.shape[0], dtype=jnp.int32)[None, :]
    ).astype(jnp.float32)
    context = jnp.dot(label_hot, class_table.astype(jnp.float32), precision=HIGH)
    value_weight = cross_value.astype(jnp.float32)
    cross_weight = cross_out.astype(jnp.float32)
    value_term = jnp.dot(context, value_weight, precision=HIGH)
    cross_term = jnp.dot(value_term, cross_weight, precision=HIGH)
    gain_one = gain_first.astype(jnp.float32)
    gain_two = gain_second.astype(jnp.float32)
    gain_three = gain_spatial.astype(jnp.float32)
    image_in = latents.astype(jnp.float32)
    center_one, scale_one = group_moments(image_in, pixel_keep, counts)
    act_first, silu_pull_one = jax.vjp(
        jax.nn.silu, pixel_keep * (image_in - center_one) * scale_one * gain_one
    )
    stack_first = conv_stack(act_first.astype(jnp.bfloat16), wide_rows, column, row_width)
    hidden = (
        jnp.einsum("npk,kc->npc", stack_first, conv_first, preferred_element_type=jnp.float32)
        + time_term[:, None, :]
    )
    center_two, scale_two = group_moments(hidden, pixel_keep, counts)
    act_second, silu_pull_two = jax.vjp(
        jax.nn.silu, pixel_keep * (hidden - center_two) * scale_two * gain_two
    )
    stack_second = conv_stack(act_second.astype(jnp.bfloat16), wide_rows, column, row_width)
    residual = image_in + jnp.einsum(
        "npk,kc->npc", stack_second, conv_second, preferred_element_type=jnp.float32
    )
    center_three, scale_three = group_moments(residual, pixel_keep, counts)
    spatial = (pixel_keep * (residual - center_three) * scale_three * gain_three).astype(
        jnp.bfloat16
    )
    stream = jnp.einsum("npc,cd->npd", spatial, proj_in, preferred_element_type=jnp.float32)
    normed_attn, attn_pull = jax.vjp(layer_norm, stream, gain_attn.astype(jnp.float32))
    normed_attn = normed_attn.astype(jnp.bfloat16)
    packed_f = jnp.einsum("npc,cd->npd", normed_attn, attn_qkv, preferred_element_type=jnp.float32)
    query_pix = (packed_f[0, :, :channels] * (1.0 / (math.sqrt(HEAD_DIM) * LN2))).astype(bf16)
    pad_pix = -local_pix % QB
    query_pix = jnp.pad(query_pix, ((0, pad_pix), (0, 0)))
    query_t = query_pix.T
    key_value = packed_f[0, :, channels:].astype(bf16)
    count = lax.axis_size("narrow")
    position = lax.axis_index("narrow")
    chunks = [key_value]
    for index in range(1, count):
        bit = low_bit(index)
        chunks.append(swap(chunks[index ^ bit], bit))
    pairs = [chunks[index : index + 2] for index in range(0, count, 2)]
    keep_chunk = lambda index: lax.dynamic_slice_in_dim(
        keep_all[0], (position ^ index) * local_pix, local_pix, 0
    )
    augs = [
        key_aug(jnp.concatenate([keep_chunk(index), keep_chunk(index + 1)]))
        for index in range(0, count, 2)
    ]
    state = ()
    for index, pair in enumerate(pairs):
        state = attend_pair(
            index == 0, index == len(pairs) - 1, query_t, pair, augs[index], state
        )
    heads_t, log_rows = state
    heads_rows = heads_t.T[None, :local_pix].astype(bf16)
    stream_mid = (
        stream
        + jnp.einsum("npc,cd->npd", heads_rows, attn_out, preferred_element_type=jnp.float32)
        + cross_term[:, None, :]
    )
    normed_ff, ff_pull = jax.vjp(layer_norm, stream_mid, gain_ff.astype(jnp.float32))
    normed_ff = normed_ff.astype(jnp.bfloat16)
    gates = jnp.einsum("npc,cf->npf", normed_ff, geglu_in, preferred_element_type=jnp.float32)
    mixed, gate_pull = jax.vjp(geglu_mix, gates)
    mixed = mixed.astype(jnp.bfloat16)
    stream_end = stream_mid + jnp.einsum(
        "npf,fc->npc", mixed, geglu_out, preferred_element_type=jnp.float32
    )
    top_in = stream_end.astype(jnp.bfloat16)
    output = (
        residual + jnp.einsum("npc,cd->npd", top_in, proj_out, preferred_element_type=jnp.float32)
    ).astype(jnp.bfloat16)
    grad_proj_out = jnp.einsum("npc,npd->dc", top_in, cotangent, preferred_element_type=jnp.float32)
    grad_end = jnp.einsum("npd,cd->npc", cotangent, proj_out, preferred_element_type=jnp.float32)
    grad_ffo = grad_end.astype(jnp.bfloat16)
    grad_geglu_out = jnp.einsum("npf,npc->cf", mixed, grad_ffo, preferred_element_type=jnp.float32)
    grad_mixed = jnp.einsum("npc,fc->npf", grad_ffo, geglu_out, preferred_element_type=jnp.float32)
    grad_gates = gate_pull(grad_mixed)[0].astype(jnp.bfloat16)
    grad_geglu_in = jnp.einsum(
        "npc,npf->fc", normed_ff, grad_gates, preferred_element_type=jnp.float32
    )
    grad_normed = jnp.einsum(
        "npf,cf->npc", grad_gates, geglu_in, preferred_element_type=jnp.float32
    )
    grad_from_ff, grad_gain_ff = ff_pull(grad_normed)
    grad_mid = grad_end + grad_from_ff
    grad_cross = jnp.sum(grad_mid, axis=1)
    grad_attn_in = grad_mid.astype(jnp.bfloat16)
    grad_attn_out = jnp.einsum(
        "npc,npd->dc", heads_rows, grad_attn_in, preferred_element_type=jnp.float32
    )
    grad_heads_rows = jnp.einsum(
        "npd,cd->npc", grad_attn_in, attn_out, preferred_element_type=jnp.float32
    ).astype(jnp.bfloat16)
    grad_rows = jnp.pad(grad_heads_rows[0], ((0, pad_pix), (0, 0)))
    grad_t = grad_rows.T
    grad_query_t = None
    arrived = [None] * count
    for index in reversed(range(len(pairs))):
        grad_query_t, grad_low, grad_high = attend_back_pair(
            index == len(pairs) - 1,
            query_t,
            query_pix,
            grad_t,
            grad_rows,
            log_rows,
            heads_t,
            pairs[index],
            augs[index],
            grad_query_t,
        )
        total = grad_low + swap(grad_high, 1).astype(f32)
        for source in range(index + 1, len(pairs)):
            bit = low_bit(2 * source)
            if (2 * source) ^ bit == 2 * index:
                total = total + arrived[source].astype(f32)
        if index:
            arrived[index] = swap(total.astype(bf16), low_bit(2 * index))
    grad_packed = jnp.concatenate(
        [
            grad_query_t.T[:local_pix].astype(bf16),
            total[0].astype(bf16),
            total[1].astype(bf16),
        ],
        axis=1,
    )[None]
    grad_attn_whole = jnp.einsum(
        "npc,npd->dc", normed_attn, grad_packed, preferred_element_type=jnp.float32
    )
    grad_normed_attn = jnp.einsum(
        "npd,cd->npc", grad_packed, attn_qkv, preferred_element_type=jnp.float32
    )
    grad_from_attn, grad_gain_attn = attn_pull(grad_normed_attn)
    grad_stream = (grad_mid + grad_from_attn).astype(jnp.bfloat16)
    grad_proj_in = jnp.einsum(
        "npc,npd->dc", spatial, grad_stream, preferred_element_type=jnp.float32
    )
    grad_spatial = jnp.einsum(
        "npd,cd->npc", grad_stream, proj_in, preferred_element_type=jnp.float32
    )
    grad_from_norm, grad_gain_spatial, early_rows = group_back(
        grad_spatial,
        residual,
        center_three,
        scale_three,
        gain_three,
        pixel_keep,
        counts,
        [grad_cross[0], grad_gain_ff, grad_gain_attn],
    )
    grad_res = cotangent.astype(jnp.float32) + grad_from_norm
    grad_res_low = grad_res.astype(jnp.bfloat16)
    grad_conv_second = jnp.einsum(
        "npk,npc->ck", stack_second, grad_res_low, preferred_element_type=jnp.float32
    )
    grad_act_second = conv_transpose(grad_res_low, conv_second, wide_rows, column, row_width)
    grad_pre_second = silu_pull_two(grad_act_second)[0]
    grad_hidden, grad_gain_second, _ = group_back(
        grad_pre_second, hidden, center_two, scale_two, gain_two, pixel_keep, counts, []
    )
    grad_hidden_low = grad_hidden.astype(jnp.bfloat16)
    grad_conv_first = jnp.einsum(
        "npk,npc->ck", stack_first, grad_hidden_low, preferred_element_type=jnp.float32
    )
    grad_act_first = conv_transpose(grad_hidden_low, conv_first, wide_rows, column, row_width)
    grad_pre_first = silu_pull_one(grad_act_first)[0]
    grad_image_norm, grad_gain_first, late_rows = group_back(
        grad_pre_first,
        image_in,
        center_one,
        scale_one,
        gain_one,
        pixel_keep,
        counts,
        [jnp.sum(grad_hidden, axis=1)[0]],
    )
    grad_latents = (grad_res + grad_image_norm).astype(jnp.bfloat16)
    owned = channels // lax.axis_size("wide")
    top = packed_sum(
        [
            grad_proj_out,
            grad_attn_out,
            grad_geglu_out,
            by_owner(grad_geglu_in, owned),
        ]
    )
    low_part = packed_sum(
        [
            grad_proj_in,
            by_owner(grad_attn_whole[: 2 * channels], owned),
            grad_attn_whole[2 * channels :],
        ]
    )
    conv_rows = conv_first.shape[0]
    sum_conv_second = conv_finish(conv_share(grad_conv_second), conv_rows)
    sum_conv_first = conv_finish(conv_share(grad_conv_first), conv_rows)
    stamp_row = jnp.pad(
        jnp.concatenate([labels, timesteps]).astype(f32), (0, channels - 2 * images)
    )
    spread = double(
        jnp.stack(
            [
                early_rows[0],
                late_rows[0],
                early_rows[1],
                early_rows[2],
                grad_gain_spatial,
                grad_gain_second,
                grad_gain_first,
                stamp_row,
            ]
        ),
        "wide",
    )
    labels_all = spread[:, 7, 0].astype(jnp.int32)
    steps_all = spread[:, 7, 1].astype(jnp.int32)
    angles_all = steps_all.astype(jnp.float32)[:, None] * frequency[None, :]
    time_all = jax.nn.silu(jnp.concatenate([jnp.cos(angles_all), jnp.sin(angles_all)], axis=1))
    hot_all = (
        labels_all[:, None] == jnp.arange(class_table.shape[0], dtype=jnp.int32)[None, :]
    ).astype(jnp.float32)
    context_all = jnp.dot(hot_all, class_table.astype(jnp.float32), precision=HIGH)
    value_all = jnp.dot(context_all, value_weight, precision=HIGH)
    cross_all = spread[:, 0]
    grad_value_all = jnp.dot(cross_all, cross_weight.T, precision=HIGH)
    grad_context_all = jnp.dot(grad_value_all, value_weight.T, precision=HIGH)
    sum_cross_out = jnp.dot(value_all.T, own_columns(cross_all), precision=HIGH)
    sum_cross_value = jnp.dot(context_all.T, own_columns(grad_value_all), precision=HIGH)
    sum_class_table = jnp.dot(hot_all.T, own_columns(grad_context_all), precision=HIGH)
    sum_time_proj = jnp.dot(time_all.T, own_columns(spread[:, 1]), precision=HIGH)
    gain_sums = own_columns(jnp.sum(spread[:, 2:7], axis=0))
    return (
        output,
        grad_latents,
        gain_sums[4],
        sum_conv_first,
        sum_time_proj,
        gain_sums[3],
        sum_conv_second,
        gain_sums[2],
        from_owner(low_part[:, :channels], channels),
        gain_sums[1],
        from_owner(low_part[:, channels : 3 * channels], channels),
        from_owner(low_part[:, 3 * channels :], channels),
        from_owner(top[:, channels : 2 * channels], channels),
        sum_class_table,
        sum_cross_value,
        sum_cross_out,
        gain_sums[0],
        from_owner(top[:, 2 * channels + geglu_out.shape[0] :], channels),
        from_owner(top[:, 2 * channels : 2 * channels + geglu_out.shape[0]], geglu_out.shape[0]),
        from_owner(top[:, :channels], channels),
    )


def solution(mesh):
    placed = (
        P("wide", "narrow", None),
        P("wide", "narrow", None),
        P("wide"),
        P("wide", None),
        P("wide"),
        P("wide"),
        P(),
        P(),
        P(),
        P(),
        P(),
        P(),
        P(),
        P(),
        P(),
        P(),
        P(),
        P(),
        P(),
        P(),
        P(),
        P(),
        P(),
    )
    return jax.shard_map(
        per_device,
        mesh=mesh,
        in_specs=placed,
        out_specs=(
            P("wide", "narrow", None),
            P("wide", "narrow", None),
            P("wide"),
            P(None, "wide"),
            P(None, "wide"),
            P("wide"),
            P(None, "wide"),
            P("wide"),
            P(None, "wide"),
            P("wide"),
            P(None, "wide"),
            P(None, "wide"),
            P(None, "wide"),
            P(None, "wide"),
            P(None, "wide"),
            P(None, "wide"),
            P("wide"),
            P(None, "wide"),
            P(None, "wide"),
            P(None, "wide"),
        ),
        check_vma=False,
    )
```

```python
import functools
import math

import jax
import jax.numpy as jnp
from jax import lax
from jax.experimental import pallas as pl
from jax.experimental.pallas import tpu as pltpu
from jax.sharding import PartitionSpec as P

HEAD_DIM = 32
GROUPS = 32
SHORT = 48
LONG = 80


HIGH = lax.Precision.HIGHEST
EPS_GROUP = 1e-06
EPS_LAYER = 1e-05
MASKED = -1e30


TILE = 128
PER_TILE = TILE // HEAD_DIM
QB = 256
ONES = 16
SAFE_REACH = 90.0
LN2 = math.log(2.0)
bf16 = jnp.bfloat16
f32 = jnp.float32


def group_sum(value):
    grouped = value.reshape(value.shape[0], GROUPS, -1)
    summed = jnp.sum(grouped, axis=2, keepdims=True)
    return jnp.broadcast_to(summed, grouped.shape).reshape(value.shape)


def group_moments(sums, counts):
    sums = group_sum(narrow_sum(sums)) / counts[0]
    center = sums[0]
    spread = sums[1] - center * center
    return center, lax.rsqrt(spread + EPS_GROUP)


def group_means(sums, gain, counts, extras=()):
    sums = narrow_sum(jnp.concatenate([sums] + [row[None] for row in extras], axis=0))
    means = group_sum(sums[:2] * gain) / counts[0]
    return means, sums


def layer_norm(field_in, gain):
    center = jnp.mean(field_in, axis=-1, keepdims=True)
    spread = jnp.mean(jnp.square(field_in - center), axis=-1, keepdims=True)
    return (field_in - center) * lax.rsqrt(spread + EPS_LAYER) * gain


def geglu_mix(gates):
    half_width = gates.shape[-1] // 2
    return gates[..., :half_width] * jax.nn.gelu(gates[..., half_width:], approximate=False)


def head_rows(block, head):
    row = lax.broadcasted_iota(jnp.int32, block.shape, 0)
    inside = (row >= head * HEAD_DIM) & (row < (head + 1) * HEAD_DIM)
    return jnp.where(inside, block, jnp.zeros_like(block))


def head_lanes(block, head):
    lane = lax.broadcasted_iota(jnp.int32, block.shape, 1)
    inside = (lane >= head * HEAD_DIM) & (lane < (head + 1) * HEAD_DIM)
    return jnp.where(inside, block, jnp.zeros_like(block))


def mask_rows():
    row = lax.broadcasted_iota(jnp.int32, (TILE, QB), 0)
    return jnp.where(row == 0, 1.0, 0.0).astype(bf16)


def attend_kernel(first, last, parts, *refs):
    qt_ref = refs[0]
    key_refs = refs[1 : 1 + parts]
    value_refs = refs[1 + parts : 1 + 2 * parts]
    aug_ref = refs[1 + 2 * parts]
    rest = refs[2 + 2 * parts :]
    if not first:
        peak_in, acc_in = rest[:2]
        rest = rest[2:]
    if last:
        heads_ref, log_ref = rest
    else:
        peak_ref, acc_ref = rest
    keys = jnp.concatenate([ref[...] for ref in key_refs], axis=0)
    keys = jnp.concatenate([keys, aug_ref[...]], axis=1)
    values = jnp.concatenate([ref[...] for ref in value_refs], axis=0)
    value_t = jnp.transpose(values, (1, 0))
    ones = jnp.ones((ONES, value_t.shape[1]), bf16)
    low_rows = mask_rows()

    head_of = lambda shape, axis: lax.broadcasted_iota(jnp.int32, shape, axis) // HEAD_DIM
    pick = jnp.where(head_of((TILE, TILE), 0) == head_of((TILE, TILE), 1), 1.0, 0.0).astype(bf16)
    all_keys = keys[:, :TILE]
    key_norms = jnp.dot(all_keys * all_keys, pick, preferred_element_type=f32)
    all_queries = qt_ref[...]
    query_norms = jnp.dot(pick, all_queries * all_queries, preferred_element_type=f32)
    reach = jnp.float32(0.0)
    for head in range(PER_TILE):
        rows = slice(head * HEAD_DIM, head * HEAD_DIM + 8)
        mine = head_of(key_norms.shape, 1) == head
        key_peak = jnp.max(jnp.where(mine, key_norms, 0.0))
        reach = jnp.maximum(reach, key_peak * jnp.max(query_norms[rows]))

    def make_step(shifted):
        def block_step(step, carry):
            cols = pl.ds(pl.multiple_of(step * QB, QB), QB)
            qt = qt_ref[:, cols]
            for head in range(PER_TILE):
                rows = slice(head * HEAD_DIM, (head + 1) * HEAD_DIM)
                query = jnp.concatenate([head_rows(qt, head), low_rows], axis=0)
                scores = jnp.dot(keys, query, preferred_element_type=f32)
                if shifted:
                    peak = jnp.max(scores, axis=0, keepdims=True)
                    probs = jnp.exp2(scores - peak).astype(bf16)
                else:
                    peak = jnp.zeros((1, QB), f32)
                    probs = jnp.exp2(scores).astype(bf16)
                value_h = jnp.concatenate([value_t[rows], ones], axis=0)
                acc = jnp.dot(value_h, probs, preferred_element_type=f32)
                if not first:
                    peak_old = peak_in[head, 0:1, cols]
                    peak_new = jnp.maximum(peak, peak_old)
                    acc = acc * jnp.exp2(peak - peak_new)
                    acc = acc + acc_in[head, :, cols] * jnp.exp2(peak_old - peak_new)
                    peak = peak_new
                if last:
                    total = acc[HEAD_DIM : HEAD_DIM + 1]
                    heads_ref[rows, cols] = acc[:HEAD_DIM] / total
                    log_ref[head, :, cols] = jnp.broadcast_to(peak + jnp.log2(total), (8, QB))
                else:
                    acc_ref[head, :, cols] = acc
                    peak_ref[head, :, cols] = jnp.broadcast_to(peak, (8, QB))
            return carry

        return block_step

    steps = qt_ref.shape[1] // QB

    @pl.when(reach < SAFE_REACH * SAFE_REACH)
    def _():
        lax.fori_loop(0, steps, make_step(False), 0)

    @pl.when(jnp.logical_not(reach < SAFE_REACH * SAFE_REACH))
    def _():
        lax.fori_loop(0, steps, make_step(True), 0)


def chunk_specs(count, tiles, parts):
    key_spec = pl.BlockSpec((count, TILE), lambda t: (0, t))
    value_spec = pl.BlockSpec((count, TILE), lambda t: (0, tiles + t))
    aug_spec = pl.BlockSpec((parts * count, TILE), lambda t: (0, 0))
    return [key_spec] * parts + [value_spec] * parts + [aug_spec]


def attend_some(first, last, query_t, chunks, aug, state):
    channels, queries = query_t.shape
    count = chunks[0].shape[0]
    heads = channels // HEAD_DIM
    tiles = channels // TILE
    t_spec = pl.BlockSpec((TILE, queries), lambda t: (t, 0))
    cube = lambda t: (t, 0, 0)
    row_spec = pl.BlockSpec((PER_TILE, 8, queries), cube)
    acc_spec = pl.BlockSpec((PER_TILE, HEAD_DIM + ONES, queries), cube)
    in_specs = [t_spec] + chunk_specs(count, tiles, len(chunks))
    if not first:
        in_specs += [row_spec, acc_spec]
    row_shape = jax.ShapeDtypeStruct((heads, 8, queries), f32)
    if last:
        out_shape = (jax.ShapeDtypeStruct((channels, queries), f32), row_shape)
        out_specs = (t_spec, row_spec)
    else:
        out_shape = (
            row_shape,
            jax.ShapeDtypeStruct((heads, HEAD_DIM + ONES, queries), f32),
        )
        out_specs = (row_spec, acc_spec)
    return pl.pallas_call(
        functools.partial(attend_kernel, first, last, len(chunks)),
        grid=(tiles,),
        in_specs=in_specs,
        out_specs=out_specs,
        out_shape=out_shape,
        compiler_params=pltpu.CompilerParams(vmem_limit_bytes=40 << 20),
        cost_estimate=pl.CostEstimate(
            flops=32 * len(chunks) * channels * queries * count,
            bytes_accessed=8 * channels * (queries + count),
            transcendentals=len(chunks) * heads * queries * count,
        ),
        name="attend",
    )(query_t, *chunks, *chunks, aug, *state)


def attend_back_kernel(first, *refs):
    qt_ref, q_ref, dt_ref, d_ref, log_ref, heads_ref = refs[:6]
    k0_ref, k1_ref, v0_ref, v1_ref, aug_ref = refs[6:11]
    refs = refs[11:]
    if not first:
        dq_in = refs[0]
        refs = refs[1:]
    dq_ref, low_ref, high_ref, dk_acc, dv_acc = refs
    count = k0_ref.shape[0]
    k_tile = jnp.concatenate([k0_ref[...], k1_ref[...]], axis=0)
    keys = jnp.concatenate([k_tile, aug_ref[...]], axis=1)
    values = jnp.concatenate([v0_ref[...], v1_ref[...]], axis=0)
    key_t = jnp.transpose(k_tile, (1, 0))
    low_rows = mask_rows()
    dk_acc[...] = jnp.zeros_like(dk_acc)
    dv_acc[...] = jnp.zeros_like(dv_acc)
    factor = 1.0 / math.sqrt(HEAD_DIM)

    def block_step(step, carry):
        cols = pl.ds(pl.multiple_of(step * QB, QB), QB)
        qt = qt_ref[:, cols]
        dt = dt_ref[:, cols]
        q_blk = q_ref[cols, :]
        d_blk = d_ref[cols, :]
        probs_all, grads_all, q_all, d_all = [], [], [], []
        for head in range(PER_TILE):
            rows = slice(head * HEAD_DIM, (head + 1) * HEAD_DIM)
            query = jnp.concatenate([head_rows(qt, head), low_rows], axis=0)
            scores = jnp.dot(keys, query, preferred_element_type=f32)
            probs = jnp.exp2(scores - log_ref[head, 0:1, cols])
            weighted = jnp.sum(
                heads_ref[rows, cols] * dt[rows].astype(f32), axis=0, keepdims=True
            )
            grad_p = jnp.dot(values, head_rows(dt, head), preferred_element_type=f32)
            grad_s = (probs * (grad_p - weighted)).astype(bf16)
            probs_all.append(probs.astype(bf16))
            grads_all.append(grad_s)
            q_all.append(head_lanes(q_blk, head))
            d_all.append(head_lanes(d_blk, head))
            dq = jnp.dot(key_t[rows], grad_s, preferred_element_type=f32) * factor
            if not first:
                dq = dq + dq_in[rows, cols]
            dq_ref[rows, cols] = dq
        dv_acc[...] += jnp.dot(
            jnp.concatenate(probs_all, axis=1),
            jnp.concatenate(d_all, axis=0),
            preferred_element_type=f32,
        )
        dk_acc[...] += jnp.dot(
            jnp.concatenate(grads_all, axis=1),
            jnp.concatenate(q_all, axis=0),
            preferred_element_type=f32,
        )
        return carry

    lax.fori_loop(0, qt_ref.shape[1] // QB, block_step, 0)
    low_ref[0] = dk_acc[:count] * LN2
    low_ref[1] = dv_acc[:count]
    high_ref[0] = (dk_acc[count:] * LN2).astype(bf16)
    high_ref[1] = dv_acc[count:].astype(bf16)


def attend_back_pair(first, query_t, query, grad_t, grad, logs, heads_t, pair, aug, dq):
    channels, queries = query_t.shape
    count = pair[0].shape[0]
    tiles = channels // TILE
    t_spec = pl.BlockSpec((TILE, queries), lambda t: (t, 0))
    n_spec = pl.BlockSpec((queries, TILE), lambda t: (0, t))
    row_spec = pl.BlockSpec((PER_TILE, 8, queries), lambda t: (t, 0, 0))
    out_spec = pl.BlockSpec((2, count, TILE), lambda t: (0, 0, t))
    in_specs = [t_spec, n_spec, t_spec, n_spec, row_spec, t_spec] + chunk_specs(count, tiles, 2)
    state = ()
    if not first:
        in_specs.append(t_spec)
        state = (dq,)
    return pl.pallas_call(
        functools.partial(attend_back_kernel, first),
        grid=(tiles,),
        in_specs=in_specs,
        out_specs=(t_spec, out_spec, out_spec),
        out_shape=(
            jax.ShapeDtypeStruct((channels, queries), f32),
            jax.ShapeDtypeStruct((2, count, channels), f32),
            jax.ShapeDtypeStruct((2, count, channels), bf16),
        ),
        scratch_shapes=[pltpu.VMEM((2 * count, TILE), f32), pltpu.VMEM((2 * count, TILE), f32)],
        compiler_params=pltpu.CompilerParams(vmem_limit_bytes=48 << 20),
        cost_estimate=pl.CostEstimate(
            flops=160 * channels * queries * count,
            bytes_accessed=12 * channels * (queries + count),
            transcendentals=2 * channels // HEAD_DIM * queries * count,
        ),
        name="attend_back",
    )(query_t, query, grad_t, grad, logs, heads_t, pair[0], pair[1], pair[0], pair[1], aug, *state)


def swap(value, bit, axis="narrow"):
    count = lax.axis_size(axis)
    return lax.ppermute(value, axis, [(i, i ^ bit) for i in range(count)])


def low_bit(index):
    return index & -index


def axis_bits(axis):
    return [1 << level for level in range(lax.axis_size(axis).bit_length() - 1)]


def my_bit(bit, axis="narrow"):
    return (lax.axis_index(axis) // bit) % 2


def narrow_sum(value):
    for bit in axis_bits("narrow"):
        value = value + swap(value, bit)
    return value


def key_aug(keep_chunk):
    lane = lax.broadcasted_iota(jnp.int32, (keep_chunk.shape[0], TILE), 1)
    bias = jnp.where(keep_chunk[:, None] > 0, 0.0, MASKED)
    return jnp.where(lane == 0, bias, 0.0).astype(bf16)


def halve(held, axis):
    for bit in axis_bits(axis):
        halves = held.reshape((held.shape[0] // 2, 2) + held.shape[1:])
        mine = my_bit(bit, axis)
        kept = lax.dynamic_index_in_dim(halves, mine, 1, keepdims=False)
        sent = lax.dynamic_index_in_dim(halves, 1 - mine, 1, keepdims=False)
        held = (kept.astype(f32) + swap(sent, bit, axis).astype(f32)).astype(bf16)
    return held[0]


def double(value, axis):
    whole = value[None]
    for bit in reversed(axis_bits(axis)):
        other = swap(whole, bit, axis)
        pair = jnp.where(
            my_bit(bit, axis) == 0,
            jnp.stack([whole, other], axis=1),
            jnp.stack([other, whole], axis=1),
        )
        whole = pair.reshape((-1,) + value.shape)
    return whole


def conv_finish(share, rows):
    wide = lax.axis_size("wide")
    share = halve(share.reshape(wide, share.shape[0] // wide, share.shape[1]), "wide")
    whole = double(share, "narrow")
    return jnp.transpose(whole, (0, 2, 1)).reshape(-1, whole.shape[1])[:rows].astype(f32)


def by_owner(grad_t, width):
    wide = lax.axis_size("wide")
    groups = grad_t.shape[0] // wide // width
    split = grad_t.reshape(wide, groups, width, grad_t.shape[1])
    return jnp.transpose(split, (0, 2, 1, 3)).reshape(wide * width, -1)


def packed_sum(parts):
    share = lax.psum_scatter(
        parts, "wide", scatter_dimension=0, tiled=True
    ).astype(bf16)
    for bit in axis_bits("narrow"):
        share = (share.astype(f32) + swap(share, bit).astype(f32)).astype(bf16)
    return share.astype(f32)


def from_owner(share, rows):
    width = share.shape[0]
    split = share.reshape(width, -1, rows)
    return jnp.transpose(split, (2, 1, 0)).reshape(rows, -1)


def own_columns(value):
    width = value.shape[-1] // lax.axis_size("wide")
    start = lax.axis_index("wide") * width
    return lax.dynamic_slice_in_dim(value, start, width, value.ndim - 1)


CONV_LIMIT = 50 << 20


def lanes_of(meta_ref, index, start, count, channels):
    return jnp.concatenate([meta_ref[index, start : start + count]] * (channels // TILE), axis=1)


def store_shifts(field, meta_ref, stack_ref):
    total, channels = field.shape
    low = jnp.where(
        lanes_of(meta_ref, 1, 0, total, channels) > 0, pltpu.roll(field, 1, 0), 0.0
    )
    high = jnp.where(
        lanes_of(meta_ref, 2, 0, total, channels) > 0, pltpu.roll(field, total - 1, 0), 0.0
    )
    stack_ref[:, :channels] = low.astype(bf16)
    stack_ref[:, channels : 2 * channels] = field.astype(bf16)
    stack_ref[:, 2 * channels :] = high.astype(bf16)


def with_halo(low_ref, own_ref, high_ref):
    parts = [low_ref[...].astype(f32), own_ref[...].astype(f32), high_ref[...].astype(f32)]
    return jnp.concatenate(parts, axis=0)


def conv_kernel(width_ref, x_ref, low_ref, high_ref, meta_ref, rows_ref, w_ref, add_ref, y_ref, sum_ref, stack_ref):
    local, channels = x_ref.shape
    total = stack_ref.shape[0]
    width = width_ref[0]
    field = with_halo(low_ref, x_ref, high_ref)
    keep = lanes_of(meta_ref, 0, 0, total, channels)
    pre = keep * (field - rows_ref[0:1]) * (rows_ref[1:2] * rows_ref[2:3])
    store_shifts(pre / (1.0 + jnp.exp(-pre)), meta_ref, stack_ref)
    block = local // 2
    sum_ref[...] = jnp.zeros_like(sum_ref)

    def block_step(step, carry):
        start = step * block
        taps = []
        for shift in (-1, 0, 1):
            offset = pl.multiple_of(LONG + start + shift * width, 16)
            taps.append(stack_ref[pl.ds(offset, block), :])
        out = jnp.dot(jnp.concatenate(taps, axis=1), w_ref[...], preferred_element_type=f32)
        own = pl.ds(pl.multiple_of(start, 16), block)
        if add_ref.shape[0] == local:
            out = out + add_ref[own, :].astype(f32)
        else:
            out = out + add_ref[0:1]
        y_ref[own, :] = out
        kept = meta_ref[0, pl.ds(pl.multiple_of(LONG + start, 16), block), :]
        kept = out * jnp.concatenate([kept] * (channels // TILE), axis=1)
        sum_ref[0:1] += jnp.sum(kept, axis=0, keepdims=True)
        sum_ref[1:2] += jnp.sum(kept * out, axis=0, keepdims=True)
        return carry

    lax.fori_loop(0, 2, block_step, 0)


def conv_forward(width, field, halo, meta, rows, weight, add):
    local, channels = field.shape
    vmem = pl.BlockSpec(memory_space=pltpu.VMEM)
    return pl.pallas_call(
        conv_kernel,
        in_specs=[pl.BlockSpec(memory_space=pltpu.SMEM)] + [vmem] * 7,
        out_specs=(vmem, vmem),
        out_shape=(
            jax.ShapeDtypeStruct((local, channels), f32),
            jax.ShapeDtypeStruct((8, channels), f32),
        ),
        scratch_shapes=[pltpu.VMEM((local + 2 * LONG, 3 * channels), bf16)],
        compiler_params=pltpu.CompilerParams(vmem_limit_bytes=CONV_LIMIT),
        cost_estimate=pl.CostEstimate(
            flops=2 * local * weight.size,
            bytes_accessed=4 * weight.size,
            transcendentals=2 * local * channels,
        ),
        name="conv_forward",
    )(width, field, halo[0], halo[1], meta, rows, weight, add)


def conv_back_kernel(with_skip, *refs):
    width_ref, d_ref, d_low, d_high, v_ref, v_low, v_high = refs[:7]
    refs = refs[7:]
    if with_skip:
        c_ref, c_low, c_high = refs[:3]
        refs = refs[3:]
    x_ref, meta_ref, rows_ref, w_ref = refs[:4]
    e_ref, pre_ref, pack_ref, sum_ref, stack_ref, act_ref = refs[4:]
    local, channels = d_ref.shape
    total = stack_ref.shape[0]
    width = width_ref[0]
    keep = lanes_of(meta_ref, 0, 0, total, channels)
    normed = (with_halo(v_low, v_ref, v_high) - rows_ref[0:1]) * rows_ref[1:2]
    inner = with_halo(d_low, d_ref, d_high) * keep * rows_ref[2:3] - rows_ref[3:4]
    field = keep * rows_ref[1:2] * (inner - normed * rows_ref[4:5])
    if with_skip:
        field = field + with_halo(c_low, c_ref, c_high)
    e_ref[...] = field[LONG : LONG + local]
    store_shifts(field, meta_ref, stack_ref)
    sum_ref[...] = jnp.zeros_like(sum_ref)
    sum_ref[2:3] = jnp.sum(field[LONG : LONG + local], axis=0, keepdims=True)
    block = local // 2

    def block_step(step, carry):
        start = step * block
        own = pl.ds(pl.multiple_of(start, 16), block)
        out = jnp.zeros((block, channels), f32)
        for row in range(3):
            offset = pl.multiple_of(LONG + start + (row - 1) * width, 16)
            for col in range(3):
                tap = 8 - (3 * row + col)
                out = out + lax.dot_general(
                    stack_ref[pl.ds(offset, block), col * channels : (col + 1) * channels],
                    w_ref[tap * channels : (tap + 1) * channels, :],
                    (((1,), (1,)), ((), ())),
                    preferred_element_type=f32,
                )
        kept = meta_ref[0, pl.ds(pl.multiple_of(LONG + start, 16), block), :]
        kept = jnp.concatenate([kept] * (channels // TILE), axis=1)
        xhat = (x_ref[own, :].astype(f32) - rows_ref[5:6]) * rows_ref[6:7]
        pre = kept * xhat * rows_ref[7:8]
        gate = 1.0 / (1.0 + jnp.exp(-pre))
        act_ref[own, :] = (pre * gate).astype(bf16)
        grad = out * (gate * (1.0 + pre * (1.0 - gate)))
        pre_ref[own, :] = grad
        grad = grad * kept
        sum_ref[0:1] += jnp.sum(grad, axis=0, keepdims=True)
        sum_ref[1:2] += jnp.sum(grad * xhat, axis=0, keepdims=True)
        return carry

    lax.fori_loop(0, 2, block_step, 0)
    act_t = jnp.transpose(act_ref[...], (1, 0))
    groups = pack_ref.shape[2] // TILE
    tiles = channels // TILE
    for row in range(3):
        offset = pl.multiple_of(LONG + (row - 1) * width, 16)
        for col in range(3):
            tap = 8 - (3 * row + col)
            grad = jnp.dot(
                act_t,
                stack_ref[pl.ds(offset, local), col * channels : (col + 1) * channels],
                preferred_element_type=f32,
            )
            grad = jnp.transpose(grad.astype(bf16), (1, 0))
            for tile in range(tiles):
                spot = tap * tiles + tile
                lane = (spot % groups) * TILE
                pack_ref[spot // groups, :, lane : lane + TILE] = grad[:, tile * TILE : (tile + 1) * TILE]
    for spot in range(9 * tiles, pack_ref.shape[0] * groups):
        lane = (spot % groups) * TILE
        pack_ref[spot // groups, :, lane : lane + TILE] = jnp.zeros((channels, TILE), bf16)


def conv_back(width, grad, grad_halo, field, field_halo, skip, skip_halo, source, meta, rows, weight):
    local, channels = grad.shape
    count = lax.axis_size("narrow")
    vmem = pl.BlockSpec(memory_space=pltpu.VMEM)
    padded = weight.shape[0] + (-weight.shape[0] % (count * TILE))
    operands = [grad, grad_halo[0], grad_halo[1], field, field_halo[0], field_halo[1]]
    if skip is not None:
        operands += [skip, skip_halo[0], skip_halo[1]]
    operands += [source, meta, rows, weight]
    return pl.pallas_call(
        functools.partial(conv_back_kernel, skip is not None),
        in_specs=[pl.BlockSpec(memory_space=pltpu.SMEM)] + [vmem] * len(operands),
        out_specs=(vmem,) * 4,
        out_shape=(
            jax.ShapeDtypeStruct((local, channels), f32),
            jax.ShapeDtypeStruct((local, channels), f32),
            jax.ShapeDtypeStruct((count, channels, padded // count), bf16),
            jax.ShapeDtypeStruct((8, channels), f32),
        ),
        scratch_shapes=[
            pltpu.VMEM((local + 2 * LONG, 3 * channels), bf16),
            pltpu.VMEM((local, channels), bf16),
        ],
        compiler_params=pltpu.CompilerParams(vmem_limit_bytes=CONV_LIMIT),
        cost_estimate=pl.CostEstimate(
            flops=4 * local * weight.size,
            bytes_accessed=6 * weight.size,
            transcendentals=local * channels,
        ),
        name="conv_back",
    )(width, *operands)


def edge_rows(field):
    count = lax.axis_size("narrow")
    forward = [(i, i + 1) for i in range(count - 1)]
    backward = [(i + 1, i) for i in range(count - 1)]
    return (
        lax.ppermute(field[-LONG:], "narrow", forward),
        lax.ppermute(field[:LONG], "narrow", backward),
    )


def pixel_meta(keep_image, row_start, local, row_width):
    rim = jnp.pad(keep_image, (LONG, LONG))
    keep = lax.dynamic_slice_in_dim(rim, row_start, local + 2 * LONG, 0)
    spot = jnp.arange(local + 2 * LONG, dtype=jnp.int32)
    column = (spot + 2 * LONG * SHORT - LONG) % row_width
    rows = jnp.stack([keep, (column > 0).astype(f32), (column < row_width - 1).astype(f32)])
    return jnp.broadcast_to(rows[:, :, None], rows.shape + (TILE,))


def row_table(*rows):
    table = jnp.stack([jnp.broadcast_to(row.reshape(-1), rows[0].reshape(-1).shape) for row in rows])
    return jnp.pad(table, ((0, 8 - len(rows)), (0, 0)))


def per_device(
    latents,
    cotangent,
    bucket,
    pixel_mask,
    labels,
    timesteps,
    gain_first,
    conv_first,
    time_proj,
    gain_second,
    conv_second,
    gain_spatial,
    proj_in,
    gain_attn,
    attn_qkv,
    attn_out,
    class_table,
    cross_value,
    cross_out,
    gain_ff,
    geglu_in,
    geglu_out,
    proj_out,
):
    images, local_pix, channels = latents.shape
    row_start = lax.axis_index("narrow") * local_pix
    keep_all = pixel_mask.astype(jnp.float32)
    pixel_keep = lax.dynamic_slice_in_dim(keep_all, row_start, local_pix, 1)[0, :, None]
    counts = jnp.sum(keep_all, axis=1) * (channels // GROUPS)
    row_width = jnp.where(bucket[0] == 0, LONG, SHORT).astype(jnp.int32)
    width = row_width[None]
    meta = pixel_meta(keep_all[0], row_start, local_pix, row_width)
    pixels = latents[0]
    pixel_halo = edge_rows(pixels)
    skip = cotangent[0]
    skip_halo = edge_rows(skip)
    half_dim = time_proj.shape[0] // 2
    frequency = jnp.exp(-math.log(10000.0) * jnp.arange(half_dim, dtype=jnp.float32) / half_dim)
    angles = timesteps.astype(jnp.float32)[:, None] * frequency[None, :]
    time_act = jax.nn.silu(jnp.concatenate([jnp.cos(angles), jnp.sin(angles)], axis=1))
    time_term = jnp.dot(time_act, time_proj.astype(jnp.float32), precision=HIGH)
    label_hot = (
        labels[:, None] == jnp.arange(class_table.shape[0], dtype=jnp.int32)[None, :]
    ).astype(jnp.float32)
    context = jnp.dot(label_hot, class_table.astype(jnp.float32), precision=HIGH)
    value_weight = cross_value.astype(jnp.float32)
    cross_weight = cross_out.astype(jnp.float32)
    value_term = jnp.dot(context, value_weight, precision=HIGH)
    cross_term = jnp.dot(value_term, cross_weight, precision=HIGH)
    gain_one = gain_first.astype(jnp.float32)
    gain_two = gain_second.astype(jnp.float32)
    gain_three = gain_spatial.astype(jnp.float32)
    image_in = pixels.astype(jnp.float32)
    kept = image_in * pixel_keep
    sums_one = jnp.stack([jnp.sum(kept, axis=0), jnp.sum(kept * image_in, axis=0)])
    center_one, scale_one = group_moments(sums_one, counts)
    hidden, sums_two = conv_forward(
        width,
        pixels,
        pixel_halo,
        meta,
        row_table(center_one, scale_one, gain_one),
        conv_first,
        row_table(time_term[0]),
    )
    hidden_halo = edge_rows(hidden)
    center_two, scale_two = group_moments(sums_two[:2], counts)
    residual, sums_three = conv_forward(
        width,
        hidden,
        hidden_halo,
        meta,
        row_table(center_two, scale_two, gain_two),
        conv_second,
        pixels,
    )
    residual_halo = edge_rows(residual)
    center_three, scale_three = group_moments(sums_three[:2], counts)
    residual_hat = (residual - center_three) * scale_three
    spatial = (pixel_keep * residual_hat * gain_three).astype(jnp.bfloat16)[None]
    stream = jnp.einsum("npc,cd->npd", spatial, proj_in, preferred_element_type=jnp.float32)
    normed_attn, attn_pull = jax.vjp(layer_norm, stream, gain_attn.astype(jnp.float32))
    normed_attn = normed_attn.astype(jnp.bfloat16)
    packed_f = jnp.einsum("npc,cd->npd", normed_attn, attn_qkv, preferred_element_type=jnp.float32)
    query_pix = (packed_f[0, :, :channels] * (1.0 / (math.sqrt(HEAD_DIM) * LN2))).astype(bf16)
    pad_pix = -local_pix % QB
    query_pix = jnp.pad(query_pix, ((0, pad_pix), (0, 0)))
    query_t = query_pix.T
    key_value = packed_f[0, :, channels:].astype(bf16)
    count = lax.axis_size("narrow")
    position = lax.axis_index("narrow")
    chunks = [key_value] + [None] * (count - 1)
    for bit in axis_bits("narrow"):
        chunks[bit] = swap(key_value, bit)
    keep_chunk = lambda index: lax.dynamic_slice_in_dim(
        keep_all[0], (position ^ index) * local_pix, local_pix, 0
    )
    keeps = [keep_chunk(index) for index in range(count)]
    augs = [
        key_aug(jnp.concatenate([keeps[index], keeps[index + 1]])) for index in range(0, count, 2)
    ]
    state = attend_some(True, count == 2, query_t, chunks[:2], augs[0], ())
    for index in range(2, count):
        bit = low_bit(index)
        if index != bit:
            chunks[index] = swap(chunks[index ^ bit], bit)
        elif index < count - 1:
            chunks[index], state = lax.optimization_barrier((chunks[index], state))
    for index in range(2, count):
        state = attend_some(
            False, index == count - 1, query_t, [chunks[index]], key_aug(keeps[index]), state
        )
    pairs = [chunks[index : index + 2] for index in range(0, count, 2)]
    heads_t, log_rows = state
    heads_rows = heads_t.T[None, :local_pix].astype(bf16)
    stream_mid = (
        stream
        + jnp.einsum("npc,cd->npd", heads_rows, attn_out, preferred_element_type=jnp.float32)
        + cross_term[:, None, :]
    )
    normed_ff, ff_pull = jax.vjp(layer_norm, stream_mid, gain_ff.astype(jnp.float32))
    normed_ff = normed_ff.astype(jnp.bfloat16)
    gates = jnp.einsum("npc,cf->npf", normed_ff, geglu_in, preferred_element_type=jnp.float32)
    mixed, gate_pull = jax.vjp(geglu_mix, gates)
    mixed = mixed.astype(jnp.bfloat16)
    stream_end = stream_mid + jnp.einsum(
        "npf,fc->npc", mixed, geglu_out, preferred_element_type=jnp.float32
    )
    top_in = stream_end.astype(jnp.bfloat16)
    output = (
        residual[None]
        + jnp.einsum("npc,cd->npd", top_in, proj_out, preferred_element_type=jnp.float32)
    ).astype(jnp.bfloat16)
    grad_proj_out = jnp.einsum("npc,npd->dc", top_in, cotangent, preferred_element_type=jnp.float32)
    grad_end = jnp.einsum("npd,cd->npc", cotangent, proj_out, preferred_element_type=jnp.float32)
    grad_ffo = grad_end.astype(jnp.bfloat16)
    grad_geglu_out = jnp.einsum("npf,npc->cf", mixed, grad_ffo, preferred_element_type=jnp.float32)
    grad_mixed = jnp.einsum("npc,fc->npf", grad_ffo, geglu_out, preferred_element_type=jnp.float32)
    grad_gates = gate_pull(grad_mixed)[0].astype(jnp.bfloat16)
    grad_geglu_in = jnp.einsum(
        "npc,npf->fc", normed_ff, grad_gates, preferred_element_type=jnp.float32
    )
    grad_normed = jnp.einsum(
        "npf,cf->npc", grad_gates, geglu_in, preferred_element_type=jnp.float32
    )
    grad_from_ff, grad_gain_ff = ff_pull(grad_normed)
    grad_mid = grad_end + grad_from_ff
    grad_cross = jnp.sum(grad_mid, axis=1)
    grad_attn_in = grad_mid.astype(jnp.bfloat16)
    grad_attn_out = jnp.einsum(
        "npc,npd->dc", heads_rows, grad_attn_in, preferred_element_type=jnp.float32
    )
    grad_heads_rows = jnp.einsum(
        "npd,cd->npc", grad_attn_in, attn_out, preferred_element_type=jnp.float32
    ).astype(jnp.bfloat16)
    owned = channels // lax.axis_size("wide")
    top_parts = jnp.concatenate(
        [
            grad_proj_out,
            grad_attn_out,
            grad_geglu_out,
            by_owner(grad_geglu_in, owned),
        ],
        axis=1,
    )
    top_parts, grad_heads_rows = lax.optimization_barrier((top_parts, grad_heads_rows))
    top = packed_sum(top_parts)
    grad_rows = jnp.pad(grad_heads_rows[0], ((0, pad_pix), (0, 0)))
    grad_t = grad_rows.T
    grad_query_t = None
    arrived = [None] * count
    for index in reversed(range(len(pairs))):
        grad_query_t, grad_low, grad_high = attend_back_pair(
            index == len(pairs) - 1,
            query_t,
            query_pix,
            grad_t,
            grad_rows,
            log_rows,
            heads_t,
            pairs[index],
            augs[index],
            grad_query_t,
        )
        total = grad_low + swap(grad_high, 1).astype(f32)
        for source in range(index + 1, len(pairs)):
            bit = low_bit(2 * source)
            if (2 * source) ^ bit == 2 * index:
                total = total + arrived[source].astype(f32)
        if index:
            arrived[index] = swap(total.astype(bf16), low_bit(2 * index))
    grad_packed = jnp.concatenate(
        [
            grad_query_t.T[:local_pix].astype(bf16),
            total[0].astype(bf16),
            total[1].astype(bf16),
        ],
        axis=1,
    )[None]
    grad_attn_whole = jnp.einsum(
        "npc,npd->dc", normed_attn, grad_packed, preferred_element_type=jnp.float32
    )
    grad_normed_attn = jnp.einsum(
        "npd,cd->npc", grad_packed, attn_qkv, preferred_element_type=jnp.float32
    )
    grad_from_attn, grad_gain_attn = attn_pull(grad_normed_attn)
    grad_stream = (grad_mid + grad_from_attn).astype(jnp.bfloat16)
    grad_proj_in = jnp.einsum(
        "npc,npd->dc", spatial, grad_stream, preferred_element_type=jnp.float32
    )
    grad_spatial = jnp.einsum(
        "npd,cd->npc", grad_stream, proj_in, preferred_element_type=jnp.float32
    )
    low_parts = jnp.concatenate(
        [
            grad_proj_in,
            by_owner(grad_attn_whole[: 2 * channels], owned),
            grad_attn_whole[2 * channels :],
        ],
        axis=1,
    )
    low_parts, grad_spatial = lax.optimization_barrier((low_parts, grad_spatial[0]))
    low_part = packed_sum(low_parts)
    grad_halo = edge_rows(grad_spatial)
    kept = grad_spatial * pixel_keep
    sums = jnp.stack([jnp.sum(kept, axis=0), jnp.sum(kept * residual_hat, axis=0)])
    means, early_rows = group_means(
        sums, gain_three, counts, [grad_cross[0], grad_gain_ff, grad_gain_attn]
    )
    grad_res, grad_pre, pack_second, sums = conv_back(
        width,
        grad_spatial,
        grad_halo,
        residual,
        residual_halo,
        skip,
        skip_halo,
        hidden,
        meta,
        row_table(
            center_three,
            scale_three,
            gain_three,
            means[0],
            means[1],
            center_two,
            scale_two,
            gain_two,
        ),
        conv_second,
    )
    grad_halo = edge_rows(grad_pre)
    means, middle_rows = group_means(sums[:2], gain_two, counts)
    share_second = halve(pack_second, "narrow")
    grad_hidden, grad_pre, pack_first, sums = conv_back(
        width,
        grad_pre,
        grad_halo,
        hidden,
        hidden_halo,
        None,
        None,
        pixels,
        meta,
        row_table(
            center_two,
            scale_two,
            gain_two,
            means[0],
            means[1],
            center_one,
            scale_one,
            gain_one,
        ),
        conv_first,
    )
    means, late_rows = group_means(sums[:3], gain_one, counts)
    share_first = halve(pack_first, "narrow")
    image_hat = (image_in - center_one) * scale_one
    grad_image = grad_pre * pixel_keep * gain_one - means[0] - image_hat * means[1]
    grad_latents = (grad_res + pixel_keep * scale_one * grad_image).astype(jnp.bfloat16)[None]
    conv_rows = conv_first.shape[0]
    sum_conv_second = conv_finish(share_second, conv_rows)
    sum_conv_first = conv_finish(share_first, conv_rows)
    stamp_row = jnp.pad(
        jnp.concatenate([labels, timesteps]).astype(f32), (0, channels - 2 * images)
    )
    spread = double(
        jnp.stack(
            [
                early_rows[2],
                late_rows[2],
                early_rows[3],
                early_rows[4],
                early_rows[1],
                middle_rows[1],
                late_rows[1],
                stamp_row,
            ]
        ),
        "wide",
    )
    labels_all = spread[:, 7, 0].astype(jnp.int32)
    steps_all = spread[:, 7, 1].astype(jnp.int32)
    angles_all = steps_all.astype(jnp.float32)[:, None] * frequency[None, :]
    time_all = jax.nn.silu(jnp.concatenate([jnp.cos(angles_all), jnp.sin(angles_all)], axis=1))
    hot_all = (
        labels_all[:, None] == jnp.arange(class_table.shape[0], dtype=jnp.int32)[None, :]
    ).astype(jnp.float32)
    context_all = jnp.dot(hot_all, class_table.astype(jnp.float32), precision=HIGH)
    value_all = jnp.dot(context_all, value_weight, precision=HIGH)
    cross_all = spread[:, 0]
    grad_value_all = jnp.dot(cross_all, cross_weight.T, precision=HIGH)
    grad_context_all = jnp.dot(grad_value_all, value_weight.T, precision=HIGH)
    sum_cross_out = jnp.dot(value_all.T, own_columns(cross_all), precision=HIGH)
    sum_cross_value = jnp.dot(context_all.T, own_columns(grad_value_all), precision=HIGH)
    sum_class_table = jnp.dot(hot_all.T, own_columns(grad_context_all), precision=HIGH)
    sum_time_proj = jnp.dot(time_all.T, own_columns(spread[:, 1]), precision=HIGH)
    gain_sums = own_columns(jnp.sum(spread[:, 2:7], axis=0))
    return (
        output,
        grad_latents,
        gain_sums[4],
        sum_conv_first,
        sum_time_proj,
        gain_sums[3],
        sum_conv_second,
        gain_sums[2],
        from_owner(low_part[:, :channels], channels),
        gain_sums[1],
        from_owner(low_part[:, channels : 3 * channels], channels),
        from_owner(low_part[:, 3 * channels :], channels),
        from_owner(top[:, channels : 2 * channels], channels),
        sum_class_table,
        sum_cross_value,
        sum_cross_out,
        gain_sums[0],
        from_owner(top[:, 2 * channels + geglu_out.shape[0] :], channels),
        from_owner(top[:, 2 * channels : 2 * channels + geglu_out.shape[0]], geglu_out.shape[0]),
        from_owner(top[:, :channels], channels),
    )


def solution(mesh):
    placed = (
        P("wide", "narrow", None),
        P("wide", "narrow", None),
        P("wide"),
        P("wide", None),
        P("wide"),
        P("wide"),
        P(),
        P(),
        P(),
        P(),
        P(),
        P(),
        P(),
        P(),
        P(),
        P(),
        P(),
        P(),
        P(),
        P(),
        P(),
        P(),
        P(),
    )
    return jax.shard_map(
        per_device,
        mesh=mesh,
        in_specs=placed,
        out_specs=(
            P("wide", "narrow", None),
            P("wide", "narrow", None),
            P("wide"),
            P(None, "wide"),
            P(None, "wide"),
            P("wide"),
            P(None, "wide"),
            P("wide"),
            P(None, "wide"),
            P("wide"),
            P(None, "wide"),
            P(None, "wide"),
            P(None, "wide"),
            P(None, "wide"),
            P(None, "wide"),
            P(None, "wide"),
            P("wide"),
            P(None, "wide"),
            P(None, "wide"),
            P(None, "wide"),
        ),
        check_vma=False,
    )
```

```python
import functools
import math

import jax
import jax.numpy as jnp
from jax import lax
from jax.experimental import pallas as pl
from jax.experimental.pallas import tpu as pltpu
from jax.sharding import PartitionSpec as P

HEAD_DIM = 32
GROUPS = 32
SHORT = 48
LONG = 80


HIGH = lax.Precision.HIGHEST
EPS_GROUP = 1e-06
EPS_LAYER = 1e-05
MASKED = -1e30


TILE = 128
PER_TILE = TILE // HEAD_DIM
QB = 256
ONES = 16
SAFE_REACH = 90.0
LN2 = math.log(2.0)
bf16 = jnp.bfloat16
f32 = jnp.float32


def group_sum(value):
    grouped = value.reshape(value.shape[0], GROUPS, -1)
    summed = jnp.sum(grouped, axis=2, keepdims=True)
    return jnp.broadcast_to(summed, grouped.shape).reshape(value.shape)


def group_moments(sums, counts):
    sums = group_sum(narrow_sum(sums)) / counts[0]
    center = sums[0]
    spread = sums[1] - center * center
    return center, lax.rsqrt(spread + EPS_GROUP)


def group_means(sums, gain, counts, extras=()):
    sums = narrow_sum(jnp.concatenate([sums] + [row[None] for row in extras], axis=0))
    means = group_sum(sums[:2] * gain) / counts[0]
    return means, sums


def layer_norm(field_in, gain):
    center = jnp.mean(field_in, axis=-1, keepdims=True)
    spread = jnp.mean(jnp.square(field_in - center), axis=-1, keepdims=True)
    return (field_in - center) * lax.rsqrt(spread + EPS_LAYER) * gain


def geglu_mix(gates):
    half_width = gates.shape[-1] // 2
    return gates[..., :half_width] * jax.nn.gelu(gates[..., half_width:], approximate=False)


def head_rows(block, head):
    row = lax.broadcasted_iota(jnp.int32, block.shape, 0)
    inside = (row >= head * HEAD_DIM) & (row < (head + 1) * HEAD_DIM)
    return jnp.where(inside, block, jnp.zeros_like(block))


def head_lanes(block, head):
    lane = lax.broadcasted_iota(jnp.int32, block.shape, 1)
    inside = (lane >= head * HEAD_DIM) & (lane < (head + 1) * HEAD_DIM)
    return jnp.where(inside, block, jnp.zeros_like(block))


def mask_rows():
    row = lax.broadcasted_iota(jnp.int32, (TILE, QB), 0)
    return jnp.where(row == 0, 1.0, 0.0).astype(bf16)


def attend_kernel(first, last, parts, *refs):
    qt_ref = refs[0]
    key_refs = refs[1 : 1 + parts]
    value_refs = refs[1 + parts : 1 + 2 * parts]
    aug_ref = refs[1 + 2 * parts]
    rest = refs[2 + 2 * parts :]
    if not first:
        peak_in, acc_in = rest[:2]
        rest = rest[2:]
    if last:
        heads_ref, log_ref = rest
    else:
        peak_ref, acc_ref = rest
    keys = jnp.concatenate([ref[...] for ref in key_refs], axis=0)
    keys = jnp.concatenate([keys, aug_ref[...]], axis=1)
    values = jnp.concatenate([ref[...] for ref in value_refs], axis=0)
    value_t = jnp.transpose(values, (1, 0))
    ones = jnp.ones((ONES, value_t.shape[1]), bf16)
    low_rows = mask_rows()

    head_of = lambda shape, axis: lax.broadcasted_iota(jnp.int32, shape, axis) // HEAD_DIM
    pick = jnp.where(head_of((TILE, TILE), 0) == head_of((TILE, TILE), 1), 1.0, 0.0).astype(bf16)
    all_keys = keys[:, :TILE]
    key_norms = jnp.dot(all_keys * all_keys, pick, preferred_element_type=f32)
    all_queries = qt_ref[...]
    query_norms = jnp.dot(pick, all_queries * all_queries, preferred_element_type=f32)
    reach = jnp.float32(0.0)
    for head in range(PER_TILE):
        rows = slice(head * HEAD_DIM, head * HEAD_DIM + 8)
        mine = head_of(key_norms.shape, 1) == head
        key_peak = jnp.max(jnp.where(mine, key_norms, 0.0))
        reach = jnp.maximum(reach, key_peak * jnp.max(query_norms[rows]))

    def make_step(shifted):
        def block_step(step, carry):
            cols = pl.ds(pl.multiple_of(step * QB, QB), QB)
            qt = qt_ref[:, cols]
            for head in range(PER_TILE):
                rows = slice(head * HEAD_DIM, (head + 1) * HEAD_DIM)
                query = jnp.concatenate([head_rows(qt, head), low_rows], axis=0)
                scores = jnp.dot(keys, query, preferred_element_type=f32)
                if shifted:
                    peak = jnp.max(scores, axis=0, keepdims=True)
                    probs = jnp.exp2(scores - peak).astype(bf16)
                else:
                    peak = jnp.zeros((1, QB), f32)
                    probs = jnp.exp2(scores).astype(bf16)
                value_h = jnp.concatenate([value_t[rows], ones], axis=0)
                acc = jnp.dot(value_h, probs, preferred_element_type=f32)
                if not first:
                    peak_old = peak_in[head, 0:1, cols]
                    peak_new = jnp.maximum(peak, peak_old)
                    acc = acc * jnp.exp2(peak - peak_new)
                    acc = acc + acc_in[head, :, cols] * jnp.exp2(peak_old - peak_new)
                    peak = peak_new
                if last:
                    total = acc[HEAD_DIM : HEAD_DIM + 1]
                    heads_ref[rows, cols] = acc[:HEAD_DIM] / total
                    log_ref[head, :, cols] = jnp.broadcast_to(peak + jnp.log2(total), (8, QB))
                else:
                    acc_ref[head, :, cols] = acc
                    peak_ref[head, :, cols] = jnp.broadcast_to(peak, (8, QB))
            return carry

        return block_step

    steps = qt_ref.shape[1] // QB

    @pl.when(reach < SAFE_REACH * SAFE_REACH)
    def _():
        lax.fori_loop(0, steps, make_step(False), 0)

    @pl.when(jnp.logical_not(reach < SAFE_REACH * SAFE_REACH))
    def _():
        lax.fori_loop(0, steps, make_step(True), 0)


def chunk_specs(count, tiles, parts):
    key_spec = pl.BlockSpec((count, TILE), lambda t: (0, t))
    value_spec = pl.BlockSpec((count, TILE), lambda t: (0, tiles + t))
    aug_spec = pl.BlockSpec((parts * count, TILE), lambda t: (0, 0))
    return [key_spec] * parts + [value_spec] * parts + [aug_spec]


def attend_some(first, last, query_t, chunks, aug, state):
    channels, queries = query_t.shape
    count = chunks[0].shape[0]
    heads = channels // HEAD_DIM
    tiles = channels // TILE
    t_spec = pl.BlockSpec((TILE, queries), lambda t: (t, 0))
    cube = lambda t: (t, 0, 0)
    row_spec = pl.BlockSpec((PER_TILE, 8, queries), cube)
    acc_spec = pl.BlockSpec((PER_TILE, HEAD_DIM + ONES, queries), cube)
    in_specs = [t_spec] + chunk_specs(count, tiles, len(chunks))
    if not first:
        in_specs += [row_spec, acc_spec]
    row_shape = jax.ShapeDtypeStruct((heads, 8, queries), f32)
    if last:
        out_shape = (jax.ShapeDtypeStruct((channels, queries), f32), row_shape)
        out_specs = (t_spec, row_spec)
    else:
        out_shape = (
            row_shape,
            jax.ShapeDtypeStruct((heads, HEAD_DIM + ONES, queries), f32),
        )
        out_specs = (row_spec, acc_spec)
    return pl.pallas_call(
        functools.partial(attend_kernel, first, last, len(chunks)),
        grid=(tiles,),
        in_specs=in_specs,
        out_specs=out_specs,
        out_shape=out_shape,
        compiler_params=pltpu.CompilerParams(vmem_limit_bytes=40 << 20),
        cost_estimate=pl.CostEstimate(
            flops=32 * len(chunks) * channels * queries * count,
            bytes_accessed=8 * channels * (queries + count),
            transcendentals=len(chunks) * heads * queries * count,
        ),
        name="attend",
    )(query_t, *chunks, *chunks, aug, *state)


def attend_back_kernel(first, parts, *refs):
    qt_ref, q_ref, dt_ref, d_ref, log_ref, heads_ref = refs[:6]
    key_refs = refs[6 : 6 + parts]
    value_refs = refs[6 + parts : 6 + 2 * parts]
    aug_ref = refs[6 + 2 * parts]
    refs = refs[7 + 2 * parts :]
    if not first:
        dq_in = refs[0]
        refs = refs[1:]
    dq_ref = refs[0]
    out_refs = refs[1 : 1 + parts]
    dk_acc, dv_acc = refs[1 + parts :]
    count = key_refs[0].shape[0]
    k_tile = jnp.concatenate([ref[...] for ref in key_refs], axis=0)
    keys = jnp.concatenate([k_tile, aug_ref[...]], axis=1)
    values = jnp.concatenate([ref[...] for ref in value_refs], axis=0)
    key_t = jnp.transpose(k_tile, (1, 0))
    low_rows = mask_rows()
    dk_acc[...] = jnp.zeros_like(dk_acc)
    dv_acc[...] = jnp.zeros_like(dv_acc)
    factor = 1.0 / math.sqrt(HEAD_DIM)

    def block_step(step, carry):
        cols = pl.ds(pl.multiple_of(step * QB, QB), QB)
        qt = qt_ref[:, cols]
        dt = dt_ref[:, cols]
        q_blk = q_ref[cols, :]
        d_blk = d_ref[cols, :]
        probs_all, grads_all, q_all, d_all = [], [], [], []
        for head in range(PER_TILE):
            rows = slice(head * HEAD_DIM, (head + 1) * HEAD_DIM)
            query = jnp.concatenate([head_rows(qt, head), low_rows], axis=0)
            scores = jnp.dot(keys, query, preferred_element_type=f32)
            probs = jnp.exp2(scores - log_ref[head, 0:1, cols])
            weighted = jnp.sum(
                heads_ref[rows, cols] * dt[rows].astype(f32), axis=0, keepdims=True
            )
            grad_p = jnp.dot(values, head_rows(dt, head), preferred_element_type=f32)
            grad_s = (probs * (grad_p - weighted)).astype(bf16)
            probs_all.append(probs.astype(bf16))
            grads_all.append(grad_s)
            q_all.append(head_lanes(q_blk, head))
            d_all.append(head_lanes(d_blk, head))
            dq = jnp.dot(key_t[rows], grad_s, preferred_element_type=f32) * factor
            if not first:
                dq = dq + dq_in[rows, cols]
            dq_ref[rows, cols] = dq
        dv_acc[...] += jnp.dot(
            jnp.concatenate(probs_all, axis=1),
            jnp.concatenate(d_all, axis=0),
            preferred_element_type=f32,
        )
        dk_acc[...] += jnp.dot(
            jnp.concatenate(grads_all, axis=1),
            jnp.concatenate(q_all, axis=0),
            preferred_element_type=f32,
        )
        return carry

    lax.fori_loop(0, qt_ref.shape[1] // QB, block_step, 0)
    for index, ref in enumerate(out_refs):
        rows = slice(index * count, (index + 1) * count)
        ref[0] = (dk_acc[rows] * LN2).astype(ref.dtype)
        ref[1] = dv_acc[rows].astype(ref.dtype)


def attend_back_some(
    first, out_types, query_t, query, grad_t, grad, logs, heads_t, chunks, aug, dq
):
    channels, queries = query_t.shape
    count = chunks[0].shape[0]
    parts = len(chunks)
    tiles = channels // TILE
    t_spec = pl.BlockSpec((TILE, queries), lambda t: (t, 0))
    n_spec = pl.BlockSpec((queries, TILE), lambda t: (0, t))
    row_spec = pl.BlockSpec((PER_TILE, 8, queries), lambda t: (t, 0, 0))
    out_spec = pl.BlockSpec((2, count, TILE), lambda t: (0, 0, t))
    in_specs = [t_spec, n_spec, t_spec, n_spec, row_spec, t_spec] + chunk_specs(count, tiles, parts)
    state = ()
    if not first:
        in_specs.append(t_spec)
        state = (dq,)
    return pl.pallas_call(
        functools.partial(attend_back_kernel, first, parts),
        grid=(tiles,),
        in_specs=in_specs,
        out_specs=(t_spec,) + (out_spec,) * parts,
        out_shape=(jax.ShapeDtypeStruct((channels, queries), f32),)
        + tuple(jax.ShapeDtypeStruct((2, count, channels), kind) for kind in out_types),
        scratch_shapes=[pltpu.VMEM((parts * count, TILE), f32)] * 2,
        compiler_params=pltpu.CompilerParams(vmem_limit_bytes=48 << 20),
        cost_estimate=pl.CostEstimate(
            flops=80 * parts * channels * queries * count,
            bytes_accessed=12 * channels * (queries + count),
            transcendentals=parts * channels // HEAD_DIM * queries * count,
        ),
        name="attend_back",
    )(query_t, query, grad_t, grad, logs, heads_t, *chunks, *chunks, aug, *state)


def swap(value, bit, axis="narrow"):
    count = lax.axis_size(axis)
    return lax.ppermute(value, axis, [(i, i ^ bit) for i in range(count)])


def low_bit(index):
    return index & -index


def axis_bits(axis):
    return [1 << level for level in range(lax.axis_size(axis).bit_length() - 1)]


def my_bit(bit, axis="narrow"):
    return (lax.axis_index(axis) // bit) % 2


def narrow_sum(value):
    for bit in axis_bits("narrow"):
        value = value + swap(value, bit)
    return value


def key_aug(keep_chunk):
    lane = lax.broadcasted_iota(jnp.int32, (keep_chunk.shape[0], TILE), 1)
    bias = jnp.where(keep_chunk[:, None] > 0, 0.0, MASKED)
    return jnp.where(lane == 0, bias, 0.0).astype(bf16)


def halve_step(held, bit, axis):
    halves = held.reshape((held.shape[0] // 2, 2) + held.shape[1:])
    mine = my_bit(bit, axis)
    kept = lax.dynamic_index_in_dim(halves, mine, 1, keepdims=False)
    sent = lax.dynamic_index_in_dim(halves, 1 - mine, 1, keepdims=False)
    return (kept.astype(f32) + swap(sent, bit, axis).astype(f32)).astype(bf16)


def halve(held, axis):
    for bit in axis_bits(axis):
        held = halve_step(held, bit, axis)
    return held[0]


def double(value, axis):
    whole = value[None]
    for bit in reversed(axis_bits(axis)):
        other = swap(whole, bit, axis)
        pair = jnp.where(
            my_bit(bit, axis) == 0,
            jnp.stack([whole, other], axis=1),
            jnp.stack([other, whole], axis=1),
        )
        whole = pair.reshape((-1,) + value.shape)
    return whole


def wide_finish(share):
    wide = lax.axis_size("wide")
    share = halve(share.reshape(wide, share.shape[0] // wide, share.shape[1]), "wide")
    return double(share, "narrow")


def conv_finish(whole, rows):
    return jnp.transpose(whole, (0, 2, 1)).reshape(-1, whole.shape[1])[:rows].astype(f32)


def by_owner(grad_t, width):
    wide = lax.axis_size("wide")
    groups = grad_t.shape[0] // wide // width
    split = grad_t.reshape(wide, groups, width, grad_t.shape[1])
    return jnp.transpose(split, (0, 2, 1, 3)).reshape(wide * width, -1)


def wide_scatter(parts):
    return lax.psum_scatter(parts, "wide", scatter_dimension=0, tiled=True)


def narrow_finish(share):
    share = share.astype(bf16)
    for bit in axis_bits("narrow"):
        share = (share.astype(f32) + swap(share, bit).astype(f32)).astype(bf16)
    return share.astype(f32)


def from_owner(share, rows):
    width = share.shape[0]
    split = share.reshape(width, -1, rows)
    return jnp.transpose(split, (2, 1, 0)).reshape(rows, -1)


def own_columns(value):
    width = value.shape[-1] // lax.axis_size("wide")
    start = lax.axis_index("wide") * width
    return lax.dynamic_slice_in_dim(value, start, width, value.ndim - 1)


CONV_LIMIT = 50 << 20


def lanes_of(meta_ref, index, start, count, channels):
    return jnp.concatenate([meta_ref[index, start : start + count]] * (channels // TILE), axis=1)


def store_shifts(field, meta_ref, stack_ref):
    total, channels = field.shape
    low = jnp.where(
        lanes_of(meta_ref, 1, 0, total, channels) > 0, pltpu.roll(field, 1, 0), 0.0
    )
    high = jnp.where(
        lanes_of(meta_ref, 2, 0, total, channels) > 0, pltpu.roll(field, total - 1, 0), 0.0
    )
    stack_ref[:, :channels] = low.astype(bf16)
    stack_ref[:, channels : 2 * channels] = field.astype(bf16)
    stack_ref[:, 2 * channels :] = high.astype(bf16)


def with_halo(low_ref, own_ref, high_ref):
    parts = [low_ref[...].astype(f32), own_ref[...].astype(f32), high_ref[...].astype(f32)]
    return jnp.concatenate(parts, axis=0)


def conv_kernel(width_ref, x_ref, low_ref, high_ref, meta_ref, rows_ref, w_ref, add_ref, y_ref, sum_ref, stack_ref):
    local, channels = x_ref.shape
    total = stack_ref.shape[0]
    width = width_ref[0]
    field = with_halo(low_ref, x_ref, high_ref)
    keep = lanes_of(meta_ref, 0, 0, total, channels)
    pre = keep * (field - rows_ref[0:1]) * (rows_ref[1:2] * rows_ref[2:3])
    store_shifts(pre / (1.0 + jnp.exp(-pre)), meta_ref, stack_ref)
    block = local // 2
    sum_ref[...] = jnp.zeros_like(sum_ref)

    def block_step(step, carry):
        start = step * block
        taps = []
        for shift in (-1, 0, 1):
            offset = pl.multiple_of(LONG + start + shift * width, 16)
            taps.append(stack_ref[pl.ds(offset, block), :])
        out = jnp.dot(jnp.concatenate(taps, axis=1), w_ref[...], preferred_element_type=f32)
        own = pl.ds(pl.multiple_of(start, 16), block)
        if add_ref.shape[0] == local:
            out = out + add_ref[own, :].astype(f32)
        else:
            out = out + add_ref[0:1]
        y_ref[own, :] = out
        kept = meta_ref[0, pl.ds(pl.multiple_of(LONG + start, 16), block), :]
        kept = out * jnp.concatenate([kept] * (channels // TILE), axis=1)
        sum_ref[0:1] += jnp.sum(kept, axis=0, keepdims=True)
        sum_ref[1:2] += jnp.sum(kept * out, axis=0, keepdims=True)
        return carry

    lax.fori_loop(0, 2, block_step, 0)


def conv_forward(width, field, halo, meta, rows, weight, add):
    local, channels = field.shape
    vmem = pl.BlockSpec(memory_space=pltpu.VMEM)
    return pl.pallas_call(
        conv_kernel,
        in_specs=[pl.BlockSpec(memory_space=pltpu.SMEM)] + [vmem] * 7,
        out_specs=(vmem, vmem),
        out_shape=(
            jax.ShapeDtypeStruct((local, channels), f32),
            jax.ShapeDtypeStruct((8, channels), f32),
        ),
        scratch_shapes=[pltpu.VMEM((local + 2 * LONG, 3 * channels), bf16)],
        compiler_params=pltpu.CompilerParams(vmem_limit_bytes=CONV_LIMIT),
        cost_estimate=pl.CostEstimate(
            flops=2 * local * weight.size,
            bytes_accessed=4 * weight.size,
            transcendentals=2 * local * channels,
        ),
        name="conv_forward",
    )(width, field, halo[0], halo[1], meta, rows, weight, add)


def conv_back_kernel(with_skip, *refs):
    width_ref, d_ref, d_low, d_high, v_ref, v_low, v_high = refs[:7]
    refs = refs[7:]
    if with_skip:
        c_ref, c_low, c_high = refs[:3]
        refs = refs[3:]
    x_ref, meta_ref, rows_ref, w_ref = refs[:4]
    e_ref, pre_ref, pack_ref, sum_ref, stack_ref, act_ref = refs[4:]
    local, channels = d_ref.shape
    total = stack_ref.shape[0]
    width = width_ref[0]
    keep = lanes_of(meta_ref, 0, 0, total, channels)
    normed = (with_halo(v_low, v_ref, v_high) - rows_ref[0:1]) * rows_ref[1:2]
    inner = with_halo(d_low, d_ref, d_high) * keep * rows_ref[2:3] - rows_ref[3:4]
    field = keep * rows_ref[1:2] * (inner - normed * rows_ref[4:5])
    if with_skip:
        field = field + with_halo(c_low, c_ref, c_high)
    e_ref[...] = field[LONG : LONG + local]
    store_shifts(field, meta_ref, stack_ref)
    sum_ref[...] = jnp.zeros_like(sum_ref)
    sum_ref[2:3] = jnp.sum(field[LONG : LONG + local], axis=0, keepdims=True)
    block = local // 2

    def block_step(step, carry):
        start = step * block
        own = pl.ds(pl.multiple_of(start, 16), block)
        out = jnp.zeros((block, channels), f32)
        for row in range(3):
            offset = pl.multiple_of(LONG + start + (row - 1) * width, 16)
            for col in range(3):
                tap = 8 - (3 * row + col)
                out = out + lax.dot_general(
                    stack_ref[pl.ds(offset, block), col * channels : (col + 1) * channels],
                    w_ref[tap * channels : (tap + 1) * channels, :],
                    (((1,), (1,)), ((), ())),
                    preferred_element_type=f32,
                )
        kept = meta_ref[0, pl.ds(pl.multiple_of(LONG + start, 16), block), :]
        kept = jnp.concatenate([kept] * (channels // TILE), axis=1)
        xhat = (x_ref[own, :].astype(f32) - rows_ref[5:6]) * rows_ref[6:7]
        pre = kept * xhat * rows_ref[7:8]
        gate = 1.0 / (1.0 + jnp.exp(-pre))
        act_ref[own, :] = (pre * gate).astype(bf16)
        grad = out * (gate * (1.0 + pre * (1.0 - gate)))
        pre_ref[own, :] = grad
        grad = grad * kept
        sum_ref[0:1] += jnp.sum(grad, axis=0, keepdims=True)
        sum_ref[1:2] += jnp.sum(grad * xhat, axis=0, keepdims=True)
        return carry

    lax.fori_loop(0, 2, block_step, 0)
    act_t = jnp.transpose(act_ref[...], (1, 0))
    groups = pack_ref.shape[2] // TILE
    tiles = channels // TILE
    for row in range(3):
        offset = pl.multiple_of(LONG + (row - 1) * width, 16)
        for col in range(3):
            tap = 8 - (3 * row + col)
            grad = jnp.dot(
                act_t,
                stack_ref[pl.ds(offset, local), col * channels : (col + 1) * channels],
                preferred_element_type=f32,
            )
            grad = jnp.transpose(grad.astype(bf16), (1, 0))
            for tile in range(tiles):
                spot = tap * tiles + tile
                lane = (spot % groups) * TILE
                pack_ref[spot // groups, :, lane : lane + TILE] = grad[:, tile * TILE : (tile + 1) * TILE]
    for spot in range(9 * tiles, pack_ref.shape[0] * groups):
        lane = (spot % groups) * TILE
        pack_ref[spot // groups, :, lane : lane + TILE] = jnp.zeros((channels, TILE), bf16)


def conv_back(width, grad, grad_halo, field, field_halo, skip, skip_halo, source, meta, rows, weight):
    local, channels = grad.shape
    count = lax.axis_size("narrow")
    vmem = pl.BlockSpec(memory_space=pltpu.VMEM)
    padded = weight.shape[0] + (-weight.shape[0] % (count * TILE))
    operands = [grad, grad_halo[0], grad_halo[1], field, field_halo[0], field_halo[1]]
    if skip is not None:
        operands += [skip, skip_halo[0], skip_halo[1]]
    operands += [source, meta, rows, weight]
    return pl.pallas_call(
        functools.partial(conv_back_kernel, skip is not None),
        in_specs=[pl.BlockSpec(memory_space=pltpu.SMEM)] + [vmem] * len(operands),
        out_specs=(vmem,) * 4,
        out_shape=(
            jax.ShapeDtypeStruct((local, channels), f32),
            jax.ShapeDtypeStruct((local, channels), f32),
            jax.ShapeDtypeStruct((count, channels, padded // count), bf16),
            jax.ShapeDtypeStruct((8, channels), f32),
        ),
        scratch_shapes=[
            pltpu.VMEM((local + 2 * LONG, 3 * channels), bf16),
            pltpu.VMEM((local, channels), bf16),
        ],
        compiler_params=pltpu.CompilerParams(vmem_limit_bytes=CONV_LIMIT),
        cost_estimate=pl.CostEstimate(
            flops=4 * local * weight.size,
            bytes_accessed=6 * weight.size,
            transcendentals=local * channels,
        ),
        name="conv_back",
    )(width, *operands)


def edge_rows(field):
    count = lax.axis_size("narrow")
    forward = [(i, i + 1) for i in range(count - 1)]
    backward = [(i + 1, i) for i in range(count - 1)]
    return (
        lax.ppermute(field[-LONG:], "narrow", forward),
        lax.ppermute(field[:LONG], "narrow", backward),
    )


def pixel_meta(keep_image, row_start, local, row_width):
    rim = jnp.pad(keep_image, (LONG, LONG))
    keep = lax.dynamic_slice_in_dim(rim, row_start, local + 2 * LONG, 0)
    spot = jnp.arange(local + 2 * LONG, dtype=jnp.int32)
    column = (spot + 2 * LONG * SHORT - LONG) % row_width
    rows = jnp.stack([keep, (column > 0).astype(f32), (column < row_width - 1).astype(f32)])
    return jnp.broadcast_to(rows[:, :, None], rows.shape + (TILE,))


def row_table(*rows):
    table = jnp.stack([jnp.broadcast_to(row.reshape(-1), rows[0].reshape(-1).shape) for row in rows])
    return jnp.pad(table, ((0, 8 - len(rows)), (0, 0)))


def per_device(
    latents,
    cotangent,
    bucket,
    pixel_mask,
    labels,
    timesteps,
    gain_first,
    conv_first,
    time_proj,
    gain_second,
    conv_second,
    gain_spatial,
    proj_in,
    gain_attn,
    attn_qkv,
    attn_out,
    class_table,
    cross_value,
    cross_out,
    gain_ff,
    geglu_in,
    geglu_out,
    proj_out,
):
    images, local_pix, channels = latents.shape
    row_start = lax.axis_index("narrow") * local_pix
    keep_all = pixel_mask.astype(jnp.float32)
    pixel_keep = lax.dynamic_slice_in_dim(keep_all, row_start, local_pix, 1)[0, :, None]
    counts = jnp.sum(keep_all, axis=1) * (channels // GROUPS)
    row_width = jnp.where(bucket[0] == 0, LONG, SHORT).astype(jnp.int32)
    width = row_width[None]
    meta = pixel_meta(keep_all[0], row_start, local_pix, row_width)
    pixels = latents[0]
    pixel_halo = edge_rows(pixels)
    skip = cotangent[0]
    skip_halo = edge_rows(skip)
    half_dim = time_proj.shape[0] // 2
    frequency = jnp.exp(-math.log(10000.0) * jnp.arange(half_dim, dtype=jnp.float32) / half_dim)
    angles = timesteps.astype(jnp.float32)[:, None] * frequency[None, :]
    time_act = jax.nn.silu(jnp.concatenate([jnp.cos(angles), jnp.sin(angles)], axis=1))
    time_term = jnp.dot(time_act, time_proj.astype(jnp.float32), precision=HIGH)
    label_hot = (
        labels[:, None] == jnp.arange(class_table.shape[0], dtype=jnp.int32)[None, :]
    ).astype(jnp.float32)
    context = jnp.dot(label_hot, class_table.astype(jnp.float32), precision=HIGH)
    value_weight = cross_value.astype(jnp.float32)
    cross_weight = cross_out.astype(jnp.float32)
    value_term = jnp.dot(context, value_weight, precision=HIGH)
    cross_term = jnp.dot(value_term, cross_weight, precision=HIGH)
    gain_one = gain_first.astype(jnp.float32)
    gain_two = gain_second.astype(jnp.float32)
    gain_three = gain_spatial.astype(jnp.float32)
    image_in = pixels.astype(jnp.float32)
    kept = image_in * pixel_keep
    sums_one = jnp.stack([jnp.sum(kept, axis=0), jnp.sum(kept * image_in, axis=0)])
    center_one, scale_one = group_moments(sums_one, counts)
    hidden, sums_two = conv_forward(
        width,
        pixels,
        pixel_halo,
        meta,
        row_table(center_one, scale_one, gain_one),
        conv_first,
        row_table(time_term[0]),
    )
    hidden_halo = edge_rows(hidden)
    center_two, scale_two = group_moments(sums_two[:2], counts)
    residual, sums_three = conv_forward(
        width,
        hidden,
        hidden_halo,
        meta,
        row_table(center_two, scale_two, gain_two),
        conv_second,
        pixels,
    )
    residual_halo = edge_rows(residual)
    center_three, scale_three = group_moments(sums_three[:2], counts)
    residual_hat = (residual - center_three) * scale_three
    spatial = (pixel_keep * residual_hat * gain_three).astype(jnp.bfloat16)[None]
    stream = jnp.einsum("npc,cd->npd", spatial, proj_in, preferred_element_type=jnp.float32)
    normed_attn, attn_pull = jax.vjp(layer_norm, stream, gain_attn.astype(jnp.float32))
    normed_attn = normed_attn.astype(jnp.bfloat16)
    packed_f = jnp.einsum("npc,cd->npd", normed_attn, attn_qkv, preferred_element_type=jnp.float32)
    query_pix = (packed_f[0, :, :channels] * (1.0 / (math.sqrt(HEAD_DIM) * LN2))).astype(bf16)
    pad_pix = -local_pix % QB
    query_pix = jnp.pad(query_pix, ((0, pad_pix), (0, 0)))
    query_t = query_pix.T
    key_value = packed_f[0, :, channels:].astype(bf16)
    count = lax.axis_size("narrow")
    position = lax.axis_index("narrow")
    chunks = [key_value] + [None] * (count - 1)
    for bit in axis_bits("narrow"):
        chunks[bit] = swap(key_value, bit)
    keep_chunk = lambda index: lax.dynamic_slice_in_dim(
        keep_all[0], (position ^ index) * local_pix, local_pix, 0
    )
    keeps = [keep_chunk(index) for index in range(count)]
    aug_of = lambda indices: key_aug(jnp.concatenate([keeps[index] for index in indices]))
    state = attend_some(True, count == 2, query_t, chunks[:2], aug_of([0, 1]), ())
    for index in range(2, count):
        bit = low_bit(index)
        if index != bit:
            chunks[index] = swap(chunks[index ^ bit], bit)
        elif index < count - 1:
            chunks[index], state = lax.optimization_barrier((chunks[index], state))
    for index in range(2, count):
        state = attend_some(
            False, index == count - 1, query_t, [chunks[index]], aug_of([index]), state
        )
    heads_t, log_rows = state
    heads_rows = heads_t.T[None, :local_pix].astype(bf16)
    stream_mid = (
        stream
        + jnp.einsum("npc,cd->npd", heads_rows, attn_out, preferred_element_type=jnp.float32)
        + cross_term[:, None, :]
    )
    normed_ff, ff_pull = jax.vjp(layer_norm, stream_mid, gain_ff.astype(jnp.float32))
    normed_ff = normed_ff.astype(jnp.bfloat16)
    gates = jnp.einsum("npc,cf->npf", normed_ff, geglu_in, preferred_element_type=jnp.float32)
    mixed, gate_pull = jax.vjp(geglu_mix, gates)
    mixed = mixed.astype(jnp.bfloat16)
    stream_end = stream_mid + jnp.einsum(
        "npf,fc->npc", mixed, geglu_out, preferred_element_type=jnp.float32
    )
    top_in = stream_end.astype(jnp.bfloat16)
    output = (
        residual[None]
        + jnp.einsum("npc,cd->npd", top_in, proj_out, preferred_element_type=jnp.float32)
    ).astype(jnp.bfloat16)
    grad_proj_out = jnp.einsum("npc,npd->dc", top_in, cotangent, preferred_element_type=jnp.float32)
    grad_end = jnp.einsum("npd,cd->npc", cotangent, proj_out, preferred_element_type=jnp.float32)
    grad_ffo = grad_end.astype(jnp.bfloat16)
    grad_geglu_out = jnp.einsum("npf,npc->cf", mixed, grad_ffo, preferred_element_type=jnp.float32)
    grad_mixed = jnp.einsum("npc,fc->npf", grad_ffo, geglu_out, preferred_element_type=jnp.float32)
    grad_gates = gate_pull(grad_mixed)[0].astype(jnp.bfloat16)
    grad_geglu_in = jnp.einsum(
        "npc,npf->fc", normed_ff, grad_gates, preferred_element_type=jnp.float32
    )
    grad_normed = jnp.einsum(
        "npf,cf->npc", grad_gates, geglu_in, preferred_element_type=jnp.float32
    )
    grad_from_ff, grad_gain_ff = ff_pull(grad_normed)
    grad_mid = grad_end + grad_from_ff
    grad_cross = jnp.sum(grad_mid, axis=1)
    grad_attn_in = grad_mid.astype(jnp.bfloat16)
    grad_attn_out = jnp.einsum(
        "npc,npd->dc", heads_rows, grad_attn_in, preferred_element_type=jnp.float32
    )
    grad_heads_rows = jnp.einsum(
        "npd,cd->npc", grad_attn_in, attn_out, preferred_element_type=jnp.float32
    ).astype(jnp.bfloat16)
    owned = channels // lax.axis_size("wide")
    top_parts = jnp.concatenate(
        [
            grad_proj_out,
            grad_attn_out,
            grad_geglu_out,
            by_owner(grad_geglu_in, owned),
        ],
        axis=1,
    )
    top_parts, grad_heads_rows = lax.optimization_barrier((top_parts, grad_heads_rows))
    top_share = wide_scatter(top_parts)
    grad_rows = jnp.pad(grad_heads_rows[0], ((0, pad_pix), (0, 0)))
    grad_t = grad_rows.T
    grad_query_t = None
    totals = [None] * count
    arrived = [None] * count
    calls = [[count - 1]] + [[last - 1, last] for last in range(count - 2, 0, -2)] + [[0]]
    for call in calls:
        grad_query_t, *parts = attend_back_some(
            call[0] == count - 1,
            [bf16 if index % 2 else f32 for index in call],
            query_t,
            query_pix,
            grad_t,
            grad_rows,
            log_rows,
            heads_t,
            [chunks[index] for index in call],
            aug_of(call),
            grad_query_t,
        )
        for index, total in zip(call, parts):
            for source in range(index + 1, count):
                if source ^ low_bit(source) == index:
                    total = total + arrived[source].astype(f32)
            if index:
                arrived[index] = swap(total.astype(bf16), low_bit(index))
            totals[index] = total
    total = totals[0]
    grad_packed = jnp.concatenate(
        [
            grad_query_t.T[:local_pix].astype(bf16),
            total[0].astype(bf16),
            total[1].astype(bf16),
        ],
        axis=1,
    )[None]
    top_share, grad_packed = lax.optimization_barrier((top_share, grad_packed))
    grad_attn_whole = jnp.einsum(
        "npc,npd->dc", normed_attn, grad_packed, preferred_element_type=jnp.float32
    )
    grad_normed_attn = jnp.einsum(
        "npd,cd->npc", grad_packed, attn_qkv, preferred_element_type=jnp.float32
    )
    grad_from_attn, grad_gain_attn = attn_pull(grad_normed_attn)
    grad_stream = (grad_mid + grad_from_attn).astype(jnp.bfloat16)
    grad_proj_in = jnp.einsum(
        "npc,npd->dc", spatial, grad_stream, preferred_element_type=jnp.float32
    )
    grad_spatial = jnp.einsum(
        "npd,cd->npc", grad_stream, proj_in, preferred_element_type=jnp.float32
    )
    grad_spatial = grad_spatial[0]
    query_key = by_owner(grad_attn_whole[: 2 * channels], owned)
    low_parts = jnp.stack(
        [
            grad_proj_in,
            query_key[:, :channels],
            query_key[:, channels:],
            grad_attn_whole[2 * channels :],
        ]
    ).astype(bf16)
    grad_halo = edge_rows(grad_spatial)
    kept = grad_spatial * pixel_keep
    sums = jnp.stack([jnp.sum(kept, axis=0), jnp.sum(kept * residual_hat, axis=0)])
    means, early_rows = group_means(
        sums, gain_three, counts, [grad_cross[0], grad_gain_ff, grad_gain_attn]
    )
    grad_res, grad_pre, pack_second, sums = conv_back(
        width,
        grad_spatial,
        grad_halo,
        residual,
        residual_halo,
        skip,
        skip_halo,
        hidden,
        meta,
        row_table(
            center_three,
            scale_three,
            gain_three,
            means[0],
            means[1],
            center_two,
            scale_two,
            gain_two,
        ),
        conv_second,
    )
    grad_halo = edge_rows(grad_pre)
    means, middle_rows = group_means(sums[:2], gain_two, counts)
    held = jnp.concatenate([pack_second, low_parts], axis=2)
    bits = axis_bits("narrow")
    for bit in bits[:-1]:
        held = halve_step(held, bit, "narrow")
    held, grad_pre = lax.optimization_barrier((held, grad_pre))
    held = halve_step(held, bits[-1], "narrow")
    grad_hidden, grad_pre, pack_first, sums = conv_back(
        width,
        grad_pre,
        grad_halo,
        hidden,
        hidden_halo,
        None,
        None,
        pixels,
        meta,
        row_table(
            center_two,
            scale_two,
            gain_two,
            means[0],
            means[1],
            center_one,
            scale_one,
            gain_one,
        ),
        conv_first,
    )
    held, sums = lax.optimization_barrier((held, sums))
    means, late_rows = group_means(sums[:3], gain_one, counts)
    share_first = halve(pack_first, "narrow")
    image_hat = (image_in - center_one) * scale_one
    grad_image = grad_pre * pixel_keep * gain_one - means[0] - image_hat * means[1]
    grad_latents = (grad_res + pixel_keep * scale_one * grad_image).astype(jnp.bfloat16)[None]
    conv_rows = conv_first.shape[0]
    whole_second = wide_finish(held[0])
    lanes = pack_second.shape[2]
    sum_conv_second = conv_finish(whole_second[:, :, :lanes], conv_rows)
    low_whole = jnp.transpose(whole_second[:, :, lanes:], (0, 2, 1)).astype(f32)
    top = narrow_finish(top_share)
    sum_conv_first = conv_finish(wide_finish(share_first), conv_rows)
    stamp_row = jnp.pad(
        jnp.concatenate([labels, timesteps]).astype(f32), (0, channels - 2 * images)
    )
    spread = double(
        jnp.stack(
            [
                early_rows[2],
                late_rows[2],
                early_rows[3],
                early_rows[4],
                early_rows[1],
                middle_rows[1],
                late_rows[1],
                stamp_row,
            ]
        ),
        "wide",
    )
    labels_all = spread[:, 7, 0].astype(jnp.int32)
    steps_all = spread[:, 7, 1].astype(jnp.int32)
    angles_all = steps_all.astype(jnp.float32)[:, None] * frequency[None, :]
    time_all = jax.nn.silu(jnp.concatenate([jnp.cos(angles_all), jnp.sin(angles_all)], axis=1))
    hot_all = (
        labels_all[:, None] == jnp.arange(class_table.shape[0], dtype=jnp.int32)[None, :]
    ).astype(jnp.float32)
    context_all = jnp.dot(hot_all, class_table.astype(jnp.float32), precision=HIGH)
    value_all = jnp.dot(context_all, value_weight, precision=HIGH)
    cross_all = spread[:, 0]
    grad_value_all = jnp.dot(cross_all, cross_weight.T, precision=HIGH)
    grad_context_all = jnp.dot(grad_value_all, value_weight.T, precision=HIGH)
    sum_cross_out = jnp.dot(value_all.T, own_columns(cross_all), precision=HIGH)
    sum_cross_value = jnp.dot(context_all.T, own_columns(grad_value_all), precision=HIGH)
    sum_class_table = jnp.dot(hot_all.T, own_columns(grad_context_all), precision=HIGH)
    sum_time_proj = jnp.dot(time_all.T, own_columns(spread[:, 1]), precision=HIGH)
    gain_sums = own_columns(jnp.sum(spread[:, 2:7], axis=0))
    return (
        output,
        grad_latents,
        gain_sums[4],
        sum_conv_first,
        sum_time_proj,
        gain_sums[3],
        sum_conv_second,
        gain_sums[2],
        low_whole[0],
        gain_sums[1],
        jnp.concatenate([low_whole[1], low_whole[2]], axis=1),
        low_whole[3],
        from_owner(top[:, channels : 2 * channels], channels),
        sum_class_table,
        sum_cross_value,
        sum_cross_out,
        gain_sums[0],
        from_owner(top[:, 2 * channels + geglu_out.shape[0] :], channels),
        from_owner(top[:, 2 * channels : 2 * channels + geglu_out.shape[0]], geglu_out.shape[0]),
        from_owner(top[:, :channels], channels),
    )


def solution(mesh):
    placed = (
        P("wide", "narrow", None),
        P("wide", "narrow", None),
        P("wide"),
        P("wide", None),
        P("wide"),
        P("wide"),
        P(),
        P(),
        P(),
        P(),
        P(),
        P(),
        P(),
        P(),
        P(),
        P(),
        P(),
        P(),
        P(),
        P(),
        P(),
        P(),
        P(),
    )
    return jax.shard_map(
        per_device,
        mesh=mesh,
        in_specs=placed,
        out_specs=(
            P("wide", "narrow", None),
            P("wide", "narrow", None),
            P("wide"),
            P(None, "wide"),
            P(None, "wide"),
            P("wide"),
            P(None, "wide"),
            P("wide"),
            P(None, "wide"),
            P("wide"),
            P(None, "wide"),
            P(None, "wide"),
            P(None, "wide"),
            P(None, "wide"),
            P(None, "wide"),
            P(None, "wide"),
            P("wide"),
            P(None, "wide"),
            P(None, "wide"),
            P(None, "wide"),
        ),
        check_vma=False,
    )
```

```python
import functools
import math

import jax
import jax.numpy as jnp
from jax import lax
from jax.experimental import pallas as pl
from jax.experimental.pallas import tpu as pltpu
from jax.sharding import PartitionSpec as P

HEAD_DIM = 32
GROUPS = 32
SHORT = 48
LONG = 80


HIGH = lax.Precision.HIGHEST
EPS_GROUP = 1e-06
EPS_LAYER = 1e-05
MASKED = -1e30


TILE = 128
PER_TILE = TILE // HEAD_DIM
QB = 256
ONES = 16
SAFE_REACH = 90.0
LN2 = math.log(2.0)
bf16 = jnp.bfloat16
f32 = jnp.float32


def group_sum(value):
    grouped = value.reshape(value.shape[0], GROUPS, -1)
    summed = jnp.sum(grouped, axis=2, keepdims=True)
    return jnp.broadcast_to(summed, grouped.shape).reshape(value.shape)


def group_moments(sums, counts):
    sums = group_sum(narrow_sum(sums)) / counts[0]
    center = sums[0]
    spread = sums[1] - center * center
    return center, lax.rsqrt(spread + EPS_GROUP)


def group_means(sums, gain, counts, extras=()):
    sums = narrow_sum(jnp.concatenate([sums] + [row[None] for row in extras], axis=0))
    means = group_sum(sums[:2] * gain) / counts[0]
    return means, sums


def layer_norm(field_in, gain):
    center = jnp.mean(field_in, axis=-1, keepdims=True)
    spread = jnp.mean(jnp.square(field_in - center), axis=-1, keepdims=True)
    return (field_in - center) * lax.rsqrt(spread + EPS_LAYER) * gain


def head_rows(block, head):
    row = lax.broadcasted_iota(jnp.int32, block.shape, 0)
    inside = (row >= head * HEAD_DIM) & (row < (head + 1) * HEAD_DIM)
    return jnp.where(inside, block, jnp.zeros_like(block))


def head_lanes(block, head):
    lane = lax.broadcasted_iota(jnp.int32, block.shape, 1)
    inside = (lane >= head * HEAD_DIM) & (lane < (head + 1) * HEAD_DIM)
    return jnp.where(inside, block, jnp.zeros_like(block))


def mask_rows():
    row = lax.broadcasted_iota(jnp.int32, (TILE, QB), 0)
    return jnp.where(row == 0, 1.0, 0.0).astype(bf16)


def attend_kernel(first, last, parts, *refs):
    qt_ref = refs[0]
    key_refs = refs[1 : 1 + parts]
    value_refs = refs[1 + parts : 1 + 2 * parts]
    aug_ref = refs[1 + 2 * parts]
    rest = refs[2 + 2 * parts :]
    if not first:
        peak_in, acc_in = rest[:2]
        rest = rest[2:]
    if last:
        heads_ref, log_ref = rest
    else:
        peak_ref, acc_ref = rest
    keys = jnp.concatenate([ref[...] for ref in key_refs], axis=0)
    keys = jnp.concatenate([keys, aug_ref[...]], axis=1)
    values = jnp.concatenate([ref[...] for ref in value_refs], axis=0)
    value_t = jnp.transpose(values, (1, 0))
    ones = jnp.ones((ONES, value_t.shape[1]), bf16)
    low_rows = mask_rows()

    head_of = lambda shape, axis: lax.broadcasted_iota(jnp.int32, shape, axis) // HEAD_DIM
    pick = jnp.where(head_of((TILE, TILE), 0) == head_of((TILE, TILE), 1), 1.0, 0.0).astype(bf16)
    all_keys = keys[:, :TILE]
    key_norms = jnp.dot(all_keys * all_keys, pick, preferred_element_type=f32)
    all_queries = qt_ref[...]
    query_norms = jnp.dot(pick, all_queries * all_queries, preferred_element_type=f32)
    reach = jnp.float32(0.0)
    for head in range(PER_TILE):
        rows = slice(head * HEAD_DIM, head * HEAD_DIM + 8)
        mine = head_of(key_norms.shape, 1) == head
        key_peak = jnp.max(jnp.where(mine, key_norms, 0.0))
        reach = jnp.maximum(reach, key_peak * jnp.max(query_norms[rows]))

    def make_step(shifted):
        def block_step(step, carry):
            cols = pl.ds(pl.multiple_of(step * QB, QB), QB)
            qt = qt_ref[:, cols]
            for head in range(PER_TILE):
                rows = slice(head * HEAD_DIM, (head + 1) * HEAD_DIM)
                query = jnp.concatenate([head_rows(qt, head), low_rows], axis=0)
                scores = jnp.dot(keys, query, preferred_element_type=f32)
                if shifted:
                    peak = jnp.max(scores, axis=0, keepdims=True)
                    probs = jnp.exp2(scores - peak).astype(bf16)
                else:
                    peak = jnp.zeros((1, QB), f32)
                    probs = jnp.exp2(scores).astype(bf16)
                value_h = jnp.concatenate([value_t[rows], ones], axis=0)
                acc = jnp.dot(value_h, probs, preferred_element_type=f32)
                if not first:
                    peak_old = peak_in[head, 0:1, cols]
                    peak_new = jnp.maximum(peak, peak_old)
                    acc = acc * jnp.exp2(peak - peak_new)
                    acc = acc + acc_in[head, :, cols] * jnp.exp2(peak_old - peak_new)
                    peak = peak_new
                if last:
                    total = acc[HEAD_DIM : HEAD_DIM + 1]
                    heads_ref[rows, cols] = acc[:HEAD_DIM] / total
                    log_ref[head, :, cols] = jnp.broadcast_to(peak + jnp.log2(total), (8, QB))
                else:
                    acc_ref[head, :, cols] = acc
                    peak_ref[head, :, cols] = jnp.broadcast_to(peak, (8, QB))
            return carry

        return block_step

    steps = qt_ref.shape[1] // QB

    @pl.when(reach < SAFE_REACH * SAFE_REACH)
    def _():
        lax.fori_loop(0, steps, make_step(False), 0)

    @pl.when(jnp.logical_not(reach < SAFE_REACH * SAFE_REACH))
    def _():
        lax.fori_loop(0, steps, make_step(True), 0)


def chunk_specs(count, tiles, parts):
    key_spec = pl.BlockSpec((count, TILE), lambda t: (0, t))
    value_spec = pl.BlockSpec((count, TILE), lambda t: (0, tiles + t))
    aug_spec = pl.BlockSpec((parts * count, TILE), lambda t: (0, 0))
    return [key_spec] * parts + [value_spec] * parts + [aug_spec]


def attend_some(first, last, query_t, chunks, aug, state):
    channels, queries = query_t.shape
    count = chunks[0].shape[0]
    heads = channels // HEAD_DIM
    tiles = channels // TILE
    t_spec = pl.BlockSpec((TILE, queries), lambda t: (t, 0))
    cube = lambda t: (t, 0, 0)
    row_spec = pl.BlockSpec((PER_TILE, 8, queries), cube)
    acc_spec = pl.BlockSpec((PER_TILE, HEAD_DIM + ONES, queries), cube)
    in_specs = [t_spec] + chunk_specs(count, tiles, len(chunks))
    if not first:
        in_specs += [row_spec, acc_spec]
    row_shape = jax.ShapeDtypeStruct((heads, 8, queries), f32)
    if last:
        out_shape = (jax.ShapeDtypeStruct((channels, queries), f32), row_shape)
        out_specs = (t_spec, row_spec)
    else:
        out_shape = (
            row_shape,
            jax.ShapeDtypeStruct((heads, HEAD_DIM + ONES, queries), f32),
        )
        out_specs = (row_spec, acc_spec)
    return pl.pallas_call(
        functools.partial(attend_kernel, first, last, len(chunks)),
        grid=(tiles,),
        in_specs=in_specs,
        out_specs=out_specs,
        out_shape=out_shape,
        compiler_params=pltpu.CompilerParams(vmem_limit_bytes=40 << 20),
        cost_estimate=pl.CostEstimate(
            flops=32 * len(chunks) * channels * queries * count,
            bytes_accessed=8 * channels * (queries + count),
            transcendentals=len(chunks) * heads * queries * count,
        ),
        name="attend",
    )(query_t, *chunks, *chunks, aug, *state)


def attend_back_kernel(first, parts, *refs):
    qt_ref, q_ref, dt_ref, d_ref, log_ref, heads_ref = refs[:6]
    key_refs = refs[6 : 6 + parts]
    value_refs = refs[6 + parts : 6 + 2 * parts]
    aug_ref = refs[6 + 2 * parts]
    refs = refs[7 + 2 * parts :]
    if not first:
        dq_in = refs[0]
        refs = refs[1:]
    dq_ref = refs[0]
    out_refs = refs[1 : 1 + parts]
    dk_acc, dv_acc = refs[1 + parts :]
    count = key_refs[0].shape[0]
    k_tile = jnp.concatenate([ref[...] for ref in key_refs], axis=0)
    keys = jnp.concatenate([k_tile, aug_ref[...]], axis=1)
    values = jnp.concatenate([ref[...] for ref in value_refs], axis=0)
    key_t = jnp.transpose(k_tile, (1, 0))
    low_rows = mask_rows()
    dk_acc[...] = jnp.zeros_like(dk_acc)
    dv_acc[...] = jnp.zeros_like(dv_acc)
    factor = 1.0 / math.sqrt(HEAD_DIM)

    def block_step(step, carry):
        cols = pl.ds(pl.multiple_of(step * QB, QB), QB)
        qt = qt_ref[:, cols]
        dt = dt_ref[:, cols]
        q_blk = q_ref[cols, :]
        d_blk = d_ref[cols, :]
        probs_all, grads_all, q_all, d_all = [], [], [], []
        for head in range(PER_TILE):
            rows = slice(head * HEAD_DIM, (head + 1) * HEAD_DIM)
            query = jnp.concatenate([head_rows(qt, head), low_rows], axis=0)
            scores = jnp.dot(keys, query, preferred_element_type=f32)
            probs = jnp.exp2(scores - log_ref[head, 0:1, cols])
            weighted = jnp.sum(
                heads_ref[rows, cols] * dt[rows].astype(f32), axis=0, keepdims=True
            )
            grad_p = jnp.dot(values, head_rows(dt, head), preferred_element_type=f32)
            grad_s = (probs * (grad_p - weighted)).astype(bf16)
            probs_all.append(probs.astype(bf16))
            grads_all.append(grad_s)
            q_all.append(head_lanes(q_blk, head))
            d_all.append(head_lanes(d_blk, head))
            dq = jnp.dot(key_t[rows], grad_s, preferred_element_type=f32) * factor
            if not first:
                dq = dq + dq_in[rows, cols]
            dq_ref[rows, cols] = dq
        dv_acc[...] += jnp.dot(
            jnp.concatenate(probs_all, axis=1),
            jnp.concatenate(d_all, axis=0),
            preferred_element_type=f32,
        )
        dk_acc[...] += jnp.dot(
            jnp.concatenate(grads_all, axis=1),
            jnp.concatenate(q_all, axis=0),
            preferred_element_type=f32,
        )
        return carry

    lax.fori_loop(0, qt_ref.shape[1] // QB, block_step, 0)
    for index, ref in enumerate(out_refs):
        rows = slice(index * count, (index + 1) * count)
        ref[0] = (dk_acc[rows] * LN2).astype(ref.dtype)
        ref[1] = dv_acc[rows].astype(ref.dtype)


def attend_back_some(
    first, out_types, query_t, query, grad_t, grad, logs, heads_t, chunks, aug, dq
):
    channels, queries = query_t.shape
    count = chunks[0].shape[0]
    parts = len(chunks)
    tiles = channels // TILE
    t_spec = pl.BlockSpec((TILE, queries), lambda t: (t, 0))
    n_spec = pl.BlockSpec((queries, TILE), lambda t: (0, t))
    row_spec = pl.BlockSpec((PER_TILE, 8, queries), lambda t: (t, 0, 0))
    out_spec = pl.BlockSpec((2, count, TILE), lambda t: (0, 0, t))
    in_specs = [t_spec, n_spec, t_spec, n_spec, row_spec, t_spec] + chunk_specs(count, tiles, parts)
    state = ()
    if not first:
        in_specs.append(t_spec)
        state = (dq,)
    return pl.pallas_call(
        functools.partial(attend_back_kernel, first, parts),
        grid=(tiles,),
        in_specs=in_specs,
        out_specs=(t_spec,) + (out_spec,) * parts,
        out_shape=(jax.ShapeDtypeStruct((channels, queries), f32),)
        + tuple(jax.ShapeDtypeStruct((2, count, channels), kind) for kind in out_types),
        scratch_shapes=[pltpu.VMEM((parts * count, TILE), f32)] * 2,
        compiler_params=pltpu.CompilerParams(vmem_limit_bytes=48 << 20),
        cost_estimate=pl.CostEstimate(
            flops=80 * parts * channels * queries * count,
            bytes_accessed=12 * channels * (queries + count),
            transcendentals=parts * channels // HEAD_DIM * queries * count,
        ),
        name="attend_back",
    )(query_t, query, grad_t, grad, logs, heads_t, *chunks, *chunks, aug, *state)


def swap(value, bit, axis="narrow"):
    count = lax.axis_size(axis)
    return lax.ppermute(value, axis, [(i, i ^ bit) for i in range(count)])


def low_bit(index):
    return index & -index


def axis_bits(axis):
    return [1 << level for level in range(lax.axis_size(axis).bit_length() - 1)]


def my_bit(bit, axis="narrow"):
    return (lax.axis_index(axis) // bit) % 2


def narrow_sum(value):
    for bit in axis_bits("narrow"):
        value = value + swap(value, bit)
    return value


def key_aug(keep_chunk):
    lane = lax.broadcasted_iota(jnp.int32, (keep_chunk.shape[0], TILE), 1)
    bias = jnp.where(keep_chunk[:, None] > 0, 0.0, MASKED)
    return jnp.where(lane == 0, bias, 0.0).astype(bf16)


def halve_step(held, bit, axis):
    halves = held.reshape((held.shape[0] // 2, 2) + held.shape[1:])
    mine = my_bit(bit, axis)
    kept = lax.dynamic_index_in_dim(halves, mine, 1, keepdims=False)
    sent = lax.dynamic_index_in_dim(halves, 1 - mine, 1, keepdims=False)
    return (kept.astype(f32) + swap(sent, bit, axis).astype(f32)).astype(bf16)


def halve(held, axis):
    for bit in axis_bits(axis):
        held = halve_step(held, bit, axis)
    return held[0]


def double(value, axis):
    whole = value[None]
    for bit in reversed(axis_bits(axis)):
        other = swap(whole, bit, axis)
        pair = jnp.where(
            my_bit(bit, axis) == 0,
            jnp.stack([whole, other], axis=1),
            jnp.stack([other, whole], axis=1),
        )
        whole = pair.reshape((-1,) + value.shape)
    return whole


def wide_finish(share):
    wide = lax.axis_size("wide")
    share = halve(share.reshape(wide, share.shape[0] // wide, share.shape[1]), "wide")
    return double(share, "narrow")


def conv_finish(whole, rows):
    return jnp.transpose(whole, (0, 2, 1)).reshape(-1, whole.shape[1])[:rows].astype(f32)


def by_owner(grad_t, width):
    wide = lax.axis_size("wide")
    groups = grad_t.shape[0] // wide // width
    split = grad_t.reshape(wide, groups, width, grad_t.shape[1])
    return jnp.transpose(split, (0, 2, 1, 3)).reshape(wide * width, -1)


def narrow_finish(share):
    share = share.astype(bf16)
    for bit in axis_bits("narrow"):
        share = (share.astype(f32) + swap(share, bit).astype(f32)).astype(bf16)
    return share.astype(f32)


def own_columns(value):
    width = value.shape[-1] // lax.axis_size("wide")
    start = lax.axis_index("wide") * width
    return lax.dynamic_slice_in_dim(value, start, width, value.ndim - 1)


CONV_LIMIT = 50 << 20


def lanes_of(meta_ref, index, start, count, channels):
    return jnp.concatenate([meta_ref[index, start : start + count]] * (channels // TILE), axis=1)


def store_shifts(field, meta_ref, stack_ref):
    total, channels = field.shape
    low = jnp.where(
        lanes_of(meta_ref, 1, 0, total, channels) > 0, pltpu.roll(field, 1, 0), 0.0
    )
    high = jnp.where(
        lanes_of(meta_ref, 2, 0, total, channels) > 0, pltpu.roll(field, total - 1, 0), 0.0
    )
    stack_ref[:, :channels] = low.astype(bf16)
    stack_ref[:, channels : 2 * channels] = field.astype(bf16)
    stack_ref[:, 2 * channels :] = high.astype(bf16)


def with_halo(low_ref, own_ref, high_ref):
    parts = [low_ref[...].astype(f32), own_ref[...].astype(f32), high_ref[...].astype(f32)]
    return jnp.concatenate(parts, axis=0)


def conv_kernel(width_ref, x_ref, low_ref, high_ref, meta_ref, rows_ref, w_ref, add_ref, y_ref, sum_ref, stack_ref):
    local, channels = x_ref.shape
    total = stack_ref.shape[0]
    width = width_ref[0]
    field = with_halo(low_ref, x_ref, high_ref)
    keep = lanes_of(meta_ref, 0, 0, total, channels)
    pre = keep * (field - rows_ref[0:1]) * (rows_ref[1:2] * rows_ref[2:3])
    store_shifts(pre / (1.0 + jnp.exp(-pre)), meta_ref, stack_ref)
    block = local // 2
    sum_ref[...] = jnp.zeros_like(sum_ref)

    def block_step(step, carry):
        start = step * block
        taps = []
        for shift in (-1, 0, 1):
            offset = pl.multiple_of(LONG + start + shift * width, 16)
            taps.append(stack_ref[pl.ds(offset, block), :])
        out = jnp.dot(jnp.concatenate(taps, axis=1), w_ref[...], preferred_element_type=f32)
        own = pl.ds(pl.multiple_of(start, 16), block)
        if add_ref.shape[0] == local:
            out = out + add_ref[own, :].astype(f32)
        else:
            out = out + add_ref[0:1]
        y_ref[own, :] = out
        kept = meta_ref[0, pl.ds(pl.multiple_of(LONG + start, 16), block), :]
        kept = out * jnp.concatenate([kept] * (channels // TILE), axis=1)
        sum_ref[0:1] += jnp.sum(kept, axis=0, keepdims=True)
        sum_ref[1:2] += jnp.sum(kept * out, axis=0, keepdims=True)
        return carry

    lax.fori_loop(0, 2, block_step, 0)


def conv_forward(width, field, halo, meta, rows, weight, add):
    local, channels = field.shape
    vmem = pl.BlockSpec(memory_space=pltpu.VMEM)
    return pl.pallas_call(
        conv_kernel,
        in_specs=[pl.BlockSpec(memory_space=pltpu.SMEM)] + [vmem] * 7,
        out_specs=(vmem, vmem),
        out_shape=(
            jax.ShapeDtypeStruct((local, channels), f32),
            jax.ShapeDtypeStruct((8, channels), f32),
        ),
        scratch_shapes=[pltpu.VMEM((local + 2 * LONG, 3 * channels), bf16)],
        compiler_params=pltpu.CompilerParams(vmem_limit_bytes=CONV_LIMIT),
        cost_estimate=pl.CostEstimate(
            flops=2 * local * weight.size,
            bytes_accessed=4 * weight.size,
            transcendentals=2 * local * channels,
        ),
        name="conv_forward",
    )(width, field, halo[0], halo[1], meta, rows, weight, add)


def conv_back_kernel(with_skip, *refs):
    width_ref, d_ref, d_low, d_high, v_ref, v_low, v_high = refs[:7]
    refs = refs[7:]
    if with_skip:
        c_ref, c_low, c_high = refs[:3]
        refs = refs[3:]
    x_ref, meta_ref, rows_ref, w_ref = refs[:4]
    e_ref, pre_ref, pack_ref, sum_ref, stack_ref, act_ref = refs[4:]
    local, channels = d_ref.shape
    total = stack_ref.shape[0]
    width = width_ref[0]
    keep = lanes_of(meta_ref, 0, 0, total, channels)
    normed = (with_halo(v_low, v_ref, v_high) - rows_ref[0:1]) * rows_ref[1:2]
    inner = with_halo(d_low, d_ref, d_high) * keep * rows_ref[2:3] - rows_ref[3:4]
    field = keep * rows_ref[1:2] * (inner - normed * rows_ref[4:5])
    if with_skip:
        field = field + with_halo(c_low, c_ref, c_high)
    e_ref[...] = field[LONG : LONG + local]
    store_shifts(field, meta_ref, stack_ref)
    sum_ref[...] = jnp.zeros_like(sum_ref)
    sum_ref[2:3] = jnp.sum(field[LONG : LONG + local], axis=0, keepdims=True)
    block = local // 2

    def block_step(step, carry):
        start = step * block
        own = pl.ds(pl.multiple_of(start, 16), block)
        out = jnp.zeros((block, channels), f32)
        for row in range(3):
            offset = pl.multiple_of(LONG + start + (row - 1) * width, 16)
            for col in range(3):
                tap = 8 - (3 * row + col)
                out = out + lax.dot_general(
                    stack_ref[pl.ds(offset, block), col * channels : (col + 1) * channels],
                    w_ref[tap * channels : (tap + 1) * channels, :],
                    (((1,), (1,)), ((), ())),
                    preferred_element_type=f32,
                )
        kept = meta_ref[0, pl.ds(pl.multiple_of(LONG + start, 16), block), :]
        kept = jnp.concatenate([kept] * (channels // TILE), axis=1)
        xhat = (x_ref[own, :].astype(f32) - rows_ref[5:6]) * rows_ref[6:7]
        pre = kept * xhat * rows_ref[7:8]
        gate = 1.0 / (1.0 + jnp.exp(-pre))
        act_ref[own, :] = (pre * gate).astype(bf16)
        grad = out * (gate * (1.0 + pre * (1.0 - gate)))
        pre_ref[own, :] = grad
        grad = grad * kept
        sum_ref[0:1] += jnp.sum(grad, axis=0, keepdims=True)
        sum_ref[1:2] += jnp.sum(grad * xhat, axis=0, keepdims=True)
        return carry

    lax.fori_loop(0, 2, block_step, 0)
    act_t = jnp.transpose(act_ref[...], (1, 0))
    groups = pack_ref.shape[2] // TILE
    tiles = channels // TILE
    for row in range(3):
        offset = pl.multiple_of(LONG + (row - 1) * width, 16)
        for col in range(3):
            tap = 8 - (3 * row + col)
            grad = jnp.dot(
                act_t,
                stack_ref[pl.ds(offset, local), col * channels : (col + 1) * channels],
                preferred_element_type=f32,
            )
            grad = jnp.transpose(grad.astype(bf16), (1, 0))
            for tile in range(tiles):
                spot = tap * tiles + tile
                lane = (spot % groups) * TILE
                pack_ref[spot // groups, :, lane : lane + TILE] = grad[:, tile * TILE : (tile + 1) * TILE]
    for spot in range(9 * tiles, pack_ref.shape[0] * groups):
        lane = (spot % groups) * TILE
        pack_ref[spot // groups, :, lane : lane + TILE] = jnp.zeros((channels, TILE), bf16)


def conv_back(width, grad, grad_halo, field, field_halo, skip, skip_halo, source, meta, rows, weight):
    local, channels = grad.shape
    count = lax.axis_size("narrow")
    vmem = pl.BlockSpec(memory_space=pltpu.VMEM)
    padded = weight.shape[0] + (-weight.shape[0] % (count * TILE))
    operands = [grad, grad_halo[0], grad_halo[1], field, field_halo[0], field_halo[1]]
    if skip is not None:
        operands += [skip, skip_halo[0], skip_halo[1]]
    operands += [source, meta, rows, weight]
    return pl.pallas_call(
        functools.partial(conv_back_kernel, skip is not None),
        in_specs=[pl.BlockSpec(memory_space=pltpu.SMEM)] + [vmem] * len(operands),
        out_specs=(vmem,) * 4,
        out_shape=(
            jax.ShapeDtypeStruct((local, channels), f32),
            jax.ShapeDtypeStruct((local, channels), f32),
            jax.ShapeDtypeStruct((count, channels, padded // count), bf16),
            jax.ShapeDtypeStruct((8, channels), f32),
        ),
        scratch_shapes=[
            pltpu.VMEM((local + 2 * LONG, 3 * channels), bf16),
            pltpu.VMEM((local, channels), bf16),
        ],
        compiler_params=pltpu.CompilerParams(vmem_limit_bytes=CONV_LIMIT),
        cost_estimate=pl.CostEstimate(
            flops=4 * local * weight.size,
            bytes_accessed=6 * weight.size,
            transcendentals=local * channels,
        ),
        name="conv_back",
    )(width, *operands)


def edge_rows(field):
    count = lax.axis_size("narrow")
    forward = [(i, i + 1) for i in range(count - 1)]
    backward = [(i + 1, i) for i in range(count - 1)]
    return (
        lax.ppermute(field[-LONG:], "narrow", forward),
        lax.ppermute(field[:LONG], "narrow", backward),
    )


def pixel_meta(keep_image, row_start, local, row_width):
    rim = jnp.pad(keep_image, (LONG, LONG))
    keep = lax.dynamic_slice_in_dim(rim, row_start, local + 2 * LONG, 0)
    spot = jnp.arange(local + 2 * LONG, dtype=jnp.int32)
    column = (spot + 2 * LONG * SHORT - LONG) % row_width
    rows = jnp.stack([keep, (column > 0).astype(f32), (column < row_width - 1).astype(f32)])
    return jnp.broadcast_to(rows[:, :, None], rows.shape + (TILE,))


def row_table(*rows):
    table = jnp.stack([jnp.broadcast_to(row.reshape(-1), rows[0].reshape(-1).shape) for row in rows])
    return jnp.pad(table, ((0, 8 - len(rows)), (0, 0)))


NT = (((1,), (1,)), ((), ()))
MID_BLOCKS = 4


def dot_nt(left, right):
    return lax.dot_general(left, right, NT, preferred_element_type=f32)


def mid_kernel(
    owned,
    heads_ref,
    stream_ref,
    residual_ref,
    cot_ref,
    row_ref,
    attn_out_ref,
    geglu_in_ref,
    geglu_out_ref,
    proj_out_ref,
    out_ref,
    grad_mid_ref,
    grad_ref,
    grad_t_ref,
    top_ref,
    gate_ref,
    sum_ref,
    heads_low,
    normed_low,
    mixed_low,
    end_low,
    ffo_low,
    gates_low,
    mid_low,
):
    local, channels = stream_ref.shape
    hidden = geglu_out_ref.shape[0]
    block = local // MID_BLOCKS
    heads_low[...] = jnp.transpose(heads_ref[...].astype(bf16), (1, 0))[:local]
    sum_ref[...] = jnp.zeros_like(sum_ref)

    def block_step(step, carry):
        own = pl.ds(pl.multiple_of(step * block, 16), block)
        mid = stream_ref[own, :] + row_ref[0:1]
        mid = mid + jnp.dot(heads_low[own, :], attn_out_ref[...], preferred_element_type=f32)
        center = jnp.mean(mid, axis=1, keepdims=True)
        inv_std = lax.rsqrt(jnp.mean(jnp.square(mid - center), axis=1, keepdims=True) + EPS_LAYER)
        xhat = (mid - center) * inv_std
        normed = (xhat * row_ref[1:2]).astype(bf16)
        normed_low[own, :] = normed
        gates = jnp.dot(normed, geglu_in_ref[...], preferred_element_type=f32)
        value, gate = gates[:, :hidden], gates[:, hidden:]
        half = 0.5 * (1.0 + lax.erf(gate * math.sqrt(0.5)))
        gelu = gate * half
        slope = half + gate * jnp.exp(-0.5 * gate * gate) * (1.0 / math.sqrt(2.0 * math.pi))
        mixed = (value * gelu).astype(bf16)
        mixed_low[own, :] = mixed
        end = mid + jnp.dot(mixed, geglu_out_ref[...], preferred_element_type=f32)
        end = end.astype(bf16)
        end_low[own, :] = end
        out = residual_ref[own, :] + jnp.dot(end, proj_out_ref[...], preferred_element_type=f32)
        out_ref[own, :] = out.astype(bf16)
        grad_end = dot_nt(cot_ref[own, :], proj_out_ref[...])
        grad_ffo = grad_end.astype(bf16)
        ffo_low[own, :] = grad_ffo
        grad_mixed = dot_nt(grad_ffo, geglu_out_ref[...])
        grad_gates = jnp.concatenate(
            [(grad_mixed * gelu).astype(bf16), (grad_mixed * value * slope).astype(bf16)], axis=1
        )
        gates_low[own, :] = grad_gates
        grad_normed = dot_nt(grad_gates, geglu_in_ref[...])
        grad_hat = grad_normed * row_ref[1:2]
        mean_one = jnp.mean(grad_hat, axis=1, keepdims=True)
        mean_two = jnp.mean(grad_hat * xhat, axis=1, keepdims=True)
        grad_mid = grad_end + inv_std * (grad_hat - mean_one - xhat * mean_two)
        grad_mid_ref[own, :] = grad_mid
        sum_ref[0:1] += jnp.sum(grad_mid, axis=0, keepdims=True)
        sum_ref[1:2] += jnp.sum(grad_normed * xhat, axis=0, keepdims=True)
        grad_mid = grad_mid.astype(bf16)
        mid_low[own, :] = grad_mid
        grad_ref[own, :] = dot_nt(grad_mid, attn_out_ref[...]).astype(bf16)
        return carry

    lax.fori_loop(0, MID_BLOCKS, block_step, 0)
    pad = grad_ref.shape[0] - local
    if pad:
        grad_ref[local:, :] = jnp.zeros((pad, channels), bf16)
    grad_t_ref[...] = jnp.transpose(grad_ref[...], (1, 0))

    def put(index, grad):
        if owned:
            for owner in range(channels // owned):
                rows = grad[owner * owned : (owner + 1) * owned]
                top_ref[owner, index * owned : (index + 1) * owned, :] = rows
        else:
            top_ref[:, index * channels : (index + 1) * channels] = grad

    put(
        0,
        jnp.dot(
            jnp.transpose(cot_ref[...], (1, 0)), end_low[...], preferred_element_type=f32
        ),
    )
    put(
        1,
        jnp.dot(
            jnp.transpose(mid_low[...], (1, 0)), heads_low[...], preferred_element_type=f32
        ),
    )
    ffo_t = jnp.transpose(ffo_low[...], (1, 0))
    pieces = hidden // channels
    for piece in range(pieces):
        mixed = mixed_low[:, piece * channels : (piece + 1) * channels]
        put(2 + piece, jnp.dot(ffo_t, mixed, preferred_element_type=f32))
    normed_t = jnp.transpose(normed_low[...], (1, 0))
    for piece in range(2 * pieces):
        grads = gates_low[:, piece * channels : (piece + 1) * channels]
        grad = jnp.dot(normed_t, grads, preferred_element_type=f32)
        if owned:
            top_ref[piece, (2 + pieces) * owned :, :] = grad
        else:
            gate_ref[:, piece * channels : (piece + 1) * channels] = grad


def mid_layer(heads_t, stream, residual, cotangent, rows, attn_out, geglu_in, geglu_out, proj_out):
    local, channels = stream.shape
    queries = heads_t.shape[1]
    hidden = geglu_out.shape[0]
    wide = lax.axis_size("wide")
    pieces = 2 + hidden // channels
    aligned = 2 * hidden == wide * channels
    owned = channels // wide if aligned else 0
    if aligned:
        top_shape = jax.ShapeDtypeStruct((wide, pieces * owned + channels, channels), f32)
        gate_shape = jax.ShapeDtypeStruct((8, channels), f32)
    else:
        top_shape = jax.ShapeDtypeStruct((channels, pieces * channels), f32)
        gate_shape = jax.ShapeDtypeStruct((channels, 2 * hidden), f32)
    vmem = pl.BlockSpec(memory_space=pltpu.VMEM)
    low = lambda width: pltpu.VMEM((local, width), bf16)
    return pl.pallas_call(
        functools.partial(mid_kernel, owned),
        in_specs=[vmem] * 9,
        out_specs=(vmem,) * 7,
        out_shape=(
            jax.ShapeDtypeStruct((local, channels), bf16),
            jax.ShapeDtypeStruct((local, channels), f32),
            jax.ShapeDtypeStruct((queries, channels), bf16),
            jax.ShapeDtypeStruct((channels, queries), bf16),
            top_shape,
            gate_shape,
            jax.ShapeDtypeStruct((8, channels), f32),
        ),
        scratch_shapes=[
            low(channels),
            low(channels),
            low(hidden),
            low(channels),
            low(channels),
            low(2 * hidden),
            low(channels),
        ],
        compiler_params=pltpu.CompilerParams(vmem_limit_bytes=57 << 20),
        cost_estimate=pl.CostEstimate(
            flops=6 * local * channels * (3 * hidden + 2 * channels),
            bytes_accessed=24 * channels * hidden,
            transcendentals=2 * local * hidden,
        ),
        name="mid_layer",
    )(heads_t, stream, residual, cotangent, rows, attn_out, geglu_in, geglu_out, proj_out)


def top_shares(top, gates):
    wide = lax.axis_size("wide")
    if top.ndim == 3:
        share = lax.psum_scatter(top, "wide", scatter_dimension=0, tiled=True)[0]
        return (share,)
    channels = top.shape[0]
    split = top.reshape(wide, channels // wide, -1, channels)
    split = jnp.transpose(split, (0, 2, 1, 3)).reshape(wide, -1, channels)
    share = lax.psum_scatter(split, "wide", scatter_dimension=0, tiled=True)[0]
    gates = jnp.transpose(gates.reshape(channels, wide, -1), (1, 0, 2))
    return share, lax.psum_scatter(gates, "wide", scatter_dimension=0, tiled=True)[0]


def split_top(shares, owned, channels):
    if len(shares) == 1:
        count = shares[0].shape[0] - channels
        gates = shares[0][count:]
    else:
        count = shares[0].shape[0]
        gates = shares[1]
    pieces = shares[0][:count].reshape(-1, owned, channels)
    pieces = jnp.transpose(pieces, (0, 2, 1))
    return pieces[0], pieces[1], pieces[2:].reshape(-1, owned), gates


def per_device(
    latents,
    cotangent,
    bucket,
    pixel_mask,
    labels,
    timesteps,
    gain_first,
    conv_first,
    time_proj,
    gain_second,
    conv_second,
    gain_spatial,
    proj_in,
    gain_attn,
    attn_qkv,
    attn_out,
    class_table,
    cross_value,
    cross_out,
    gain_ff,
    geglu_in,
    geglu_out,
    proj_out,
):
    images, local_pix, channels = latents.shape
    row_start = lax.axis_index("narrow") * local_pix
    keep_all = pixel_mask.astype(jnp.float32)
    pixel_keep = lax.dynamic_slice_in_dim(keep_all, row_start, local_pix, 1)[0, :, None]
    counts = jnp.sum(keep_all, axis=1) * (channels // GROUPS)
    row_width = jnp.where(bucket[0] == 0, LONG, SHORT).astype(jnp.int32)
    width = row_width[None]
    meta = pixel_meta(keep_all[0], row_start, local_pix, row_width)
    pixels = latents[0]
    pixel_halo = edge_rows(pixels)
    skip = cotangent[0]
    skip_halo = edge_rows(skip)
    half_dim = time_proj.shape[0] // 2
    frequency = jnp.exp(-math.log(10000.0) * jnp.arange(half_dim, dtype=jnp.float32) / half_dim)
    angles = timesteps.astype(jnp.float32)[:, None] * frequency[None, :]
    time_act = jax.nn.silu(jnp.concatenate([jnp.cos(angles), jnp.sin(angles)], axis=1))
    time_term = jnp.dot(time_act, time_proj.astype(jnp.float32), precision=HIGH)
    label_hot = (
        labels[:, None] == jnp.arange(class_table.shape[0], dtype=jnp.int32)[None, :]
    ).astype(jnp.float32)
    context = jnp.dot(label_hot, class_table.astype(jnp.float32), precision=HIGH)
    value_weight = cross_value.astype(jnp.float32)
    cross_weight = cross_out.astype(jnp.float32)
    value_term = jnp.dot(context, value_weight, precision=HIGH)
    cross_term = jnp.dot(value_term, cross_weight, precision=HIGH)
    gain_one = gain_first.astype(jnp.float32)
    gain_two = gain_second.astype(jnp.float32)
    gain_three = gain_spatial.astype(jnp.float32)
    image_in = pixels.astype(jnp.float32)
    kept = image_in * pixel_keep
    sums_one = jnp.stack([jnp.sum(kept, axis=0), jnp.sum(kept * image_in, axis=0)])
    center_one, scale_one = group_moments(sums_one, counts)
    hidden, sums_two = conv_forward(
        width,
        pixels,
        pixel_halo,
        meta,
        row_table(center_one, scale_one, gain_one),
        conv_first,
        row_table(time_term[0]),
    )
    hidden_halo = edge_rows(hidden)
    center_two, scale_two = group_moments(sums_two[:2], counts)
    residual, sums_three = conv_forward(
        width,
        hidden,
        hidden_halo,
        meta,
        row_table(center_two, scale_two, gain_two),
        conv_second,
        pixels,
    )
    residual_halo = edge_rows(residual)
    center_three, scale_three = group_moments(sums_three[:2], counts)
    residual_hat = (residual - center_three) * scale_three
    spatial = (pixel_keep * residual_hat * gain_three).astype(jnp.bfloat16)[None]
    stream = jnp.einsum("npc,cd->npd", spatial, proj_in, preferred_element_type=jnp.float32)
    normed_attn, attn_pull = jax.vjp(layer_norm, stream, gain_attn.astype(jnp.float32))
    normed_attn = normed_attn.astype(jnp.bfloat16)
    packed_f = jnp.einsum("npc,cd->npd", normed_attn, attn_qkv, preferred_element_type=jnp.float32)
    query_pix = (packed_f[0, :, :channels] * (1.0 / (math.sqrt(HEAD_DIM) * LN2))).astype(bf16)
    pad_pix = -local_pix % QB
    query_pix = jnp.pad(query_pix, ((0, pad_pix), (0, 0)))
    query_t = query_pix.T
    key_value = packed_f[0, :, channels:].astype(bf16)
    count = lax.axis_size("narrow")
    position = lax.axis_index("narrow")
    chunks = [key_value] + [None] * (count - 1)
    for bit in axis_bits("narrow"):
        chunks[bit] = swap(key_value, bit)
    keep_chunk = lambda index: lax.dynamic_slice_in_dim(
        keep_all[0], (position ^ index) * local_pix, local_pix, 0
    )
    keeps = [keep_chunk(index) for index in range(count)]
    aug_of = lambda indices: key_aug(jnp.concatenate([keeps[index] for index in indices]))
    state = attend_some(True, count == 2, query_t, chunks[:2], aug_of([0, 1]), ())
    for index in range(2, count):
        bit = low_bit(index)
        if index != bit:
            chunks[index] = swap(chunks[index ^ bit], bit)
        elif index < count - 1:
            chunks[index], state = lax.optimization_barrier((chunks[index], state))
    for index in range(2, count):
        state = attend_some(
            False, index == count - 1, query_t, [chunks[index]], aug_of([index]), state
        )
    heads_t, log_rows = state
    output, grad_mid, grad_rows, grad_t, top_grads, gate_grads, mid_sums = mid_layer(
        heads_t,
        stream[0],
        residual,
        skip,
        row_table(cross_term[0], gain_ff.astype(jnp.float32)),
        attn_out,
        geglu_in,
        geglu_out,
        proj_out,
    )
    owned = channels // lax.axis_size("wide")
    shares = top_shares(top_grads, gate_grads)
    grad_query_t = None
    totals = [None] * count
    arrived = [None] * count
    calls = [[count - 1]] + [[last - 1, last] for last in range(count - 2, 0, -2)] + [[0]]
    for call in calls:
        grad_query_t, *parts = attend_back_some(
            call[0] == count - 1,
            [bf16 if index % 2 else f32 for index in call],
            query_t,
            query_pix,
            grad_t,
            grad_rows,
            log_rows,
            heads_t,
            [chunks[index] for index in call],
            aug_of(call),
            grad_query_t,
        )
        for index, total in zip(call, parts):
            for source in range(index + 1, count):
                if source ^ low_bit(source) == index:
                    total = total + arrived[source].astype(f32)
            if index:
                arrived[index] = swap(total.astype(bf16), low_bit(index))
            totals[index] = total
    total = totals[0]
    grad_packed = jnp.concatenate(
        [
            grad_query_t.T[:local_pix].astype(bf16),
            total[0].astype(bf16),
            total[1].astype(bf16),
        ],
        axis=1,
    )[None]
    shares, grad_packed = lax.optimization_barrier((shares, grad_packed))
    grad_attn_whole = jnp.einsum(
        "npc,npd->dc", normed_attn, grad_packed, preferred_element_type=jnp.float32
    )
    grad_normed_attn = jnp.einsum(
        "npd,cd->npc", grad_packed, attn_qkv, preferred_element_type=jnp.float32
    )
    grad_from_attn, grad_gain_attn = attn_pull(grad_normed_attn)
    grad_stream = (grad_mid[None] + grad_from_attn).astype(jnp.bfloat16)
    grad_proj_in = jnp.einsum(
        "npc,npd->dc", spatial, grad_stream, preferred_element_type=jnp.float32
    )
    grad_spatial = jnp.einsum(
        "npd,cd->npc", grad_stream, proj_in, preferred_element_type=jnp.float32
    )
    grad_spatial = grad_spatial[0]
    query_key = by_owner(grad_attn_whole[: 2 * channels], owned)
    low_parts = jnp.stack(
        [
            grad_proj_in,
            query_key[:, :channels],
            query_key[:, channels:],
            grad_attn_whole[2 * channels :],
        ]
    ).astype(bf16)
    grad_halo = edge_rows(grad_spatial)
    kept = grad_spatial * pixel_keep
    sums = jnp.stack([jnp.sum(kept, axis=0), jnp.sum(kept * residual_hat, axis=0)])
    means, early_rows = group_means(
        sums, gain_three, counts, [mid_sums[0], mid_sums[1], grad_gain_attn]
    )
    grad_res, grad_pre, pack_second, sums = conv_back(
        width,
        grad_spatial,
        grad_halo,
        residual,
        residual_halo,
        skip,
        skip_halo,
        hidden,
        meta,
        row_table(
            center_three,
            scale_three,
            gain_three,
            means[0],
            means[1],
            center_two,
            scale_two,
            gain_two,
        ),
        conv_second,
    )
    grad_halo = edge_rows(grad_pre)
    means, middle_rows = group_means(sums[:2], gain_two, counts)
    held = jnp.concatenate([pack_second, low_parts], axis=2)
    bits = axis_bits("narrow")
    for bit in bits[:-1]:
        held = halve_step(held, bit, "narrow")
    held, grad_pre = lax.optimization_barrier((held, grad_pre))
    held = halve_step(held, bits[-1], "narrow")
    grad_hidden, grad_pre, pack_first, sums = conv_back(
        width,
        grad_pre,
        grad_halo,
        hidden,
        hidden_halo,
        None,
        None,
        pixels,
        meta,
        row_table(
            center_two,
            scale_two,
            gain_two,
            means[0],
            means[1],
            center_one,
            scale_one,
            gain_one,
        ),
        conv_first,
    )
    held, sums = lax.optimization_barrier((held, sums))
    means, late_rows = group_means(sums[:3], gain_one, counts)
    share_first = halve(pack_first, "narrow")
    image_hat = (image_in - center_one) * scale_one
    grad_image = grad_pre * pixel_keep * gain_one - means[0] - image_hat * means[1]
    grad_latents = (grad_res + pixel_keep * scale_one * grad_image).astype(jnp.bfloat16)[None]
    conv_rows = conv_first.shape[0]
    whole_second = wide_finish(held[0])
    lanes = pack_second.shape[2]
    sum_conv_second = conv_finish(whole_second[:, :, :lanes], conv_rows)
    low_whole = jnp.transpose(whole_second[:, :, lanes:], (0, 2, 1)).astype(f32)
    shares = [narrow_finish(share) for share in shares]
    sum_proj_out, sum_attn_out, sum_geglu_out, sum_geglu_in = split_top(shares, owned, channels)
    sum_conv_first = conv_finish(wide_finish(share_first), conv_rows)
    stamp_row = jnp.pad(
        jnp.concatenate([labels, timesteps]).astype(f32), (0, channels - 2 * images)
    )
    spread = double(
        jnp.stack(
            [
                early_rows[2],
                late_rows[2],
                early_rows[3],
                early_rows[4],
                early_rows[1],
                middle_rows[1],
                late_rows[1],
                stamp_row,
            ]
        ),
        "wide",
    )
    labels_all = spread[:, 7, 0].astype(jnp.int32)
    steps_all = spread[:, 7, 1].astype(jnp.int32)
    angles_all = steps_all.astype(jnp.float32)[:, None] * frequency[None, :]
    time_all = jax.nn.silu(jnp.concatenate([jnp.cos(angles_all), jnp.sin(angles_all)], axis=1))
    hot_all = (
        labels_all[:, None] == jnp.arange(class_table.shape[0], dtype=jnp.int32)[None, :]
    ).astype(jnp.float32)
    context_all = jnp.dot(hot_all, class_table.astype(jnp.float32), precision=HIGH)
    value_all = jnp.dot(context_all, value_weight, precision=HIGH)
    cross_all = spread[:, 0]
    grad_value_all = jnp.dot(cross_all, cross_weight.T, precision=HIGH)
    grad_context_all = jnp.dot(grad_value_all, value_weight.T, precision=HIGH)
    sum_cross_out = jnp.dot(value_all.T, own_columns(cross_all), precision=HIGH)
    sum_cross_value = jnp.dot(context_all.T, own_columns(grad_value_all), precision=HIGH)
    sum_class_table = jnp.dot(hot_all.T, own_columns(grad_context_all), precision=HIGH)
    sum_time_proj = jnp.dot(time_all.T, own_columns(spread[:, 1]), precision=HIGH)
    gain_sums = own_columns(jnp.sum(spread[:, 2:7], axis=0))
    return (
        output[None],
        grad_latents,
        gain_sums[4],
        sum_conv_first,
        sum_time_proj,
        gain_sums[3],
        sum_conv_second,
        gain_sums[2],
        low_whole[0],
        gain_sums[1],
        jnp.concatenate([low_whole[1], low_whole[2]], axis=1),
        low_whole[3],
        sum_attn_out,
        sum_class_table,
        sum_cross_value,
        sum_cross_out,
        gain_sums[0],
        sum_geglu_in,
        sum_geglu_out,
        sum_proj_out,
    )


def solution(mesh):
    placed = (
        P("wide", "narrow", None),
        P("wide", "narrow", None),
        P("wide"),
        P("wide", None),
        P("wide"),
        P("wide"),
        P(),
        P(),
        P(),
        P(),
        P(),
        P(),
        P(),
        P(),
        P(),
        P(),
        P(),
        P(),
        P(),
        P(),
        P(),
        P(),
        P(),
    )
    return jax.shard_map(
        per_device,
        mesh=mesh,
        in_specs=placed,
        out_specs=(
            P("wide", "narrow", None),
            P("wide", "narrow", None),
            P("wide"),
            P(None, "wide"),
            P(None, "wide"),
            P("wide"),
            P(None, "wide"),
            P("wide"),
            P(None, "wide"),
            P("wide"),
            P(None, "wide"),
            P(None, "wide"),
            P(None, "wide"),
            P(None, "wide"),
            P(None, "wide"),
            P(None, "wide"),
            P("wide"),
            P(None, "wide"),
            P(None, "wide"),
            P(None, "wide"),
        ),
        check_vma=False,
    )
```

```python
import functools
import math

import jax
import jax.numpy as jnp
from jax import lax
from jax.experimental import pallas as pl
from jax.experimental.pallas import tpu as pltpu
from jax.sharding import PartitionSpec as P

HEAD_DIM = 32
GROUPS = 32
SHORT = 48
LONG = 80


HIGH = lax.Precision.HIGHEST
EPS_GROUP = 1e-06
EPS_LAYER = 1e-05
MASKED = -1e30


TILE = 128
PER_TILE = TILE // HEAD_DIM
QB = 256
ONES = 16
SAFE_REACH = 90.0
LN2 = math.log(2.0)
bf16 = jnp.bfloat16
f32 = jnp.float32


def group_sum(value):
    grouped = value.reshape(value.shape[0], GROUPS, -1)
    summed = jnp.sum(grouped, axis=2, keepdims=True)
    return jnp.broadcast_to(summed, grouped.shape).reshape(value.shape)


def group_moments(sums, counts):
    sums = group_sum(narrow_sum(sums)) / counts[0]
    center = sums[0]
    spread = sums[1] - center * center
    return center, lax.rsqrt(spread + EPS_GROUP)


def group_means(sums, gain, counts, extras=()):
    sums = narrow_sum(jnp.concatenate([sums] + [row[None] for row in extras], axis=0))
    means = group_sum(sums[:2] * gain) / counts[0]
    return means, sums


def layer_norm(field_in, gain):
    center = jnp.mean(field_in, axis=-1, keepdims=True)
    spread = jnp.mean(jnp.square(field_in - center), axis=-1, keepdims=True)
    return (field_in - center) * lax.rsqrt(spread + EPS_LAYER) * gain


def head_rows(block, head):
    row = lax.broadcasted_iota(jnp.int32, block.shape, 0)
    inside = (row >= head * HEAD_DIM) & (row < (head + 1) * HEAD_DIM)
    return jnp.where(inside, block, jnp.zeros_like(block))


def head_lanes(block, head):
    lane = lax.broadcasted_iota(jnp.int32, block.shape, 1)
    inside = (lane >= head * HEAD_DIM) & (lane < (head + 1) * HEAD_DIM)
    return jnp.where(inside, block, jnp.zeros_like(block))


def mask_rows():
    row = lax.broadcasted_iota(jnp.int32, (TILE, QB), 0)
    return jnp.where(row == 0, 1.0, 0.0).astype(bf16)


def attend_kernel(first, last, parts, *refs):
    qt_ref = refs[0]
    key_refs = refs[1 : 1 + parts]
    value_refs = refs[1 + parts : 1 + 2 * parts]
    aug_ref = refs[1 + 2 * parts]
    rest = refs[2 + 2 * parts :]
    if not first:
        peak_in, acc_in = rest[:2]
        rest = rest[2:]
    if last:
        heads_ref, log_ref = rest
    else:
        peak_ref, acc_ref = rest
    keys = jnp.concatenate([ref[...] for ref in key_refs], axis=0)
    keys = jnp.concatenate([keys, aug_ref[...]], axis=1)
    values = jnp.concatenate([ref[...] for ref in value_refs], axis=0)
    value_t = jnp.transpose(values, (1, 0))
    ones = jnp.ones((ONES, value_t.shape[1]), bf16)
    low_rows = mask_rows()

    head_of = lambda shape, axis: lax.broadcasted_iota(jnp.int32, shape, axis) // HEAD_DIM
    pick = jnp.where(head_of((TILE, TILE), 0) == head_of((TILE, TILE), 1), 1.0, 0.0).astype(bf16)
    all_keys = keys[:, :TILE]
    key_norms = jnp.dot(all_keys * all_keys, pick, preferred_element_type=f32)
    all_queries = qt_ref[...]
    query_norms = jnp.dot(pick, all_queries * all_queries, preferred_element_type=f32)
    reach = jnp.float32(0.0)
    for head in range(PER_TILE):
        rows = slice(head * HEAD_DIM, head * HEAD_DIM + 8)
        mine = head_of(key_norms.shape, 1) == head
        key_peak = jnp.max(jnp.where(mine, key_norms, 0.0))
        reach = jnp.maximum(reach, key_peak * jnp.max(query_norms[rows]))

    def make_step(shifted):
        def block_step(step, carry):
            cols = pl.ds(pl.multiple_of(step * QB, QB), QB)
            qt = qt_ref[:, cols]
            for head in range(PER_TILE):
                rows = slice(head * HEAD_DIM, (head + 1) * HEAD_DIM)
                query = jnp.concatenate([head_rows(qt, head), low_rows], axis=0)
                scores = jnp.dot(keys, query, preferred_element_type=f32)
                if shifted:
                    peak = jnp.max(scores, axis=0, keepdims=True)
                    probs = jnp.exp2(scores - peak).astype(bf16)
                else:
                    peak = jnp.zeros((1, QB), f32)
                    probs = jnp.exp2(scores).astype(bf16)
                value_h = jnp.concatenate([value_t[rows], ones], axis=0)
                acc = jnp.dot(value_h, probs, preferred_element_type=f32)
                if not first:
                    peak_old = peak_in[head, 0:1, cols]
                    peak_new = jnp.maximum(peak, peak_old)
                    acc = acc * jnp.exp2(peak - peak_new)
                    acc = acc + acc_in[head, :, cols] * jnp.exp2(peak_old - peak_new)
                    peak = peak_new
                if last:
                    total = acc[HEAD_DIM : HEAD_DIM + 1]
                    heads_ref[rows, cols] = acc[:HEAD_DIM] / total
                    log_ref[head, :, cols] = jnp.broadcast_to(peak + jnp.log2(total), (8, QB))
                else:
                    acc_ref[head, :, cols] = acc
                    peak_ref[head, :, cols] = jnp.broadcast_to(peak, (8, QB))
            return carry

        return block_step

    steps = qt_ref.shape[1] // QB

    @pl.when(reach < SAFE_REACH * SAFE_REACH)
    def _():
        lax.fori_loop(0, steps, make_step(False), 0)

    @pl.when(jnp.logical_not(reach < SAFE_REACH * SAFE_REACH))
    def _():
        lax.fori_loop(0, steps, make_step(True), 0)


def chunk_specs(count, tiles, parts):
    key_spec = pl.BlockSpec((count, TILE), lambda t: (0, t))
    value_spec = pl.BlockSpec((count, TILE), lambda t: (0, tiles + t))
    aug_spec = pl.BlockSpec((parts * count, TILE), lambda t: (0, 0))
    return [key_spec] * parts + [value_spec] * parts + [aug_spec]


def attend_some(first, last, query_t, chunks, aug, state):
    channels, queries = query_t.shape
    count = chunks[0].shape[0]
    heads = channels // HEAD_DIM
    tiles = channels // TILE
    t_spec = pl.BlockSpec((TILE, queries), lambda t: (t, 0))
    cube = lambda t: (t, 0, 0)
    row_spec = pl.BlockSpec((PER_TILE, 8, queries), cube)
    acc_spec = pl.BlockSpec((PER_TILE, HEAD_DIM + ONES, queries), cube)
    in_specs = [t_spec] + chunk_specs(count, tiles, len(chunks))
    if not first:
        in_specs += [row_spec, acc_spec]
    row_shape = jax.ShapeDtypeStruct((heads, 8, queries), f32)
    if last:
        out_shape = (jax.ShapeDtypeStruct((channels, queries), f32), row_shape)
        out_specs = (t_spec, row_spec)
    else:
        out_shape = (
            row_shape,
            jax.ShapeDtypeStruct((heads, HEAD_DIM + ONES, queries), f32),
        )
        out_specs = (row_spec, acc_spec)
    return pl.pallas_call(
        functools.partial(attend_kernel, first, last, len(chunks)),
        grid=(tiles,),
        in_specs=in_specs,
        out_specs=out_specs,
        out_shape=out_shape,
        compiler_params=pltpu.CompilerParams(vmem_limit_bytes=58 << 20),
        cost_estimate=pl.CostEstimate(
            flops=32 * len(chunks) * channels * queries * count,
            bytes_accessed=8 * channels * (queries + count),
            transcendentals=len(chunks) * heads * queries * count,
        ),
        name="attend",
    )(query_t, *chunks, *chunks, aug, *state)


def attend_back_kernel(first, parts, *refs):
    qt_ref, q_ref, dt_ref, d_ref, log_ref, heads_ref = refs[:6]
    key_refs = refs[6 : 6 + parts]
    value_refs = refs[6 + parts : 6 + 2 * parts]
    aug_ref = refs[6 + 2 * parts]
    refs = refs[7 + 2 * parts :]
    if not first:
        dq_in = refs[0]
        refs = refs[1:]
    dq_ref = refs[0]
    out_refs = refs[1 : 1 + parts]
    dk_acc, dv_acc = refs[1 + parts :]
    count = key_refs[0].shape[0]
    k_tile = jnp.concatenate([ref[...] for ref in key_refs], axis=0)
    keys = jnp.concatenate([k_tile, aug_ref[...]], axis=1)
    values = jnp.concatenate([ref[...] for ref in value_refs], axis=0)
    key_t = jnp.transpose(k_tile, (1, 0))
    low_rows = mask_rows()
    dk_acc[...] = jnp.zeros_like(dk_acc)
    dv_acc[...] = jnp.zeros_like(dv_acc)
    factor = 1.0 / math.sqrt(HEAD_DIM)

    def block_step(step, carry):
        cols = pl.ds(pl.multiple_of(step * QB, QB), QB)
        qt = qt_ref[:, cols]
        dt = dt_ref[:, cols]
        q_blk = q_ref[cols, :]
        d_blk = d_ref[cols, :]
        probs_all, grads_all, q_all, d_all = [], [], [], []
        for head in range(PER_TILE):
            rows = slice(head * HEAD_DIM, (head + 1) * HEAD_DIM)
            query = jnp.concatenate([head_rows(qt, head), low_rows], axis=0)
            scores = jnp.dot(keys, query, preferred_element_type=f32)
            probs = jnp.exp2(scores - log_ref[head, 0:1, cols])
            weighted = jnp.sum(
                heads_ref[rows, cols] * dt[rows].astype(f32), axis=0, keepdims=True
            )
            grad_p = jnp.dot(values, head_rows(dt, head), preferred_element_type=f32)
            grad_s = (probs * (grad_p - weighted)).astype(bf16)
            probs_all.append(probs.astype(bf16))
            grads_all.append(grad_s)
            q_all.append(head_lanes(q_blk, head))
            d_all.append(head_lanes(d_blk, head))
            dq = jnp.dot(key_t[rows], grad_s, preferred_element_type=f32) * factor
            if not first:
                dq = dq + dq_in[rows, cols]
            dq_ref[rows, cols] = dq
        dv_acc[...] += jnp.dot(
            jnp.concatenate(probs_all, axis=1),
            jnp.concatenate(d_all, axis=0),
            preferred_element_type=f32,
        )
        dk_acc[...] += jnp.dot(
            jnp.concatenate(grads_all, axis=1),
            jnp.concatenate(q_all, axis=0),
            preferred_element_type=f32,
        )
        return carry

    lax.fori_loop(0, qt_ref.shape[1] // QB, block_step, 0)
    for index, ref in enumerate(out_refs):
        rows = slice(index * count, (index + 1) * count)
        ref[0] = (dk_acc[rows] * LN2).astype(ref.dtype)
        ref[1] = dv_acc[rows].astype(ref.dtype)


def attend_back_some(
    first, out_types, query_t, query, grad_t, grad, logs, heads_t, chunks, aug, dq
):
    channels, queries = query_t.shape
    count = chunks[0].shape[0]
    parts = len(chunks)
    tiles = channels // TILE
    t_spec = pl.BlockSpec((TILE, queries), lambda t: (t, 0))
    n_spec = pl.BlockSpec((queries, TILE), lambda t: (0, t))
    row_spec = pl.BlockSpec((PER_TILE, 8, queries), lambda t: (t, 0, 0))
    out_spec = pl.BlockSpec((2, count, TILE), lambda t: (0, 0, t))
    in_specs = [t_spec, n_spec, t_spec, n_spec, row_spec, t_spec] + chunk_specs(count, tiles, parts)
    state = ()
    if not first:
        in_specs.append(t_spec)
        state = (dq,)
    return pl.pallas_call(
        functools.partial(attend_back_kernel, first, parts),
        grid=(tiles,),
        in_specs=in_specs,
        out_specs=(t_spec,) + (out_spec,) * parts,
        out_shape=(jax.ShapeDtypeStruct((channels, queries), f32),)
        + tuple(jax.ShapeDtypeStruct((2, count, channels), kind) for kind in out_types),
        scratch_shapes=[pltpu.VMEM((parts * count, TILE), f32)] * 2,
        compiler_params=pltpu.CompilerParams(vmem_limit_bytes=58 << 20),
        cost_estimate=pl.CostEstimate(
            flops=80 * parts * channels * queries * count,
            bytes_accessed=12 * channels * (queries + count),
            transcendentals=parts * channels // HEAD_DIM * queries * count,
        ),
        name="attend_back",
    )(query_t, query, grad_t, grad, logs, heads_t, *chunks, *chunks, aug, *state)


def swap(value, bit, axis="narrow"):
    count = lax.axis_size(axis)
    return lax.ppermute(value, axis, [(i, i ^ bit) for i in range(count)])


def low_bit(index):
    return index & -index


def axis_bits(axis):
    return [1 << level for level in range(lax.axis_size(axis).bit_length() - 1)]


def my_bit(bit, axis="narrow"):
    return (lax.axis_index(axis) // bit) % 2


def narrow_sum(value):
    for bit in axis_bits("narrow"):
        value = value + swap(value, bit)
    return value


def key_aug(keep_chunk):
    lane = lax.broadcasted_iota(jnp.int32, (keep_chunk.shape[0], TILE), 1)
    bias = jnp.where(keep_chunk[:, None] > 0, 0.0, MASKED)
    return jnp.where(lane == 0, bias, 0.0).astype(bf16)


def halve_step(held, bit, axis):
    halves = held.reshape((held.shape[0] // 2, 2) + held.shape[1:])
    mine = my_bit(bit, axis)
    kept = lax.dynamic_index_in_dim(halves, mine, 1, keepdims=False)
    sent = lax.dynamic_index_in_dim(halves, 1 - mine, 1, keepdims=False)
    return (kept.astype(f32) + swap(sent, bit, axis).astype(f32)).astype(bf16)


def halve(held, axis):
    for bit in axis_bits(axis):
        held = halve_step(held, bit, axis)
    return held[0]


def double(value, axis):
    whole = value[None]
    for bit in reversed(axis_bits(axis)):
        other = swap(whole, bit, axis)
        pair = jnp.where(
            my_bit(bit, axis) == 0,
            jnp.stack([whole, other], axis=1),
            jnp.stack([other, whole], axis=1),
        )
        whole = pair.reshape((-1,) + value.shape)
    return whole


def narrow_share(pack):
    count = lax.axis_size("narrow")
    spot = lax.axis_index("narrow")
    pick = lambda index: lax.dynamic_index_in_dim(pack, spot ^ index, 0, keepdims=False)
    total = pick(0).astype(f32)
    for index in range(1, count):
        total = total + swap(pick(index), index).astype(f32)
    return total.astype(bf16)


def wide_finish(share):
    wide = lax.axis_size("wide")
    count = lax.axis_size("narrow")
    spot = lax.axis_index("narrow")
    share = halve(share.reshape(wide, share.shape[0] // wide, share.shape[1]), "wide")
    near = jnp.stack([share] + [swap(share, index) for index in range(1, count)])
    pick = lambda index: lax.dynamic_index_in_dim(near, spot ^ index, 0, keepdims=False)
    return jnp.stack([pick(index) for index in range(count)])


def conv_finish(whole, rows):
    return jnp.transpose(whole, (0, 2, 1)).reshape(-1, whole.shape[1])[:rows].astype(f32)


def by_owner(grad_t, width):
    wide = lax.axis_size("wide")
    groups = grad_t.shape[0] // wide // width
    split = grad_t.reshape(wide, groups, width, grad_t.shape[1])
    return jnp.transpose(split, (0, 2, 1, 3)).reshape(wide * width, -1)


def narrow_finish(share):
    share = share.astype(bf16)
    for bit in axis_bits("narrow"):
        share = (share.astype(f32) + swap(share, bit).astype(f32)).astype(bf16)
    return share.astype(f32)


def own_columns(value):
    width = value.shape[-1] // lax.axis_size("wide")
    start = lax.axis_index("wide") * width
    return lax.dynamic_slice_in_dim(value, start, width, value.ndim - 1)


CONV_LIMIT = 50 << 20
NT = (((1,), (1,)), ((), ()))


def lanes_of(meta_ref, index, start, count, channels):
    return jnp.concatenate([meta_ref[index, start : start + count]] * (channels // TILE), axis=1)


def store_shifts(field, meta_ref, stack_ref):
    total, channels = field.shape
    low = jnp.where(
        lanes_of(meta_ref, 1, 0, total, channels) > 0, pltpu.roll(field, 1, 0), 0.0
    )
    high = jnp.where(
        lanes_of(meta_ref, 2, 0, total, channels) > 0, pltpu.roll(field, total - 1, 0), 0.0
    )
    stack_ref[:, :channels] = low.astype(bf16)
    stack_ref[:, channels : 2 * channels] = field.astype(bf16)
    stack_ref[:, 2 * channels :] = high.astype(bf16)


def with_halo(low_ref, own_ref, high_ref):
    parts = [low_ref[...].astype(f32), own_ref[...].astype(f32), high_ref[...].astype(f32)]
    return jnp.concatenate(parts, axis=0)


def conv_kernel(width_ref, x_ref, low_ref, high_ref, meta_ref, rows_ref, w_ref, add_ref, y_ref, sum_ref, stack_ref):
    local, channels = x_ref.shape
    total = stack_ref.shape[0]
    width = width_ref[0]
    field = with_halo(low_ref, x_ref, high_ref)
    keep = lanes_of(meta_ref, 0, 0, total, channels)
    pre = keep * (field - rows_ref[0:1]) * (rows_ref[1:2] * rows_ref[2:3])
    store_shifts(pre / (1.0 + jnp.exp(-pre)), meta_ref, stack_ref)
    block = local // 2
    sum_ref[...] = jnp.zeros_like(sum_ref)

    def block_step(step, carry):
        start = step * block
        taps = []
        for shift in (-1, 0, 1):
            offset = pl.multiple_of(LONG + start + shift * width, 16)
            taps.append(stack_ref[pl.ds(offset, block), :])
        out = jnp.dot(jnp.concatenate(taps, axis=1), w_ref[...], preferred_element_type=f32)
        own = pl.ds(pl.multiple_of(start, 16), block)
        if add_ref.shape[0] == local:
            out = out + add_ref[own, :].astype(f32)
        else:
            out = out + add_ref[0:1]
        y_ref[own, :] = out
        kept = meta_ref[0, pl.ds(pl.multiple_of(LONG + start, 16), block), :]
        kept = out * jnp.concatenate([kept] * (channels // TILE), axis=1)
        sum_ref[0:1] += jnp.sum(kept, axis=0, keepdims=True)
        sum_ref[1:2] += jnp.sum(kept * out, axis=0, keepdims=True)
        return carry

    lax.fori_loop(0, 2, block_step, 0)


def conv_forward(width, field, halo, meta, rows, weight, add):
    local, channels = field.shape
    vmem = pl.BlockSpec(memory_space=pltpu.VMEM)
    return pl.pallas_call(
        conv_kernel,
        in_specs=[pl.BlockSpec(memory_space=pltpu.SMEM)] + [vmem] * 7,
        out_specs=(vmem, vmem),
        out_shape=(
            jax.ShapeDtypeStruct((local, channels), f32),
            jax.ShapeDtypeStruct((8, channels), f32),
        ),
        scratch_shapes=[pltpu.VMEM((local + 2 * LONG, 3 * channels), bf16)],
        compiler_params=pltpu.CompilerParams(vmem_limit_bytes=CONV_LIMIT),
        cost_estimate=pl.CostEstimate(
            flops=2 * local * weight.size,
            bytes_accessed=4 * weight.size,
            transcendentals=2 * local * channels,
        ),
        name="conv_forward",
    )(width, field, halo[0], halo[1], meta, rows, weight, add)


def conv_build(with_skip, refs, meta_ref, rows_ref, stack_ref):
    d_ref, d_low, d_high, v_ref, v_low, v_high = refs[:6]
    local, channels = d_ref.shape
    total = stack_ref.shape[0]
    keep = lanes_of(meta_ref, 0, 0, total, channels)
    normed = (with_halo(v_low, v_ref, v_high) - rows_ref[0:1]) * rows_ref[1:2]
    inner = with_halo(d_low, d_ref, d_high) * keep * rows_ref[2:3] - rows_ref[3:4]
    field = keep * rows_ref[1:2] * (inner - normed * rows_ref[4:5])
    if with_skip:
        c_ref, c_low, c_high = refs[6:9]
        field = field + with_halo(c_low, c_ref, c_high)
    store_shifts(field, meta_ref, stack_ref)
    return field[LONG : LONG + local]


def conv_pull(width, x_ref, meta_ref, rows_ref, w_ref, stack_ref, pre_ref, sum_ref):
    local, channels = x_ref.shape
    block = local // 2

    def block_step(step, carry):
        start = step * block
        own = pl.ds(pl.multiple_of(start, 16), block)
        out = jnp.zeros((block, channels), f32)
        for row in range(3):
            offset = pl.multiple_of(LONG + start + (row - 1) * width, 16)
            for col in range(3):
                tap = 8 - (3 * row + col)
                out = out + lax.dot_general(
                    stack_ref[pl.ds(offset, block), col * channels : (col + 1) * channels],
                    w_ref[tap * channels : (tap + 1) * channels, :],
                    NT,
                    preferred_element_type=f32,
                )
        kept = meta_ref[0, pl.ds(pl.multiple_of(LONG + start, 16), block), :]
        kept = jnp.concatenate([kept] * (channels // TILE), axis=1)
        xhat = (x_ref[own, :].astype(f32) - rows_ref[5:6]) * rows_ref[6:7]
        pre = kept * xhat * rows_ref[7:8]
        gate = 1.0 / (1.0 + jnp.exp(-pre))
        grad = out * (gate * (1.0 + pre * (1.0 - gate)))
        pre_ref[own, :] = grad
        grad = grad * kept
        sum_ref[0:1] += jnp.sum(grad, axis=0, keepdims=True)
        sum_ref[1:2] += jnp.sum(grad * xhat, axis=0, keepdims=True)
        return carry

    lax.fori_loop(0, 2, block_step, 0)


def conv_weight(width, x_ref, meta_ref, rows_ref, stack_ref, pack_ref, extra_ref):
    local, channels = x_ref.shape
    kept = lanes_of(meta_ref, 0, LONG, local, channels)
    pre = kept * (x_ref[...].astype(f32) - rows_ref[5:6]) * (rows_ref[6:7] * rows_ref[7:8])
    act_t = jnp.transpose((pre / (1.0 + jnp.exp(-pre))).astype(bf16), (1, 0))
    extra = 0 if extra_ref is None else extra_ref.shape[2]
    groups = (pack_ref.shape[2] - extra) // TILE
    tiles = channels // TILE
    for row in range(3):
        offset = pl.multiple_of(LONG + (row - 1) * width, 16)
        for col in range(3):
            tap = 8 - (3 * row + col)
            grad = jnp.dot(
                act_t,
                stack_ref[pl.ds(offset, local), col * channels : (col + 1) * channels],
                preferred_element_type=f32,
            )
            grad = jnp.transpose(grad.astype(bf16), (1, 0))
            for tile in range(tiles):
                spot = tap * tiles + tile
                lane = (spot % groups) * TILE
                pack_ref[spot // groups, :, lane : lane + TILE] = grad[
                    :, tile * TILE : (tile + 1) * TILE
                ]
    for spot in range(9 * tiles, pack_ref.shape[0] * groups):
        lane = (spot % groups) * TILE
        pack_ref[spot // groups, :, lane : lane + TILE] = jnp.zeros((channels, TILE), bf16)
    if extra:
        pack_ref[:, :, groups * TILE :] = extra_ref[...]


def pull_first_kernel(width_ref, *refs):
    x_ref, meta_ref, rows_ref, w_ref, e_ref, stack_ref, pre_ref, sum_ref = refs[9:]
    e_ref[...] = conv_build(True, refs, meta_ref, rows_ref, stack_ref)
    sum_ref[...] = jnp.zeros_like(sum_ref)
    conv_pull(width_ref[0], x_ref, meta_ref, rows_ref, w_ref, stack_ref, pre_ref, sum_ref)


def weight_after_kernel(width_ref, stack_ref, x_ref, meta_ref, rows_ref, extra_ref, pack_ref):
    conv_weight(width_ref[0], x_ref, meta_ref, rows_ref, stack_ref, pack_ref, extra_ref)


def weight_first_kernel(width_ref, *refs):
    x_ref, meta_ref, rows_ref, stack_ref, pack_ref, sum_ref = refs[6:]
    field = conv_build(False, refs, meta_ref, rows_ref, stack_ref)
    sum_ref[...] = jnp.broadcast_to(jnp.sum(field, axis=0, keepdims=True), sum_ref.shape)
    conv_weight(width_ref[0], x_ref, meta_ref, rows_ref, stack_ref, pack_ref, None)


def pull_after_kernel(width_ref, stack_ref, x_ref, meta_ref, rows_ref, w_ref, pre_ref, sum_ref):
    sum_ref[...] = jnp.zeros_like(sum_ref)
    conv_pull(width_ref[0], x_ref, meta_ref, rows_ref, w_ref, stack_ref, pre_ref, sum_ref)


def conv_call(kernel, name, width, operands, shapes, flops):
    vmem = pl.BlockSpec(memory_space=pltpu.VMEM)
    return pl.pallas_call(
        kernel,
        in_specs=[pl.BlockSpec(memory_space=pltpu.SMEM)] + [vmem] * len(operands),
        out_specs=(vmem,) * len(shapes),
        out_shape=tuple(jax.ShapeDtypeStruct(shape, kind) for shape, kind in shapes),
        compiler_params=pltpu.CompilerParams(vmem_limit_bytes=CONV_LIMIT),
        cost_estimate=pl.CostEstimate(flops=flops, bytes_accessed=1 << 24, transcendentals=0),
        name=name,
    )(width, *operands)


def pack_width(weight):
    count = lax.axis_size("narrow")
    return (weight.shape[0] + (-weight.shape[0] % (count * TILE))) // count


def edge_rows(*fields):
    count = lax.axis_size("narrow")
    forward = [(i, i + 1) for i in range(count - 1)]
    backward = [(i + 1, i) for i in range(count - 1)]
    tails = jnp.concatenate([field[-LONG:] for field in fields], axis=0)
    heads = jnp.concatenate([field[:LONG] for field in fields], axis=0)
    low = lax.ppermute(tails, "narrow", forward)
    high = lax.ppermute(heads, "narrow", backward)
    cut = lambda rim, index: rim[index * LONG : (index + 1) * LONG]
    return [(cut(low, index), cut(high, index)) for index in range(len(fields))]


def pixel_meta(keep_image, row_start, local, row_width):
    rim = jnp.pad(keep_image, (LONG, LONG))
    keep = lax.dynamic_slice_in_dim(rim, row_start, local + 2 * LONG, 0)
    spot = jnp.arange(local + 2 * LONG, dtype=jnp.int32)
    column = (spot + 2 * LONG * SHORT - LONG) % row_width
    rows = jnp.stack([keep, (column > 0).astype(f32), (column < row_width - 1).astype(f32)])
    return jnp.broadcast_to(rows[:, :, None], rows.shape + (TILE,))


def row_table(*rows):
    table = jnp.stack([jnp.broadcast_to(row.reshape(-1), rows[0].reshape(-1).shape) for row in rows])
    return jnp.pad(table, ((0, 8 - len(rows)), (0, 0)))


MID_BLOCKS = 4


def dot_nt(left, right):
    return lax.dot_general(left, right, NT, preferred_element_type=f32)


def mid_kernel(
    owned,
    heads_ref,
    stream_ref,
    residual_ref,
    cot_ref,
    row_ref,
    attn_out_ref,
    geglu_in_ref,
    geglu_out_ref,
    proj_out_ref,
    out_ref,
    grad_mid_ref,
    grad_ref,
    grad_t_ref,
    top_ref,
    gate_ref,
    sum_ref,
    heads_low,
    normed_low,
    mixed_low,
    end_low,
    ffo_low,
    gates_low,
    mid_low,
):
    local, channels = stream_ref.shape
    hidden = geglu_out_ref.shape[0]
    block = local // MID_BLOCKS
    heads_low[...] = jnp.transpose(heads_ref[...].astype(bf16), (1, 0))[:local]
    sum_ref[...] = jnp.zeros_like(sum_ref)

    def block_step(step, carry):
        own = pl.ds(pl.multiple_of(step * block, 16), block)
        mid = stream_ref[own, :] + row_ref[0:1]
        mid = mid + jnp.dot(heads_low[own, :], attn_out_ref[...], preferred_element_type=f32)
        center = jnp.mean(mid, axis=1, keepdims=True)
        inv_std = lax.rsqrt(jnp.mean(jnp.square(mid - center), axis=1, keepdims=True) + EPS_LAYER)
        xhat = (mid - center) * inv_std
        normed = (xhat * row_ref[1:2]).astype(bf16)
        normed_low[own, :] = normed
        gates = jnp.dot(normed, geglu_in_ref[...], preferred_element_type=f32)
        value, gate = gates[:, :hidden], gates[:, hidden:]
        half = 0.5 * (1.0 + lax.erf(gate * math.sqrt(0.5)))
        gelu = gate * half
        slope = half + gate * jnp.exp(-0.5 * gate * gate) * (1.0 / math.sqrt(2.0 * math.pi))
        mixed = (value * gelu).astype(bf16)
        mixed_low[own, :] = mixed
        end = mid + jnp.dot(mixed, geglu_out_ref[...], preferred_element_type=f32)
        end = end.astype(bf16)
        end_low[own, :] = end
        out = residual_ref[own, :] + jnp.dot(end, proj_out_ref[...], preferred_element_type=f32)
        out_ref[own, :] = out.astype(bf16)
        grad_end = dot_nt(cot_ref[own, :], proj_out_ref[...])
        grad_ffo = grad_end.astype(bf16)
        ffo_low[own, :] = grad_ffo
        grad_mixed = dot_nt(grad_ffo, geglu_out_ref[...])
        grad_gates = jnp.concatenate(
            [(grad_mixed * gelu).astype(bf16), (grad_mixed * value * slope).astype(bf16)], axis=1
        )
        gates_low[own, :] = grad_gates
        grad_normed = dot_nt(grad_gates, geglu_in_ref[...])
        grad_hat = grad_normed * row_ref[1:2]
        mean_one = jnp.mean(grad_hat, axis=1, keepdims=True)
        mean_two = jnp.mean(grad_hat * xhat, axis=1, keepdims=True)
        grad_mid = grad_end + inv_std * (grad_hat - mean_one - xhat * mean_two)
        grad_mid_ref[own, :] = grad_mid
        sum_ref[0:1] += jnp.sum(grad_mid, axis=0, keepdims=True)
        sum_ref[1:2] += jnp.sum(grad_normed * xhat, axis=0, keepdims=True)
        grad_mid = grad_mid.astype(bf16)
        mid_low[own, :] = grad_mid
        grad_ref[own, :] = dot_nt(grad_mid, attn_out_ref[...]).astype(bf16)
        return carry

    lax.fori_loop(0, MID_BLOCKS, block_step, 0)
    pad = grad_ref.shape[0] - local
    if pad:
        grad_ref[local:, :] = jnp.zeros((pad, channels), bf16)
    grad_t_ref[...] = jnp.transpose(grad_ref[...], (1, 0))

    def put(index, grad):
        if owned:
            for owner in range(channels // owned):
                rows = grad[owner * owned : (owner + 1) * owned]
                top_ref[owner, index * owned : (index + 1) * owned, :] = rows
        else:
            top_ref[:, index * channels : (index + 1) * channels] = grad

    put(
        0,
        jnp.dot(
            jnp.transpose(cot_ref[...], (1, 0)), end_low[...], preferred_element_type=f32
        ),
    )
    put(
        1,
        jnp.dot(
            jnp.transpose(mid_low[...], (1, 0)), heads_low[...], preferred_element_type=f32
        ),
    )
    ffo_t = jnp.transpose(ffo_low[...], (1, 0))
    pieces = hidden // channels
    for piece in range(pieces):
        mixed = mixed_low[:, piece * channels : (piece + 1) * channels]
        put(2 + piece, jnp.dot(ffo_t, mixed, preferred_element_type=f32))
    normed_t = jnp.transpose(normed_low[...], (1, 0))
    for piece in range(2 * pieces):
        grads = gates_low[:, piece * channels : (piece + 1) * channels]
        grad = jnp.dot(normed_t, grads, preferred_element_type=f32)
        if owned:
            top_ref[piece, (2 + pieces) * owned :, :] = grad
        else:
            gate_ref[:, piece * channels : (piece + 1) * channels] = grad


def mid_layer(heads_t, stream, residual, cotangent, rows, attn_out, geglu_in, geglu_out, proj_out):
    local, channels = stream.shape
    queries = heads_t.shape[1]
    hidden = geglu_out.shape[0]
    wide = lax.axis_size("wide")
    pieces = 2 + hidden // channels
    aligned = 2 * hidden == wide * channels
    owned = channels // wide if aligned else 0
    if aligned:
        top_shape = jax.ShapeDtypeStruct((wide, pieces * owned + channels, channels), f32)
        gate_shape = jax.ShapeDtypeStruct((8, channels), f32)
    else:
        top_shape = jax.ShapeDtypeStruct((channels, pieces * channels), f32)
        gate_shape = jax.ShapeDtypeStruct((channels, 2 * hidden), f32)
    vmem = pl.BlockSpec(memory_space=pltpu.VMEM)
    low = lambda width: pltpu.VMEM((local, width), bf16)
    return pl.pallas_call(
        functools.partial(mid_kernel, owned),
        in_specs=[vmem] * 9,
        out_specs=(vmem,) * 7,
        out_shape=(
            jax.ShapeDtypeStruct((local, channels), bf16),
            jax.ShapeDtypeStruct((local, channels), f32),
            jax.ShapeDtypeStruct((queries, channels), bf16),
            jax.ShapeDtypeStruct((channels, queries), bf16),
            top_shape,
            gate_shape,
            jax.ShapeDtypeStruct((8, channels), f32),
        ),
        scratch_shapes=[
            low(channels),
            low(channels),
            low(hidden),
            low(channels),
            low(channels),
            low(2 * hidden),
            low(channels),
        ],
        compiler_params=pltpu.CompilerParams(vmem_limit_bytes=57 << 20),
        cost_estimate=pl.CostEstimate(
            flops=6 * local * channels * (3 * hidden + 2 * channels),
            bytes_accessed=24 * channels * hidden,
            transcendentals=2 * local * hidden,
        ),
        name="mid_layer",
    )(heads_t, stream, residual, cotangent, rows, attn_out, geglu_in, geglu_out, proj_out)


def top_shares(top, gates):
    wide = lax.axis_size("wide")
    if top.ndim == 3:
        share = lax.psum_scatter(top, "wide", scatter_dimension=0, tiled=True)[0]
        return (share,)
    channels = top.shape[0]
    split = top.reshape(wide, channels // wide, -1, channels)
    split = jnp.transpose(split, (0, 2, 1, 3)).reshape(wide, -1, channels)
    share = lax.psum_scatter(split, "wide", scatter_dimension=0, tiled=True)[0]
    gates = jnp.transpose(gates.reshape(channels, wide, -1), (1, 0, 2))
    return share, lax.psum_scatter(gates, "wide", scatter_dimension=0, tiled=True)[0]


def split_top(shares, owned, channels):
    if len(shares) == 1:
        count = shares[0].shape[0] - channels
        gates = shares[0][count:]
    else:
        count = shares[0].shape[0]
        gates = shares[1]
    pieces = shares[0][:count].reshape(-1, owned, channels)
    pieces = jnp.transpose(pieces, (0, 2, 1))
    return pieces[0], pieces[1], pieces[2:].reshape(-1, owned), gates


def per_device(
    latents,
    cotangent,
    bucket,
    pixel_mask,
    labels,
    timesteps,
    gain_first,
    conv_first,
    time_proj,
    gain_second,
    conv_second,
    gain_spatial,
    proj_in,
    gain_attn,
    attn_qkv,
    attn_out,
    class_table,
    cross_value,
    cross_out,
    gain_ff,
    geglu_in,
    geglu_out,
    proj_out,
):
    images, local_pix, channels = latents.shape
    row_start = lax.axis_index("narrow") * local_pix
    keep_all = pixel_mask.astype(jnp.float32)
    pixel_keep = lax.dynamic_slice_in_dim(keep_all, row_start, local_pix, 1)[0, :, None]
    counts = jnp.sum(keep_all, axis=1) * (channels // GROUPS)
    row_width = jnp.where(bucket[0] == 0, LONG, SHORT).astype(jnp.int32)
    width = row_width[None]
    meta = pixel_meta(keep_all[0], row_start, local_pix, row_width)
    pixels = latents[0]
    skip = cotangent[0]
    pixel_halo, skip_halo = edge_rows(pixels, skip)
    half_dim = time_proj.shape[0] // 2
    frequency = jnp.exp(-math.log(10000.0) * jnp.arange(half_dim, dtype=jnp.float32) / half_dim)
    angles = timesteps.astype(jnp.float32)[:, None] * frequency[None, :]
    time_act = jax.nn.silu(jnp.concatenate([jnp.cos(angles), jnp.sin(angles)], axis=1))
    time_term = jnp.dot(time_act, time_proj.astype(jnp.float32), precision=HIGH)
    label_hot = (
        labels[:, None] == jnp.arange(class_table.shape[0], dtype=jnp.int32)[None, :]
    ).astype(jnp.float32)
    context = jnp.dot(label_hot, class_table.astype(jnp.float32), precision=HIGH)
    value_weight = cross_value.astype(jnp.float32)
    cross_weight = cross_out.astype(jnp.float32)
    value_term = jnp.dot(context, value_weight, precision=HIGH)
    cross_term = jnp.dot(value_term, cross_weight, precision=HIGH)
    gain_one = gain_first.astype(jnp.float32)
    gain_two = gain_second.astype(jnp.float32)
    gain_three = gain_spatial.astype(jnp.float32)
    image_in = pixels.astype(jnp.float32)
    kept = image_in * pixel_keep
    sums_one = jnp.stack([jnp.sum(kept, axis=0), jnp.sum(kept * image_in, axis=0)])
    center_one, scale_one = group_moments(sums_one, counts)
    hidden, sums_two = conv_forward(
        width,
        pixels,
        pixel_halo,
        meta,
        row_table(center_one, scale_one, gain_one),
        conv_first,
        row_table(time_term[0]),
    )
    (hidden_halo,) = edge_rows(hidden)
    center_two, scale_two = group_moments(sums_two[:2], counts)
    residual, sums_three = conv_forward(
        width,
        hidden,
        hidden_halo,
        meta,
        row_table(center_two, scale_two, gain_two),
        conv_second,
        pixels,
    )
    center_three, scale_three = group_moments(sums_three[:2], counts)
    residual_hat = (residual - center_three) * scale_three
    spatial = (pixel_keep * residual_hat * gain_three).astype(jnp.bfloat16)[None]
    stream = jnp.einsum("npc,cd->npd", spatial, proj_in, preferred_element_type=jnp.float32)
    normed_attn, attn_pull = jax.vjp(layer_norm, stream, gain_attn.astype(jnp.float32))
    normed_attn = normed_attn.astype(jnp.bfloat16)
    packed_f = jnp.einsum("npc,cd->npd", normed_attn, attn_qkv, preferred_element_type=jnp.float32)
    query_pix = (packed_f[0, :, :channels] * (1.0 / (math.sqrt(HEAD_DIM) * LN2))).astype(bf16)
    pad_pix = -local_pix % QB
    query_pix = jnp.pad(query_pix, ((0, pad_pix), (0, 0)))
    query_t = query_pix.T
    key_value = packed_f[0, :, channels:].astype(bf16)
    count = lax.axis_size("narrow")
    position = lax.axis_index("narrow")
    chunks = [key_value] + [None] * (count - 1)
    for bit in axis_bits("narrow"):
        chunks[bit] = swap(key_value, bit)
    keep_chunk = lambda index: lax.dynamic_slice_in_dim(
        keep_all[0], (position ^ index) * local_pix, local_pix, 0
    )
    keeps = [keep_chunk(index) for index in range(count)]
    aug_of = lambda indices: key_aug(jnp.concatenate([keeps[index] for index in indices]))
    state = attend_some(True, count == 2, query_t, chunks[:2], aug_of([0, 1]), ())
    for index in range(2, count):
        bit = low_bit(index)
        if index != bit:
            chunks[index] = swap(chunks[index ^ bit], bit)
        elif index < count - 1:
            chunks[index], state = lax.optimization_barrier((chunks[index], state))
    for index in range(2, count):
        state = attend_some(
            False, index == count - 1, query_t, [chunks[index]], aug_of([index]), state
        )
    heads_t, log_rows = state
    output, grad_mid, grad_rows, grad_t, top_grads, gate_grads, mid_sums = mid_layer(
        heads_t,
        stream[0],
        residual,
        skip,
        row_table(cross_term[0], gain_ff.astype(jnp.float32)),
        attn_out,
        geglu_in,
        geglu_out,
        proj_out,
    )
    owned = channels // lax.axis_size("wide")
    shares = top_shares(top_grads, gate_grads)
    grad_query_t = None
    totals = [None] * count
    arrived = [None] * count
    calls = [[count - 1]] + [[last - 1, last] for last in range(count - 2, 0, -2)] + [[0]]
    for call in calls:
        grad_query_t, *parts = attend_back_some(
            call[0] == count - 1,
            [bf16 if index % 2 else f32 for index in call],
            query_t,
            query_pix,
            grad_t,
            grad_rows,
            log_rows,
            heads_t,
            [chunks[index] for index in call],
            aug_of(call),
            grad_query_t,
        )
        for index, total in zip(call, parts):
            for source in range(index + 1, count):
                if source ^ low_bit(source) == index:
                    total = total + arrived[source].astype(f32)
            if index:
                arrived[index] = swap(total.astype(bf16), low_bit(index))
            totals[index] = total
    total = totals[0]
    grad_packed = jnp.concatenate(
        [
            grad_query_t.T[:local_pix].astype(bf16),
            total[0].astype(bf16),
            total[1].astype(bf16),
        ],
        axis=1,
    )[None]
    shares, grad_packed = lax.optimization_barrier((shares, grad_packed))
    grad_attn_whole = jnp.einsum(
        "npc,npd->dc", normed_attn, grad_packed, preferred_element_type=jnp.float32
    )
    grad_normed_attn = jnp.einsum(
        "npd,cd->npc", grad_packed, attn_qkv, preferred_element_type=jnp.float32
    )
    grad_from_attn, grad_gain_attn = attn_pull(grad_normed_attn)
    grad_stream = (grad_mid[None] + grad_from_attn).astype(jnp.bfloat16)
    grad_proj_in = jnp.einsum(
        "npc,npd->dc", spatial, grad_stream, preferred_element_type=jnp.float32
    )
    grad_spatial = jnp.einsum(
        "npd,cd->npc", grad_stream, proj_in, preferred_element_type=jnp.float32
    )
    grad_spatial = grad_spatial[0]
    query_key = by_owner(grad_attn_whole[: 2 * channels], owned)
    low_parts = jnp.stack(
        [
            grad_proj_in,
            query_key[:, :channels],
            query_key[:, channels:],
            grad_attn_whole[2 * channels :],
        ]
    ).astype(bf16)
    grad_halo, residual_halo = edge_rows(grad_spatial, residual)
    kept = grad_spatial * pixel_keep
    sums = jnp.stack([jnp.sum(kept, axis=0), jnp.sum(kept * residual_hat, axis=0)])
    means, early_rows = group_means(
        sums, gain_three, counts, [mid_sums[0], mid_sums[1], grad_gain_attn]
    )
    pixel_shape = (local_pix, channels)
    stack_shape = ((local_pix + 2 * LONG, 3 * channels), bf16)
    sum_shape = ((8, channels), f32)
    lanes = pack_width(conv_second)
    flops = 2 * local_pix * conv_second.size
    rows_back = row_table(
        center_three,
        scale_three,
        gain_three,
        means[0],
        means[1],
        center_two,
        scale_two,
        gain_two,
    )
    grad_res, stack_second, grad_pre, sums = conv_call(
        pull_first_kernel,
        "conv_pull",
        width,
        [grad_spatial, *grad_halo, residual, *residual_halo, skip, *skip_halo]
        + [hidden, meta, rows_back, conv_second],
        [(pixel_shape, f32), stack_shape, (pixel_shape, f32), sum_shape],
        flops,
    )
    (grad_halo,) = edge_rows(grad_pre)
    means, middle_rows = group_means(sums[:2], gain_two, counts)
    (pack_second,) = conv_call(
        weight_after_kernel,
        "conv_weight",
        width,
        [stack_second, hidden, meta, rows_back, low_parts],
        [((count, channels, lanes + channels), bf16)],
        flops,
    )
    rows_back = row_table(
        center_two,
        scale_two,
        gain_two,
        means[0],
        means[1],
        center_one,
        scale_one,
        gain_one,
    )
    share_second = narrow_share(pack_second)
    stack_first, pack_first, hidden_sums = conv_call(
        weight_first_kernel,
        "conv_weight",
        width,
        [grad_pre, *grad_halo, hidden, *hidden_halo, pixels, meta, rows_back],
        [stack_shape, ((count, channels, lanes), bf16), sum_shape],
        flops,
    )
    share_first = narrow_share(pack_first)
    grad_pre, sums = conv_call(
        pull_after_kernel,
        "conv_pull",
        width,
        [stack_first, pixels, meta, rows_back, conv_first],
        [(pixel_shape, f32), sum_shape],
        flops,
    )
    means, late_rows = group_means(sums[:2], gain_one, counts, [hidden_sums[0]])
    image_hat = (image_in - center_one) * scale_one
    grad_image = grad_pre * pixel_keep * gain_one - means[0] - image_hat * means[1]
    grad_latents = (grad_res + pixel_keep * scale_one * grad_image).astype(jnp.bfloat16)[None]
    conv_rows = conv_first.shape[0]
    whole_second = wide_finish(share_second)
    sum_conv_second = conv_finish(whole_second[:, :, :lanes], conv_rows)
    low_whole = jnp.transpose(whole_second[:, :, lanes:], (0, 2, 1)).astype(f32)
    shares = [narrow_finish(share) for share in shares]
    sum_proj_out, sum_attn_out, sum_geglu_out, sum_geglu_in = split_top(shares, owned, channels)
    sum_conv_first = conv_finish(wide_finish(share_first), conv_rows)
    stamp_row = jnp.pad(
        jnp.concatenate([labels, timesteps]).astype(f32), (0, channels - 2 * images)
    )
    spread = double(
        jnp.stack(
            [
                early_rows[2],
                late_rows[2],
                early_rows[3],
                early_rows[4],
                early_rows[1],
                middle_rows[1],
                late_rows[1],
                stamp_row,
            ]
        ),
        "wide",
    )
    labels_all = spread[:, 7, 0].astype(jnp.int32)
    steps_all = spread[:, 7, 1].astype(jnp.int32)
    angles_all = steps_all.astype(jnp.float32)[:, None] * frequency[None, :]
    time_all = jax.nn.silu(jnp.concatenate([jnp.cos(angles_all), jnp.sin(angles_all)], axis=1))
    hot_all = (
        labels_all[:, None] == jnp.arange(class_table.shape[0], dtype=jnp.int32)[None, :]
    ).astype(jnp.float32)
    context_all = jnp.dot(hot_all, class_table.astype(jnp.float32), precision=HIGH)
    value_all = jnp.dot(context_all, value_weight, precision=HIGH)
    cross_all = spread[:, 0]
    grad_value_all = jnp.dot(cross_all, cross_weight.T, precision=HIGH)
    grad_context_all = jnp.dot(grad_value_all, value_weight.T, precision=HIGH)
    sum_cross_out = jnp.dot(value_all.T, own_columns(cross_all), precision=HIGH)
    sum_cross_value = jnp.dot(context_all.T, own_columns(grad_value_all), precision=HIGH)
    sum_class_table = jnp.dot(hot_all.T, own_columns(grad_context_all), precision=HIGH)
    sum_time_proj = jnp.dot(time_all.T, own_columns(spread[:, 1]), precision=HIGH)
    gain_sums = own_columns(jnp.sum(spread[:, 2:7], axis=0))
    return (
        output[None],
        grad_latents,
        gain_sums[4],
        sum_conv_first,
        sum_time_proj,
        gain_sums[3],
        sum_conv_second,
        gain_sums[2],
        low_whole[0],
        gain_sums[1],
        jnp.concatenate([low_whole[1], low_whole[2]], axis=1),
        low_whole[3],
        sum_attn_out,
        sum_class_table,
        sum_cross_value,
        sum_cross_out,
        gain_sums[0],
        sum_geglu_in,
        sum_geglu_out,
        sum_proj_out,
    )


def solution(mesh):
    placed = (
        P("wide", "narrow", None),
        P("wide", "narrow", None),
        P("wide"),
        P("wide", None),
        P("wide"),
        P("wide"),
        P(),
        P(),
        P(),
        P(),
        P(),
        P(),
        P(),
        P(),
        P(),
        P(),
        P(),
        P(),
        P(),
        P(),
        P(),
        P(),
        P(),
    )
    return jax.shard_map(
        per_device,
        mesh=mesh,
        in_specs=placed,
        out_specs=(
            P("wide", "narrow", None),
            P("wide", "narrow", None),
            P("wide"),
            P(None, "wide"),
            P(None, "wide"),
            P("wide"),
            P(None, "wide"),
            P("wide"),
            P(None, "wide"),
            P("wide"),
            P(None, "wide"),
            P(None, "wide"),
            P(None, "wide"),
            P(None, "wide"),
            P(None, "wide"),
            P(None, "wide"),
            P("wide"),
            P(None, "wide"),
            P(None, "wide"),
            P(None, "wide"),
        ),
        check_vma=False,
    )
```

```python
import functools
import math

import jax
import jax.numpy as jnp
from jax import lax
from jax.experimental import pallas as pl
from jax.experimental.pallas import tpu as pltpu
from jax.sharding import PartitionSpec as P

HEAD_DIM = 32
GROUPS = 32
SHORT = 48
LONG = 80


HIGH = lax.Precision.HIGHEST
EPS_GROUP = 1e-06
EPS_LAYER = 1e-05
MASKED = -1e30


TILE = 128
PER_TILE = TILE // HEAD_DIM
QB = 256
ONES = 16
SAFE_REACH = 90.0
LN2 = math.log(2.0)
bf16 = jnp.bfloat16
f32 = jnp.float32


def group_sum(value):
    grouped = value.reshape(value.shape[0], GROUPS, -1)
    summed = jnp.sum(grouped, axis=2, keepdims=True)
    return jnp.broadcast_to(summed, grouped.shape).reshape(value.shape)


def group_moments(sums, counts):
    sums = group_sum(narrow_sum(sums)) / counts[0]
    center = sums[0]
    spread = sums[1] - center * center
    return center, lax.rsqrt(spread + EPS_GROUP)


def group_means(sums, gain, counts, extras=()):
    sums = narrow_sum(jnp.concatenate([sums] + [row[None] for row in extras], axis=0))
    means = group_sum(sums[:2] * gain) / counts[0]
    return means, sums


def layer_norm(field_in, gain):
    center = jnp.mean(field_in, axis=-1, keepdims=True)
    spread = jnp.mean(jnp.square(field_in - center), axis=-1, keepdims=True)
    return (field_in - center) * lax.rsqrt(spread + EPS_LAYER) * gain


def head_rows(block, head):
    row = lax.broadcasted_iota(jnp.int32, block.shape, 0)
    inside = (row >= head * HEAD_DIM) & (row < (head + 1) * HEAD_DIM)
    return jnp.where(inside, block, jnp.zeros_like(block))


def head_lanes(block, head):
    lane = lax.broadcasted_iota(jnp.int32, block.shape, 1)
    inside = (lane >= head * HEAD_DIM) & (lane < (head + 1) * HEAD_DIM)
    return jnp.where(inside, block, jnp.zeros_like(block))


def mask_rows():
    row = lax.broadcasted_iota(jnp.int32, (TILE, QB), 0)
    return jnp.where(row == 0, 1.0, 0.0).astype(bf16)


def attend_kernel(first, last, parts, *refs):
    qt_ref = refs[0]
    key_refs = refs[1 : 1 + parts]
    value_refs = refs[1 + parts : 1 + 2 * parts]
    aug_ref = refs[1 + 2 * parts]
    rest = refs[2 + 2 * parts :]
    if not first:
        peak_in, acc_in = rest[:2]
        rest = rest[2:]
    if last:
        heads_ref, log_ref = rest
    else:
        peak_ref, acc_ref = rest
    keys = jnp.concatenate([ref[...] for ref in key_refs], axis=0)
    keys = jnp.concatenate([keys, aug_ref[...]], axis=1)
    values = jnp.concatenate([ref[...] for ref in value_refs], axis=0)
    value_t = jnp.transpose(values, (1, 0))
    ones = jnp.ones((ONES, value_t.shape[1]), bf16)
    low_rows = mask_rows()

    head_of = lambda shape, axis: lax.broadcasted_iota(jnp.int32, shape, axis) // HEAD_DIM
    pick = jnp.where(head_of((TILE, TILE), 0) == head_of((TILE, TILE), 1), 1.0, 0.0).astype(bf16)
    all_keys = keys[:, :TILE]
    key_norms = jnp.dot(all_keys * all_keys, pick, preferred_element_type=f32)
    all_queries = qt_ref[...]
    query_norms = jnp.dot(pick, all_queries * all_queries, preferred_element_type=f32)
    reach = jnp.float32(0.0)
    for head in range(PER_TILE):
        rows = slice(head * HEAD_DIM, head * HEAD_DIM + 8)
        mine = head_of(key_norms.shape, 1) == head
        key_peak = jnp.max(jnp.where(mine, key_norms, 0.0))
        reach = jnp.maximum(reach, key_peak * jnp.max(query_norms[rows]))

    def make_step(shifted):
        def block_step(step, carry):
            cols = pl.ds(pl.multiple_of(step * QB, QB), QB)
            qt = qt_ref[:, cols]
            for head in range(PER_TILE):
                rows = slice(head * HEAD_DIM, (head + 1) * HEAD_DIM)
                query = jnp.concatenate([head_rows(qt, head), low_rows], axis=0)
                scores = jnp.dot(keys, query, preferred_element_type=f32)
                if shifted:
                    peak = jnp.max(scores, axis=0, keepdims=True)
                    probs = jnp.exp2(scores - peak).astype(bf16)
                else:
                    peak = jnp.zeros((1, QB), f32)
                    probs = jnp.exp2(scores).astype(bf16)
                value_h = jnp.concatenate([value_t[rows], ones], axis=0)
                acc = jnp.dot(value_h, probs, preferred_element_type=f32)
                if not first:
                    peak_old = peak_in[head, 0:1, cols]
                    peak_new = jnp.maximum(peak, peak_old)
                    acc = acc * jnp.exp2(peak - peak_new)
                    acc = acc + acc_in[head, :, cols] * jnp.exp2(peak_old - peak_new)
                    peak = peak_new
                if last:
                    total = acc[HEAD_DIM : HEAD_DIM + 1]
                    heads_ref[rows, cols] = acc[:HEAD_DIM] / total
                    log_ref[head, :, cols] = jnp.broadcast_to(peak + jnp.log2(total), (8, QB))
                else:
                    acc_ref[head, :, cols] = acc
                    peak_ref[head, :, cols] = jnp.broadcast_to(peak, (8, QB))
            return carry

        return block_step

    steps = qt_ref.shape[1] // QB

    @pl.when(reach < SAFE_REACH * SAFE_REACH)
    def _():
        lax.fori_loop(0, steps, make_step(False), 0)

    @pl.when(jnp.logical_not(reach < SAFE_REACH * SAFE_REACH))
    def _():
        lax.fori_loop(0, steps, make_step(True), 0)


def chunk_specs(count, tiles, parts):
    key_spec = pl.BlockSpec((count, TILE), lambda t: (0, t))
    value_spec = pl.BlockSpec((count, TILE), lambda t: (0, tiles + t))
    aug_spec = pl.BlockSpec((parts * count, TILE), lambda t: (0, 0))
    return [key_spec] * parts + [value_spec] * parts + [aug_spec]


def attend_some(first, last, query_t, chunks, aug, state):
    channels, queries = query_t.shape
    count = chunks[0].shape[0]
    heads = channels // HEAD_DIM
    tiles = channels // TILE
    t_spec = pl.BlockSpec((TILE, queries), lambda t: (t, 0))
    cube = lambda t: (t, 0, 0)
    row_spec = pl.BlockSpec((PER_TILE, 8, queries), cube)
    acc_spec = pl.BlockSpec((PER_TILE, HEAD_DIM + ONES, queries), cube)
    in_specs = [t_spec] + chunk_specs(count, tiles, len(chunks))
    if not first:
        in_specs += [row_spec, acc_spec]
    row_shape = jax.ShapeDtypeStruct((heads, 8, queries), f32)
    if last:
        out_shape = (jax.ShapeDtypeStruct((channels, queries), f32), row_shape)
        out_specs = (t_spec, row_spec)
    else:
        out_shape = (
            row_shape,
            jax.ShapeDtypeStruct((heads, HEAD_DIM + ONES, queries), f32),
        )
        out_specs = (row_spec, acc_spec)
    return pl.pallas_call(
        functools.partial(attend_kernel, first, last, len(chunks)),
        grid=(tiles,),
        in_specs=in_specs,
        out_specs=out_specs,
        out_shape=out_shape,
        compiler_params=pltpu.CompilerParams(vmem_limit_bytes=58 << 20),
        cost_estimate=pl.CostEstimate(
            flops=32 * len(chunks) * channels * queries * count,
            bytes_accessed=8 * channels * (queries + count),
            transcendentals=len(chunks) * heads * queries * count,
        ),
        name="attend",
    )(query_t, *chunks, *chunks, aug, *state)


def attend_back_kernel(first, parts, *refs):
    qt_ref, q_ref, dt_ref, d_ref, log_ref, heads_ref = refs[:6]
    key_refs = refs[6 : 6 + parts]
    value_refs = refs[6 + parts : 6 + 2 * parts]
    aug_ref = refs[6 + 2 * parts]
    refs = refs[7 + 2 * parts :]
    if not first:
        dq_in = refs[0]
        refs = refs[1:]
    dq_ref = refs[0]
    out_refs = refs[1 : 1 + parts]
    dk_acc, dv_acc = refs[1 + parts :]
    count = key_refs[0].shape[0]
    k_tile = jnp.concatenate([ref[...] for ref in key_refs], axis=0)
    keys = jnp.concatenate([k_tile, aug_ref[...]], axis=1)
    values = jnp.concatenate([ref[...] for ref in value_refs], axis=0)
    key_t = jnp.transpose(k_tile, (1, 0))
    low_rows = mask_rows()
    dk_acc[...] = jnp.zeros_like(dk_acc)
    dv_acc[...] = jnp.zeros_like(dv_acc)
    factor = 1.0 / math.sqrt(HEAD_DIM)

    def block_step(step, carry):
        cols = pl.ds(pl.multiple_of(step * QB, QB), QB)
        qt = qt_ref[:, cols]
        dt = dt_ref[:, cols]
        q_blk = q_ref[cols, :]
        d_blk = d_ref[cols, :]
        probs_all, grads_all, q_all, d_all = [], [], [], []
        for head in range(PER_TILE):
            rows = slice(head * HEAD_DIM, (head + 1) * HEAD_DIM)
            query = jnp.concatenate([head_rows(qt, head), low_rows], axis=0)
            scores = jnp.dot(keys, query, preferred_element_type=f32)
            probs = jnp.exp2(scores - log_ref[head, 0:1, cols])
            weighted = jnp.sum(
                heads_ref[rows, cols] * dt[rows].astype(f32), axis=0, keepdims=True
            )
            grad_p = jnp.dot(values, head_rows(dt, head), preferred_element_type=f32)
            grad_s = (probs * (grad_p - weighted)).astype(bf16)
            probs_all.append(probs.astype(bf16))
            grads_all.append(grad_s)
            q_all.append(head_lanes(q_blk, head))
            d_all.append(head_lanes(d_blk, head))
            dq = jnp.dot(key_t[rows], grad_s, preferred_element_type=f32) * factor
            if not first:
                dq = dq + dq_in[rows, cols]
            dq_ref[rows, cols] = dq
        dv_acc[...] += jnp.dot(
            jnp.concatenate(probs_all, axis=1),
            jnp.concatenate(d_all, axis=0),
            preferred_element_type=f32,
        )
        dk_acc[...] += jnp.dot(
            jnp.concatenate(grads_all, axis=1),
            jnp.concatenate(q_all, axis=0),
            preferred_element_type=f32,
        )
        return carry

    lax.fori_loop(0, qt_ref.shape[1] // QB, block_step, 0)
    for index, ref in enumerate(out_refs):
        rows = slice(index * count, (index + 1) * count)
        ref[0] = (dk_acc[rows] * LN2).astype(ref.dtype)
        ref[1] = dv_acc[rows].astype(ref.dtype)


def attend_back_some(
    first, out_types, query_t, query, grad_t, grad, logs, heads_t, chunks, aug, dq
):
    channels, queries = query_t.shape
    count = chunks[0].shape[0]
    parts = len(chunks)
    tiles = channels // TILE
    t_spec = pl.BlockSpec((TILE, queries), lambda t: (t, 0))
    n_spec = pl.BlockSpec((queries, TILE), lambda t: (0, t))
    row_spec = pl.BlockSpec((PER_TILE, 8, queries), lambda t: (t, 0, 0))
    out_spec = pl.BlockSpec((2, count, TILE), lambda t: (0, 0, t))
    in_specs = [t_spec, n_spec, t_spec, n_spec, row_spec, t_spec] + chunk_specs(count, tiles, parts)
    state = ()
    if not first:
        in_specs.append(t_spec)
        state = (dq,)
    return pl.pallas_call(
        functools.partial(attend_back_kernel, first, parts),
        grid=(tiles,),
        in_specs=in_specs,
        out_specs=(t_spec,) + (out_spec,) * parts,
        out_shape=(jax.ShapeDtypeStruct((channels, queries), f32),)
        + tuple(jax.ShapeDtypeStruct((2, count, channels), kind) for kind in out_types),
        scratch_shapes=[pltpu.VMEM((parts * count, TILE), f32)] * 2,
        compiler_params=pltpu.CompilerParams(vmem_limit_bytes=58 << 20),
        cost_estimate=pl.CostEstimate(
            flops=80 * parts * channels * queries * count,
            bytes_accessed=12 * channels * (queries + count),
            transcendentals=parts * channels // HEAD_DIM * queries * count,
        ),
        name="attend_back",
    )(query_t, query, grad_t, grad, logs, heads_t, *chunks, *chunks, aug, *state)


def swap(value, bit, axis="narrow"):
    count = lax.axis_size(axis)
    return lax.ppermute(value, axis, [(i, i ^ bit) for i in range(count)])


def low_bit(index):
    return index & -index


def axis_bits(axis):
    return [1 << level for level in range(lax.axis_size(axis).bit_length() - 1)]


def my_bit(bit, axis="narrow"):
    return (lax.axis_index(axis) // bit) % 2


def narrow_sum(value):
    for bit in axis_bits("narrow"):
        value = value + swap(value, bit)
    return value


def key_aug(keep_chunk):
    lane = lax.broadcasted_iota(jnp.int32, (keep_chunk.shape[0], TILE), 1)
    bias = jnp.where(keep_chunk[:, None] > 0, 0.0, MASKED)
    return jnp.where(lane == 0, bias, 0.0).astype(bf16)


def halve_step(held, bit, axis):
    halves = held.reshape((held.shape[0] // 2, 2) + held.shape[1:])
    mine = my_bit(bit, axis)
    kept = lax.dynamic_index_in_dim(halves, mine, 1, keepdims=False)
    sent = lax.dynamic_index_in_dim(halves, 1 - mine, 1, keepdims=False)
    return (kept.astype(f32) + swap(sent, bit, axis).astype(f32)).astype(bf16)


def halve(held, axis):
    for bit in axis_bits(axis):
        held = halve_step(held, bit, axis)
    return held[0]


def double(value, axis):
    whole = value[None]
    for bit in reversed(axis_bits(axis)):
        other = swap(whole, bit, axis)
        pair = jnp.where(
            my_bit(bit, axis) == 0,
            jnp.stack([whole, other], axis=1),
            jnp.stack([other, whole], axis=1),
        )
        whole = pair.reshape((-1,) + value.shape)
    return whole


def wide_finish(share):
    wide = lax.axis_size("wide")
    count = lax.axis_size("narrow")
    spot = lax.axis_index("narrow")
    share = halve(share.reshape(wide, share.shape[0] // wide, share.shape[1]), "wide")
    near = jnp.stack([share] + [swap(share, index) for index in range(1, count)])
    pick = lambda index: lax.dynamic_index_in_dim(near, spot ^ index, 0, keepdims=False)
    return jnp.stack([pick(index) for index in range(count)])


def conv_finish(whole, rows):
    return jnp.transpose(whole, (0, 2, 1)).reshape(-1, whole.shape[1])[:rows].astype(f32)


def by_owner(grad_t, width):
    wide = lax.axis_size("wide")
    groups = grad_t.shape[0] // wide // width
    split = grad_t.reshape(wide, groups, width, grad_t.shape[1])
    return jnp.transpose(split, (0, 2, 1, 3)).reshape(wide * width, -1)


def narrow_finish(share):
    share = share.astype(bf16)
    for bit in axis_bits("narrow"):
        share = (share.astype(f32) + swap(share, bit).astype(f32)).astype(bf16)
    return share.astype(f32)


def own_columns(value):
    width = value.shape[-1] // lax.axis_size("wide")
    start = lax.axis_index("wide") * width
    return lax.dynamic_slice_in_dim(value, start, width, value.ndim - 1)


CONV_LIMIT = 50 << 20
NT = (((1,), (1,)), ((), ()))


def lanes_of(meta_ref, index, start, count, channels):
    return jnp.concatenate([meta_ref[index, start : start + count]] * (channels // TILE), axis=1)


def store_shifts(field, meta_ref, stack_ref):
    total, channels = field.shape
    low = jnp.where(
        lanes_of(meta_ref, 1, 0, total, channels) > 0, pltpu.roll(field, 1, 0), 0.0
    )
    high = jnp.where(
        lanes_of(meta_ref, 2, 0, total, channels) > 0, pltpu.roll(field, total - 1, 0), 0.0
    )
    stack_ref[:, :channels] = low.astype(bf16)
    stack_ref[:, channels : 2 * channels] = field.astype(bf16)
    stack_ref[:, 2 * channels :] = high.astype(bf16)


def with_halo(low_ref, own_ref, high_ref):
    parts = [low_ref[...].astype(f32), own_ref[...].astype(f32), high_ref[...].astype(f32)]
    return jnp.concatenate(parts, axis=0)


def conv_kernel(width_ref, x_ref, low_ref, high_ref, meta_ref, rows_ref, w_ref, add_ref, y_ref, sum_ref, stack_ref):
    local, channels = x_ref.shape
    total = stack_ref.shape[0]
    width = width_ref[0]
    field = with_halo(low_ref, x_ref, high_ref)
    keep = lanes_of(meta_ref, 0, 0, total, channels)
    pre = keep * (field - rows_ref[0:1]) * (rows_ref[1:2] * rows_ref[2:3])
    store_shifts(pre / (1.0 + jnp.exp(-pre)), meta_ref, stack_ref)
    block = local // 2
    sum_ref[...] = jnp.zeros_like(sum_ref)

    def block_step(step, carry):
        start = step * block
        taps = []
        for shift in (-1, 0, 1):
            offset = pl.multiple_of(LONG + start + shift * width, 16)
            taps.append(stack_ref[pl.ds(offset, block), :])
        out = jnp.dot(jnp.concatenate(taps, axis=1), w_ref[...], preferred_element_type=f32)
        own = pl.ds(pl.multiple_of(start, 16), block)
        if add_ref.shape[0] == local:
            out = out + add_ref[own, :].astype(f32)
        else:
            out = out + add_ref[0:1]
        y_ref[own, :] = out
        kept = meta_ref[0, pl.ds(pl.multiple_of(LONG + start, 16), block), :]
        kept = out * jnp.concatenate([kept] * (channels // TILE), axis=1)
        sum_ref[0:1] += jnp.sum(kept, axis=0, keepdims=True)
        sum_ref[1:2] += jnp.sum(kept * out, axis=0, keepdims=True)
        return carry

    lax.fori_loop(0, 2, block_step, 0)


def conv_forward(width, field, halo, meta, rows, weight, add):
    local, channels = field.shape
    vmem = pl.BlockSpec(memory_space=pltpu.VMEM)
    return pl.pallas_call(
        conv_kernel,
        in_specs=[pl.BlockSpec(memory_space=pltpu.SMEM)] + [vmem] * 7,
        out_specs=(vmem, vmem),
        out_shape=(
            jax.ShapeDtypeStruct((local, channels), f32),
            jax.ShapeDtypeStruct((8, channels), f32),
        ),
        scratch_shapes=[pltpu.VMEM((local + 2 * LONG, 3 * channels), bf16)],
        compiler_params=pltpu.CompilerParams(vmem_limit_bytes=CONV_LIMIT),
        cost_estimate=pl.CostEstimate(
            flops=2 * local * weight.size,
            bytes_accessed=4 * weight.size,
            transcendentals=2 * local * channels,
        ),
        name="conv_forward",
    )(width, field, halo[0], halo[1], meta, rows, weight, add)


def conv_build(with_skip, refs, meta_ref, rows_ref, stack_ref):
    d_ref, d_low, d_high, v_ref, v_low, v_high = refs[:6]
    local, channels = d_ref.shape
    total = stack_ref.shape[0]
    keep = lanes_of(meta_ref, 0, 0, total, channels)
    normed = (with_halo(v_low, v_ref, v_high) - rows_ref[0:1]) * rows_ref[1:2]
    inner = with_halo(d_low, d_ref, d_high) * keep * rows_ref[2:3] - rows_ref[3:4]
    field = keep * rows_ref[1:2] * (inner - normed * rows_ref[4:5])
    if with_skip:
        c_ref, c_low, c_high = refs[6:9]
        field = field + with_halo(c_low, c_ref, c_high)
    store_shifts(field, meta_ref, stack_ref)
    return field[LONG : LONG + local]


def conv_pull(width, x_ref, meta_ref, rows_ref, w_ref, stack_ref, pre_ref, sum_ref):
    local, channels = x_ref.shape
    block = local // 2

    def block_step(step, carry):
        start = step * block
        own = pl.ds(pl.multiple_of(start, 16), block)
        out = jnp.zeros((block, channels), f32)
        for row in range(3):
            offset = pl.multiple_of(LONG + start + (row - 1) * width, 16)
            for col in range(3):
                tap = 8 - (3 * row + col)
                out = out + lax.dot_general(
                    stack_ref[pl.ds(offset, block), col * channels : (col + 1) * channels],
                    w_ref[tap * channels : (tap + 1) * channels, :],
                    NT,
                    preferred_element_type=f32,
                )
        kept = meta_ref[0, pl.ds(pl.multiple_of(LONG + start, 16), block), :]
        kept = jnp.concatenate([kept] * (channels // TILE), axis=1)
        xhat = (x_ref[own, :].astype(f32) - rows_ref[5:6]) * rows_ref[6:7]
        pre = kept * xhat * rows_ref[7:8]
        gate = 1.0 / (1.0 + jnp.exp(-pre))
        grad = out * (gate * (1.0 + pre * (1.0 - gate)))
        pre_ref[own, :] = grad
        grad = grad * kept
        sum_ref[0:1] += jnp.sum(grad, axis=0, keepdims=True)
        sum_ref[1:2] += jnp.sum(grad * xhat, axis=0, keepdims=True)
        return carry

    lax.fori_loop(0, 2, block_step, 0)


def conv_weight(width, x_ref, meta_ref, rows_ref, stack_ref, pack_ref, extra_ref):
    local, channels = x_ref.shape
    kept = lanes_of(meta_ref, 0, LONG, local, channels)
    pre = kept * (x_ref[...].astype(f32) - rows_ref[5:6]) * (rows_ref[6:7] * rows_ref[7:8])
    act_t = jnp.transpose((pre / (1.0 + jnp.exp(-pre))).astype(bf16), (1, 0))
    extra = 0 if extra_ref is None else extra_ref.shape[2]
    groups = (pack_ref.shape[2] - extra) // TILE
    tiles = channels // TILE
    for row in range(3):
        offset = pl.multiple_of(LONG + (row - 1) * width, 16)
        for col in range(3):
            tap = 8 - (3 * row + col)
            grad = jnp.dot(
                act_t,
                stack_ref[pl.ds(offset, local), col * channels : (col + 1) * channels],
                preferred_element_type=f32,
            )
            grad = jnp.transpose(grad.astype(bf16), (1, 0))
            for tile in range(tiles):
                spot = tap * tiles + tile
                lane = (spot % groups) * TILE
                pack_ref[spot // groups, :, lane : lane + TILE] = grad[
                    :, tile * TILE : (tile + 1) * TILE
                ]
    for spot in range(9 * tiles, pack_ref.shape[0] * groups):
        lane = (spot % groups) * TILE
        pack_ref[spot // groups, :, lane : lane + TILE] = jnp.zeros((channels, TILE), bf16)
    if extra:
        pack_ref[:, :, groups * TILE :] = extra_ref[...]


def pull_first_kernel(width_ref, *refs):
    x_ref, meta_ref, rows_ref, w_ref, e_ref, stack_ref, pre_ref, sum_ref = refs[9:]
    e_ref[...] = conv_build(True, refs, meta_ref, rows_ref, stack_ref)
    sum_ref[...] = jnp.zeros_like(sum_ref)
    conv_pull(width_ref[0], x_ref, meta_ref, rows_ref, w_ref, stack_ref, pre_ref, sum_ref)


def weight_after_kernel(width_ref, stack_ref, x_ref, meta_ref, rows_ref, extra_ref, pack_ref):
    conv_weight(width_ref[0], x_ref, meta_ref, rows_ref, stack_ref, pack_ref, extra_ref)


def weight_first_kernel(width_ref, *refs):
    x_ref, meta_ref, rows_ref, stack_ref, pack_ref, sum_ref = refs[6:]
    field = conv_build(False, refs, meta_ref, rows_ref, stack_ref)
    sum_ref[...] = jnp.broadcast_to(jnp.sum(field, axis=0, keepdims=True), sum_ref.shape)
    conv_weight(width_ref[0], x_ref, meta_ref, rows_ref, stack_ref, pack_ref, None)


def pull_after_kernel(width_ref, stack_ref, x_ref, meta_ref, rows_ref, w_ref, pre_ref, sum_ref):
    sum_ref[...] = jnp.zeros_like(sum_ref)
    conv_pull(width_ref[0], x_ref, meta_ref, rows_ref, w_ref, stack_ref, pre_ref, sum_ref)


def conv_call(kernel, name, width, operands, shapes, flops):
    vmem = pl.BlockSpec(memory_space=pltpu.VMEM)
    return pl.pallas_call(
        kernel,
        in_specs=[pl.BlockSpec(memory_space=pltpu.SMEM)] + [vmem] * len(operands),
        out_specs=(vmem,) * len(shapes),
        out_shape=tuple(jax.ShapeDtypeStruct(shape, kind) for shape, kind in shapes),
        compiler_params=pltpu.CompilerParams(vmem_limit_bytes=CONV_LIMIT),
        cost_estimate=pl.CostEstimate(flops=flops, bytes_accessed=1 << 24, transcendentals=0),
        name=name,
    )(width, *operands)


def pack_width(weight):
    count = lax.axis_size("narrow")
    return (weight.shape[0] + (-weight.shape[0] % (count * TILE))) // count


def edge_rows(*fields):
    count = lax.axis_size("narrow")
    forward = [(i, i + 1) for i in range(count - 1)]
    backward = [(i + 1, i) for i in range(count - 1)]
    tails = jnp.concatenate([field[-LONG:] for field in fields], axis=0)
    heads = jnp.concatenate([field[:LONG] for field in fields], axis=0)
    low = lax.ppermute(tails, "narrow", forward)
    high = lax.ppermute(heads, "narrow", backward)
    cut = lambda rim, index: rim[index * LONG : (index + 1) * LONG]
    return [(cut(low, index), cut(high, index)) for index in range(len(fields))]


def pixel_meta(keep_image, row_start, local, row_width):
    rim = jnp.pad(keep_image, (LONG, LONG))
    keep = lax.dynamic_slice_in_dim(rim, row_start, local + 2 * LONG, 0)
    spot = jnp.arange(local + 2 * LONG, dtype=jnp.int32)
    column = (spot + 2 * LONG * SHORT - LONG) % row_width
    rows = jnp.stack([keep, (column > 0).astype(f32), (column < row_width - 1).astype(f32)])
    return jnp.broadcast_to(rows[:, :, None], rows.shape + (TILE,))


def row_table(*rows):
    table = jnp.stack([jnp.broadcast_to(row.reshape(-1), rows[0].reshape(-1).shape) for row in rows])
    return jnp.pad(table, ((0, 8 - len(rows)), (0, 0)))


MID_BLOCKS = 4


def dot_nt(left, right):
    return lax.dot_general(left, right, NT, preferred_element_type=f32)


def mid_kernel(
    owned,
    heads_ref,
    stream_ref,
    residual_ref,
    cot_ref,
    row_ref,
    attn_out_ref,
    geglu_in_ref,
    geglu_out_ref,
    proj_out_ref,
    out_ref,
    grad_mid_ref,
    grad_ref,
    grad_t_ref,
    top_ref,
    gate_ref,
    sum_ref,
    heads_low,
    normed_low,
    mixed_low,
    end_low,
    ffo_low,
    gates_low,
    mid_low,
):
    local, channels = stream_ref.shape
    hidden = geglu_out_ref.shape[0]
    block = local // MID_BLOCKS
    heads_low[...] = jnp.transpose(heads_ref[...].astype(bf16), (1, 0))[:local]
    sum_ref[...] = jnp.zeros_like(sum_ref)

    def block_step(step, carry):
        own = pl.ds(pl.multiple_of(step * block, 16), block)
        mid = stream_ref[own, :] + row_ref[0:1]
        mid = mid + jnp.dot(heads_low[own, :], attn_out_ref[...], preferred_element_type=f32)
        center = jnp.mean(mid, axis=1, keepdims=True)
        inv_std = lax.rsqrt(jnp.mean(jnp.square(mid - center), axis=1, keepdims=True) + EPS_LAYER)
        xhat = (mid - center) * inv_std
        normed = (xhat * row_ref[1:2]).astype(bf16)
        normed_low[own, :] = normed
        gates = jnp.dot(normed, geglu_in_ref[...], preferred_element_type=f32)
        value, gate = gates[:, :hidden], gates[:, hidden:]
        half = 0.5 * (1.0 + lax.erf(gate * math.sqrt(0.5)))
        gelu = gate * half
        slope = half + gate * jnp.exp(-0.5 * gate * gate) * (1.0 / math.sqrt(2.0 * math.pi))
        mixed = (value * gelu).astype(bf16)
        mixed_low[own, :] = mixed
        end = mid + jnp.dot(mixed, geglu_out_ref[...], preferred_element_type=f32)
        end = end.astype(bf16)
        end_low[own, :] = end
        out = residual_ref[own, :] + jnp.dot(end, proj_out_ref[...], preferred_element_type=f32)
        out_ref[own, :] = out.astype(bf16)
        grad_end = dot_nt(cot_ref[own, :], proj_out_ref[...])
        grad_ffo = grad_end.astype(bf16)
        ffo_low[own, :] = grad_ffo
        grad_mixed = dot_nt(grad_ffo, geglu_out_ref[...])
        grad_gates = jnp.concatenate(
            [(grad_mixed * gelu).astype(bf16), (grad_mixed * value * slope).astype(bf16)], axis=1
        )
        gates_low[own, :] = grad_gates
        grad_normed = dot_nt(grad_gates, geglu_in_ref[...])
        grad_hat = grad_normed * row_ref[1:2]
        mean_one = jnp.mean(grad_hat, axis=1, keepdims=True)
        mean_two = jnp.mean(grad_hat * xhat, axis=1, keepdims=True)
        grad_mid = grad_end + inv_std * (grad_hat - mean_one - xhat * mean_two)
        grad_mid_ref[own, :] = grad_mid
        sum_ref[0:1] += jnp.sum(grad_mid, axis=0, keepdims=True)
        sum_ref[1:2] += jnp.sum(grad_normed * xhat, axis=0, keepdims=True)
        grad_mid = grad_mid.astype(bf16)
        mid_low[own, :] = grad_mid
        grad_ref[own, :] = dot_nt(grad_mid, attn_out_ref[...]).astype(bf16)
        return carry

    lax.fori_loop(0, MID_BLOCKS, block_step, 0)
    pad = grad_ref.shape[0] - local
    if pad:
        grad_ref[local:, :] = jnp.zeros((pad, channels), bf16)
    grad_t_ref[...] = jnp.transpose(grad_ref[...], (1, 0))

    def put(index, grad):
        if owned:
            for owner in range(channels // owned):
                rows = grad[owner * owned : (owner + 1) * owned]
                top_ref[owner, index * owned : (index + 1) * owned, :] = rows
        else:
            top_ref[:, index * channels : (index + 1) * channels] = grad

    put(
        0,
        jnp.dot(
            jnp.transpose(cot_ref[...], (1, 0)), end_low[...], preferred_element_type=f32
        ),
    )
    put(
        1,
        jnp.dot(
            jnp.transpose(mid_low[...], (1, 0)), heads_low[...], preferred_element_type=f32
        ),
    )
    ffo_t = jnp.transpose(ffo_low[...], (1, 0))
    pieces = hidden // channels
    for piece in range(pieces):
        mixed = mixed_low[:, piece * channels : (piece + 1) * channels]
        put(2 + piece, jnp.dot(ffo_t, mixed, preferred_element_type=f32))
    normed_t = jnp.transpose(normed_low[...], (1, 0))
    for piece in range(2 * pieces):
        grads = gates_low[:, piece * channels : (piece + 1) * channels]
        grad = jnp.dot(normed_t, grads, preferred_element_type=f32)
        if owned:
            top_ref[piece, (2 + pieces) * owned :, :] = grad
        else:
            gate_ref[:, piece * channels : (piece + 1) * channels] = grad


def mid_layer(heads_t, stream, residual, cotangent, rows, attn_out, geglu_in, geglu_out, proj_out):
    local, channels = stream.shape
    queries = heads_t.shape[1]
    hidden = geglu_out.shape[0]
    wide = lax.axis_size("wide")
    pieces = 2 + hidden // channels
    aligned = 2 * hidden == wide * channels
    owned = channels // wide if aligned else 0
    if aligned:
        top_shape = jax.ShapeDtypeStruct((wide, pieces * owned + channels, channels), f32)
        gate_shape = jax.ShapeDtypeStruct((8, channels), f32)
    else:
        top_shape = jax.ShapeDtypeStruct((channels, pieces * channels), f32)
        gate_shape = jax.ShapeDtypeStruct((channels, 2 * hidden), f32)
    vmem = pl.BlockSpec(memory_space=pltpu.VMEM)
    low = lambda width: pltpu.VMEM((local, width), bf16)
    return pl.pallas_call(
        functools.partial(mid_kernel, owned),
        in_specs=[vmem] * 9,
        out_specs=(vmem,) * 7,
        out_shape=(
            jax.ShapeDtypeStruct((local, channels), bf16),
            jax.ShapeDtypeStruct((local, channels), f32),
            jax.ShapeDtypeStruct((queries, channels), bf16),
            jax.ShapeDtypeStruct((channels, queries), bf16),
            top_shape,
            gate_shape,
            jax.ShapeDtypeStruct((8, channels), f32),
        ),
        scratch_shapes=[
            low(channels),
            low(channels),
            low(hidden),
            low(channels),
            low(channels),
            low(2 * hidden),
            low(channels),
        ],
        compiler_params=pltpu.CompilerParams(vmem_limit_bytes=57 << 20),
        cost_estimate=pl.CostEstimate(
            flops=6 * local * channels * (3 * hidden + 2 * channels),
            bytes_accessed=24 * channels * hidden,
            transcendentals=2 * local * hidden,
        ),
        name="mid_layer",
    )(heads_t, stream, residual, cotangent, rows, attn_out, geglu_in, geglu_out, proj_out)


def top_shares(top, gates):
    wide = lax.axis_size("wide")
    if top.ndim == 3:
        share = lax.psum_scatter(top, "wide", scatter_dimension=0, tiled=True)[0]
        return (share,)
    channels = top.shape[0]
    split = top.reshape(wide, channels // wide, -1, channels)
    split = jnp.transpose(split, (0, 2, 1, 3)).reshape(wide, -1, channels)
    share = lax.psum_scatter(split, "wide", scatter_dimension=0, tiled=True)[0]
    gates = jnp.transpose(gates.reshape(channels, wide, -1), (1, 0, 2))
    return share, lax.psum_scatter(gates, "wide", scatter_dimension=0, tiled=True)[0]


def split_top(shares, owned, channels):
    if len(shares) == 1:
        count = shares[0].shape[0] - channels
        gates = shares[0][count:]
    else:
        count = shares[0].shape[0]
        gates = shares[1]
    pieces = shares[0][:count].reshape(-1, owned, channels)
    pieces = jnp.transpose(pieces, (0, 2, 1))
    return pieces[0], pieces[1], pieces[2:].reshape(-1, owned), gates


def per_device(
    latents,
    cotangent,
    bucket,
    pixel_mask,
    labels,
    timesteps,
    gain_first,
    conv_first,
    time_proj,
    gain_second,
    conv_second,
    gain_spatial,
    proj_in,
    gain_attn,
    attn_qkv,
    attn_out,
    class_table,
    cross_value,
    cross_out,
    gain_ff,
    geglu_in,
    geglu_out,
    proj_out,
):
    images, local_pix, channels = latents.shape
    row_start = lax.axis_index("narrow") * local_pix
    keep_all = pixel_mask.astype(jnp.float32)
    pixel_keep = lax.dynamic_slice_in_dim(keep_all, row_start, local_pix, 1)[0, :, None]
    counts = jnp.sum(keep_all, axis=1) * (channels // GROUPS)
    row_width = jnp.where(bucket[0] == 0, LONG, SHORT).astype(jnp.int32)
    width = row_width[None]
    meta = pixel_meta(keep_all[0], row_start, local_pix, row_width)
    pixels = latents[0]
    skip = cotangent[0]
    pixel_halo, skip_halo = edge_rows(pixels, skip)
    half_dim = time_proj.shape[0] // 2
    frequency = jnp.exp(-math.log(10000.0) * jnp.arange(half_dim, dtype=jnp.float32) / half_dim)
    angles = timesteps.astype(jnp.float32)[:, None] * frequency[None, :]
    time_act = jax.nn.silu(jnp.concatenate([jnp.cos(angles), jnp.sin(angles)], axis=1))
    time_term = jnp.dot(time_act, time_proj.astype(jnp.float32), precision=HIGH)
    label_hot = (
        labels[:, None] == jnp.arange(class_table.shape[0], dtype=jnp.int32)[None, :]
    ).astype(jnp.float32)
    context = jnp.dot(label_hot, class_table.astype(jnp.float32), precision=HIGH)
    value_weight = cross_value.astype(jnp.float32)
    cross_weight = cross_out.astype(jnp.float32)
    value_term = jnp.dot(context, value_weight, precision=HIGH)
    cross_term = jnp.dot(value_term, cross_weight, precision=HIGH)
    gain_one = gain_first.astype(jnp.float32)
    gain_two = gain_second.astype(jnp.float32)
    gain_three = gain_spatial.astype(jnp.float32)
    image_in = pixels.astype(jnp.float32)
    kept = image_in * pixel_keep
    sums_one = jnp.stack([jnp.sum(kept, axis=0), jnp.sum(kept * image_in, axis=0)])
    center_one, scale_one = group_moments(sums_one, counts)
    hidden, sums_two = conv_forward(
        width,
        pixels,
        pixel_halo,
        meta,
        row_table(center_one, scale_one, gain_one),
        conv_first,
        row_table(time_term[0]),
    )
    (hidden_halo,) = edge_rows(hidden)
    center_two, scale_two = group_moments(sums_two[:2], counts)
    residual, sums_three = conv_forward(
        width,
        hidden,
        hidden_halo,
        meta,
        row_table(center_two, scale_two, gain_two),
        conv_second,
        pixels,
    )
    center_three, scale_three = group_moments(sums_three[:2], counts)
    residual_hat = (residual - center_three) * scale_three
    spatial = (pixel_keep * residual_hat * gain_three).astype(jnp.bfloat16)[None]
    stream = jnp.einsum("npc,cd->npd", spatial, proj_in, preferred_element_type=jnp.float32)
    normed_attn, attn_pull = jax.vjp(layer_norm, stream, gain_attn.astype(jnp.float32))
    normed_attn = normed_attn.astype(jnp.bfloat16)
    packed_f = jnp.einsum("npc,cd->npd", normed_attn, attn_qkv, preferred_element_type=jnp.float32)
    query_pix = (packed_f[0, :, :channels] * (1.0 / (math.sqrt(HEAD_DIM) * LN2))).astype(bf16)
    pad_pix = -local_pix % QB
    query_pix = jnp.pad(query_pix, ((0, pad_pix), (0, 0)))
    query_t = query_pix.T
    key_value = packed_f[0, :, channels:].astype(bf16)
    count = lax.axis_size("narrow")
    position = lax.axis_index("narrow")
    chunks = [key_value] + [None] * (count - 1)
    for bit in axis_bits("narrow"):
        chunks[bit] = swap(key_value, bit)
    keep_chunk = lambda index: lax.dynamic_slice_in_dim(
        keep_all[0], (position ^ index) * local_pix, local_pix, 0
    )
    keeps = [keep_chunk(index) for index in range(count)]
    aug_of = lambda indices: key_aug(jnp.concatenate([keeps[index] for index in indices]))
    state = attend_some(True, count == 2, query_t, chunks[:2], aug_of([0, 1]), ())
    for index in range(2, count):
        bit = low_bit(index)
        if index != bit:
            chunks[index] = swap(chunks[index ^ bit], bit)
        elif index < count - 1:
            chunks[index], state = lax.optimization_barrier((chunks[index], state))
    for index in range(2, count):
        state = attend_some(
            False, index == count - 1, query_t, [chunks[index]], aug_of([index]), state
        )
    heads_t, log_rows = state
    output, grad_mid, grad_rows, grad_t, top_grads, gate_grads, mid_sums = mid_layer(
        heads_t,
        stream[0],
        residual,
        skip,
        row_table(cross_term[0], gain_ff.astype(jnp.float32)),
        attn_out,
        geglu_in,
        geglu_out,
        proj_out,
    )
    owned = channels // lax.axis_size("wide")
    shares = top_shares(top_grads, gate_grads)
    grad_query_t = None
    totals = [None] * count
    arrived = [None] * count
    calls = [[count - 1]] + [[last - 1, last] for last in range(count - 2, 0, -2)] + [[0]]
    for call in calls:
        grad_query_t, *parts = attend_back_some(
            call[0] == count - 1,
            [bf16 if index % 2 else f32 for index in call],
            query_t,
            query_pix,
            grad_t,
            grad_rows,
            log_rows,
            heads_t,
            [chunks[index] for index in call],
            aug_of(call),
            grad_query_t,
        )
        for index, total in zip(call, parts):
            for source in range(index + 1, count):
                if source ^ low_bit(source) == index:
                    total = total + arrived[source].astype(f32)
            if index:
                arrived[index] = swap(total.astype(bf16), low_bit(index))
            totals[index] = total
    total = totals[0]
    grad_packed = jnp.concatenate(
        [
            grad_query_t.T[:local_pix].astype(bf16),
            total[0].astype(bf16),
            total[1].astype(bf16),
        ],
        axis=1,
    )[None]
    shares, grad_packed = lax.optimization_barrier((shares, grad_packed))
    grad_attn_whole = jnp.einsum(
        "npc,npd->dc", normed_attn, grad_packed, preferred_element_type=jnp.float32
    )
    grad_normed_attn = jnp.einsum(
        "npd,cd->npc", grad_packed, attn_qkv, preferred_element_type=jnp.float32
    )
    grad_from_attn, grad_gain_attn = attn_pull(grad_normed_attn)
    grad_stream = (grad_mid[None] + grad_from_attn).astype(jnp.bfloat16)
    grad_proj_in = jnp.einsum(
        "npc,npd->dc", spatial, grad_stream, preferred_element_type=jnp.float32
    )
    grad_spatial = jnp.einsum(
        "npd,cd->npc", grad_stream, proj_in, preferred_element_type=jnp.float32
    )
    grad_spatial = grad_spatial[0]
    query_key = by_owner(grad_attn_whole[: 2 * channels], owned)
    low_parts = jnp.stack(
        [
            grad_proj_in,
            query_key[:, :channels],
            query_key[:, channels:],
            grad_attn_whole[2 * channels :],
        ]
    ).astype(bf16)
    grad_halo, residual_halo = edge_rows(grad_spatial, residual)
    kept = grad_spatial * pixel_keep
    sums = jnp.stack([jnp.sum(kept, axis=0), jnp.sum(kept * residual_hat, axis=0)])
    means, early_rows = group_means(
        sums, gain_three, counts, [mid_sums[0], mid_sums[1], grad_gain_attn]
    )
    pixel_shape = (local_pix, channels)
    stack_shape = ((local_pix + 2 * LONG, 3 * channels), bf16)
    sum_shape = ((8, channels), f32)
    lanes = pack_width(conv_second)
    flops = 2 * local_pix * conv_second.size
    rows_back = row_table(
        center_three,
        scale_three,
        gain_three,
        means[0],
        means[1],
        center_two,
        scale_two,
        gain_two,
    )
    grad_res, stack_second, grad_pre, sums = conv_call(
        pull_first_kernel,
        "conv_pull",
        width,
        [grad_spatial, *grad_halo, residual, *residual_halo, skip, *skip_halo]
        + [hidden, meta, rows_back, conv_second],
        [(pixel_shape, f32), stack_shape, (pixel_shape, f32), sum_shape],
        flops,
    )
    (grad_halo,) = edge_rows(grad_pre)
    means, middle_rows = group_means(sums[:2], gain_two, counts)
    (pack_second,) = conv_call(
        weight_after_kernel,
        "conv_weight",
        width,
        [stack_second, hidden, meta, rows_back, low_parts],
        [((count, channels, lanes + channels), bf16)],
        flops,
    )
    rows_back = row_table(
        center_two,
        scale_two,
        gain_two,
        means[0],
        means[1],
        center_one,
        scale_one,
        gain_one,
    )
    bits = axis_bits("narrow")
    held_second = pack_second
    for bit in bits[:-1]:
        held_second = halve_step(held_second, bit, "narrow")
    stack_first, pack_first, hidden_sums = conv_call(
        weight_first_kernel,
        "conv_weight",
        width,
        [grad_pre, *grad_halo, hidden, *hidden_halo, pixels, meta, rows_back],
        [stack_shape, ((count, channels, lanes), bf16), sum_shape],
        flops,
    )
    held_first = pack_first
    for bit in bits[:-1]:
        held_first = halve_step(held_first, bit, "narrow")
    held_second, stack_first = lax.optimization_barrier((held_second, stack_first))
    held_second = halve_step(held_second, bits[-1], "narrow")
    grad_pre, sums = conv_call(
        pull_after_kernel,
        "conv_pull",
        width,
        [stack_first, pixels, meta, rows_back, conv_first],
        [(pixel_shape, f32), sum_shape],
        flops,
    )
    held_second, held_first, sums = lax.optimization_barrier((held_second, held_first, sums))
    held_first = halve_step(held_first, bits[-1], "narrow")
    means, late_rows = group_means(sums[:2], gain_one, counts, [hidden_sums[0]])
    image_hat = (image_in - center_one) * scale_one
    grad_image = grad_pre * pixel_keep * gain_one - means[0] - image_hat * means[1]
    grad_latents = (grad_res + pixel_keep * scale_one * grad_image).astype(jnp.bfloat16)[None]
    conv_rows = conv_first.shape[0]
    whole_second = wide_finish(held_second[0])
    sum_conv_second = conv_finish(whole_second[:, :, :lanes], conv_rows)
    low_whole = jnp.transpose(whole_second[:, :, lanes:], (0, 2, 1)).astype(f32)
    shares = [narrow_finish(share) for share in shares]
    sum_proj_out, sum_attn_out, sum_geglu_out, sum_geglu_in = split_top(shares, owned, channels)
    sum_conv_first = conv_finish(wide_finish(held_first[0]), conv_rows)
    stamp_row = jnp.pad(
        jnp.concatenate([labels, timesteps]).astype(f32), (0, channels - 2 * images)
    )
    spread = double(
        jnp.stack(
            [
                early_rows[2],
                late_rows[2],
                early_rows[3],
                early_rows[4],
                early_rows[1],
                middle_rows[1],
                late_rows[1],
                stamp_row,
            ]
        ),
        "wide",
    )
    labels_all = spread[:, 7, 0].astype(jnp.int32)
    steps_all = spread[:, 7, 1].astype(jnp.int32)
    angles_all = steps_all.astype(jnp.float32)[:, None] * frequency[None, :]
    time_all = jax.nn.silu(jnp.concatenate([jnp.cos(angles_all), jnp.sin(angles_all)], axis=1))
    hot_all = (
        labels_all[:, None] == jnp.arange(class_table.shape[0], dtype=jnp.int32)[None, :]
    ).astype(jnp.float32)
    context_all = jnp.dot(hot_all, class_table.astype(jnp.float32), precision=HIGH)
    value_all = jnp.dot(context_all, value_weight, precision=HIGH)
    cross_all = spread[:, 0]
    grad_value_all = jnp.dot(cross_all, cross_weight.T, precision=HIGH)
    grad_context_all = jnp.dot(grad_value_all, value_weight.T, precision=HIGH)
    sum_cross_out = jnp.dot(value_all.T, own_columns(cross_all), precision=HIGH)
    sum_cross_value = jnp.dot(context_all.T, own_columns(grad_value_all), precision=HIGH)
    sum_class_table = jnp.dot(hot_all.T, own_columns(grad_context_all), precision=HIGH)
    sum_time_proj = jnp.dot(time_all.T, own_columns(spread[:, 1]), precision=HIGH)
    gain_sums = own_columns(jnp.sum(spread[:, 2:7], axis=0))
    return (
        output[None],
        grad_latents,
        gain_sums[4],
        sum_conv_first,
        sum_time_proj,
        gain_sums[3],
        sum_conv_second,
        gain_sums[2],
        low_whole[0],
        gain_sums[1],
        jnp.concatenate([low_whole[1], low_whole[2]], axis=1),
        low_whole[3],
        sum_attn_out,
        sum_class_table,
        sum_cross_value,
        sum_cross_out,
        gain_sums[0],
        sum_geglu_in,
        sum_geglu_out,
        sum_proj_out,
    )


def solution(mesh):
    placed = (
        P("wide", "narrow", None),
        P("wide", "narrow", None),
        P("wide"),
        P("wide", None),
        P("wide"),
        P("wide"),
        P(),
        P(),
        P(),
        P(),
        P(),
        P(),
        P(),
        P(),
        P(),
        P(),
        P(),
        P(),
        P(),
        P(),
        P(),
        P(),
        P(),
    )
    return jax.shard_map(
        per_device,
        mesh=mesh,
        in_specs=placed,
        out_specs=(
            P("wide", "narrow", None),
            P("wide", "narrow", None),
            P("wide"),
            P(None, "wide"),
            P(None, "wide"),
            P("wide"),
            P(None, "wide"),
            P("wide"),
            P(None, "wide"),
            P("wide"),
            P(None, "wide"),
            P(None, "wide"),
            P(None, "wide"),
            P(None, "wide"),
            P(None, "wide"),
            P(None, "wide"),
            P("wide"),
            P(None, "wide"),
            P(None, "wide"),
            P(None, "wide"),
        ),
        check_vma=False,
    )
```

```python
import functools
import math

import jax
import jax.numpy as jnp
from jax import lax
from jax.experimental import pallas as pl
from jax.experimental.pallas import tpu as pltpu
from jax.sharding import PartitionSpec as P

HEAD_DIM = 32
GROUPS = 32
SHORT = 48
LONG = 80


HIGH = lax.Precision.HIGHEST
EPS_GROUP = 1e-06
EPS_LAYER = 1e-05
MASKED = -1e30


TILE = 128
PER_TILE = TILE // HEAD_DIM
QB = 256
ONES = 16
SAFE_REACH = 90.0
LN2 = math.log(2.0)
bf16 = jnp.bfloat16
f32 = jnp.float32


def group_sum(value):
    grouped = value.reshape(value.shape[0], GROUPS, -1)
    summed = jnp.sum(grouped, axis=2, keepdims=True)
    return jnp.broadcast_to(summed, grouped.shape).reshape(value.shape)


def group_moments(sums, counts):
    sums = group_sum(narrow_sum(sums)) / counts[0]
    center = sums[0]
    spread = sums[1] - center * center
    return center, lax.rsqrt(spread + EPS_GROUP)


def group_means(sums, gain, counts, extras=()):
    sums = narrow_sum(jnp.concatenate([sums] + [row[None] for row in extras], axis=0))
    means = group_sum(sums[:2] * gain) / counts[0]
    return means, sums


def layer_norm(field_in, gain):
    center = jnp.mean(field_in, axis=-1, keepdims=True)
    spread = jnp.mean(jnp.square(field_in - center), axis=-1, keepdims=True)
    return (field_in - center) * lax.rsqrt(spread + EPS_LAYER) * gain


def head_rows(block, head):
    row = lax.broadcasted_iota(jnp.int32, block.shape, 0)
    inside = (row >= head * HEAD_DIM) & (row < (head + 1) * HEAD_DIM)
    return jnp.where(inside, block, jnp.zeros_like(block))


def head_lanes(block, head):
    lane = lax.broadcasted_iota(jnp.int32, block.shape, 1)
    inside = (lane >= head * HEAD_DIM) & (lane < (head + 1) * HEAD_DIM)
    return jnp.where(inside, block, jnp.zeros_like(block))


def mask_rows():
    row = lax.broadcasted_iota(jnp.int32, (TILE, QB), 0)
    return jnp.where(row == 0, 1.0, 0.0).astype(bf16)


def attend_kernel(first, last, parts, *refs):
    qt_ref = refs[0]
    key_refs = refs[1 : 1 + parts]
    value_refs = refs[1 + parts : 1 + 2 * parts]
    aug_ref = refs[1 + 2 * parts]
    rest = refs[2 + 2 * parts :]
    if not first:
        peak_in, acc_in = rest[:2]
        rest = rest[2:]
    if last:
        heads_ref, log_ref = rest
    else:
        peak_ref, acc_ref = rest
    keys = jnp.concatenate([ref[...] for ref in key_refs], axis=0)
    keys = jnp.concatenate([keys, aug_ref[...]], axis=1)
    values = jnp.concatenate([ref[...] for ref in value_refs], axis=0)
    value_t = jnp.transpose(values, (1, 0))
    ones = jnp.ones((ONES, value_t.shape[1]), bf16)
    low_rows = mask_rows()

    head_of = lambda shape, axis: lax.broadcasted_iota(jnp.int32, shape, axis) // HEAD_DIM
    pick = jnp.where(head_of((TILE, TILE), 0) == head_of((TILE, TILE), 1), 1.0, 0.0).astype(bf16)
    all_keys = keys[:, :TILE]
    key_norms = jnp.dot(all_keys * all_keys, pick, preferred_element_type=f32)
    all_queries = qt_ref[...]
    query_norms = jnp.dot(pick, all_queries * all_queries, preferred_element_type=f32)
    reach = jnp.float32(0.0)
    for head in range(PER_TILE):
        rows = slice(head * HEAD_DIM, head * HEAD_DIM + 8)
        mine = head_of(key_norms.shape, 1) == head
        key_peak = jnp.max(jnp.where(mine, key_norms, 0.0))
        reach = jnp.maximum(reach, key_peak * jnp.max(query_norms[rows]))

    def make_step(shifted):
        def block_step(step, carry):
            cols = pl.ds(pl.multiple_of(step * QB, QB), QB)
            qt = qt_ref[:, cols]
            for head in range(PER_TILE):
                rows = slice(head * HEAD_DIM, (head + 1) * HEAD_DIM)
                query = jnp.concatenate([head_rows(qt, head), low_rows], axis=0)
                scores = jnp.dot(keys, query, preferred_element_type=f32)
                if shifted:
                    peak = jnp.max(scores, axis=0, keepdims=True)
                    probs = jnp.exp2(scores - peak).astype(bf16)
                else:
                    peak = jnp.zeros((1, QB), f32)
                    probs = jnp.exp2(scores).astype(bf16)
                value_h = jnp.concatenate([value_t[rows], ones], axis=0)
                acc = jnp.dot(value_h, probs, preferred_element_type=f32)
                if not first:
                    peak_old = peak_in[head, 0:1, cols]
                    peak_new = jnp.maximum(peak, peak_old)
                    acc = acc * jnp.exp2(peak - peak_new)
                    acc = acc + acc_in[head, :, cols] * jnp.exp2(peak_old - peak_new)
                    peak = peak_new
                if last:
                    total = acc[HEAD_DIM : HEAD_DIM + 1]
                    heads_ref[rows, cols] = acc[:HEAD_DIM] / total
                    log_ref[head, :, cols] = jnp.broadcast_to(peak + jnp.log2(total), (8, QB))
                else:
                    acc_ref[head, :, cols] = acc
                    peak_ref[head, :, cols] = jnp.broadcast_to(peak, (8, QB))
            return carry

        return block_step

    steps = qt_ref.shape[1] // QB

    @pl.when(reach < SAFE_REACH * SAFE_REACH)
    def _():
        lax.fori_loop(0, steps, make_step(False), 0)

    @pl.when(jnp.logical_not(reach < SAFE_REACH * SAFE_REACH))
    def _():
        lax.fori_loop(0, steps, make_step(True), 0)


def chunk_specs(count, tiles, parts):
    key_spec = pl.BlockSpec((count, TILE), lambda t: (0, t))
    value_spec = pl.BlockSpec((count, TILE), lambda t: (0, tiles + t))
    aug_spec = pl.BlockSpec((parts * count, TILE), lambda t: (0, 0))
    return [key_spec] * parts + [value_spec] * parts + [aug_spec]


def attend_some(first, last, query_t, chunks, aug, state):
    channels, queries = query_t.shape
    count = chunks[0].shape[0]
    heads = channels // HEAD_DIM
    tiles = channels // TILE
    t_spec = pl.BlockSpec((TILE, queries), lambda t: (t, 0))
    cube = lambda t: (t, 0, 0)
    row_spec = pl.BlockSpec((PER_TILE, 8, queries), cube)
    acc_spec = pl.BlockSpec((PER_TILE, HEAD_DIM + ONES, queries), cube)
    in_specs = [t_spec] + chunk_specs(count, tiles, len(chunks))
    if not first:
        in_specs += [row_spec, acc_spec]
    row_shape = jax.ShapeDtypeStruct((heads, 8, queries), f32)
    if last:
        out_shape = (jax.ShapeDtypeStruct((channels, queries), f32), row_shape)
        out_specs = (t_spec, row_spec)
    else:
        out_shape = (
            row_shape,
            jax.ShapeDtypeStruct((heads, HEAD_DIM + ONES, queries), f32),
        )
        out_specs = (row_spec, acc_spec)
    return pl.pallas_call(
        functools.partial(attend_kernel, first, last, len(chunks)),
        grid=(tiles,),
        in_specs=in_specs,
        out_specs=out_specs,
        out_shape=out_shape,
        compiler_params=pltpu.CompilerParams(vmem_limit_bytes=58 << 20),
        cost_estimate=pl.CostEstimate(
            flops=32 * len(chunks) * channels * queries * count,
            bytes_accessed=8 * channels * (queries + count),
            transcendentals=len(chunks) * heads * queries * count,
        ),
        name="attend",
    )(query_t, *chunks, *chunks, aug, *state)


def attend_back_kernel(first, parts, *refs):
    qt_ref, q_ref, dt_ref, d_ref, log_ref, heads_ref = refs[:6]
    key_refs = refs[6 : 6 + parts]
    value_refs = refs[6 + parts : 6 + 2 * parts]
    aug_ref = refs[6 + 2 * parts]
    refs = refs[7 + 2 * parts :]
    if not first:
        dq_in = refs[0]
        refs = refs[1:]
    dq_ref = refs[0]
    out_refs = refs[1 : 1 + parts]
    dk_acc, dv_acc = refs[1 + parts :]
    count = key_refs[0].shape[0]
    k_tile = jnp.concatenate([ref[...] for ref in key_refs], axis=0)
    keys = jnp.concatenate([k_tile, aug_ref[...]], axis=1)
    values = jnp.concatenate([ref[...] for ref in value_refs], axis=0)
    key_t = jnp.transpose(k_tile, (1, 0))
    low_rows = mask_rows()
    dk_acc[...] = jnp.zeros_like(dk_acc)
    dv_acc[...] = jnp.zeros_like(dv_acc)
    factor = 1.0 / math.sqrt(HEAD_DIM)

    def block_step(step, carry):
        cols = pl.ds(pl.multiple_of(step * QB, QB), QB)
        qt = qt_ref[:, cols]
        dt = dt_ref[:, cols]
        q_blk = q_ref[cols, :]
        d_blk = d_ref[cols, :]
        probs_all, grads_all, q_all, d_all = [], [], [], []
        for head in range(PER_TILE):
            rows = slice(head * HEAD_DIM, (head + 1) * HEAD_DIM)
            query = jnp.concatenate([head_rows(qt, head), low_rows], axis=0)
            scores = jnp.dot(keys, query, preferred_element_type=f32)
            probs = jnp.exp2(scores - log_ref[head, 0:1, cols])
            weighted = jnp.sum(
                heads_ref[rows, cols] * dt[rows].astype(f32), axis=0, keepdims=True
            )
            grad_p = jnp.dot(values, head_rows(dt, head), preferred_element_type=f32)
            grad_s = (probs * (grad_p - weighted)).astype(bf16)
            probs_all.append(probs.astype(bf16))
            grads_all.append(grad_s)
            q_all.append(head_lanes(q_blk, head))
            d_all.append(head_lanes(d_blk, head))
            dq = jnp.dot(key_t[rows], grad_s, preferred_element_type=f32) * factor
            if not first:
                dq = dq + dq_in[rows, cols]
            dq_ref[rows, cols] = dq
        dv_acc[...] += jnp.dot(
            jnp.concatenate(probs_all, axis=1),
            jnp.concatenate(d_all, axis=0),
            preferred_element_type=f32,
        )
        dk_acc[...] += jnp.dot(
            jnp.concatenate(grads_all, axis=1),
            jnp.concatenate(q_all, axis=0),
            preferred_element_type=f32,
        )
        return carry

    lax.fori_loop(0, qt_ref.shape[1] // QB, block_step, 0)
    for index, ref in enumerate(out_refs):
        rows = slice(index * count, (index + 1) * count)
        ref[0] = (dk_acc[rows] * LN2).astype(ref.dtype)
        ref[1] = dv_acc[rows].astype(ref.dtype)


def attend_back_some(
    first, out_types, query_t, query, grad_t, grad, logs, heads_t, chunks, aug, dq
):
    channels, queries = query_t.shape
    count = chunks[0].shape[0]
    parts = len(chunks)
    tiles = channels // TILE
    t_spec = pl.BlockSpec((TILE, queries), lambda t: (t, 0))
    n_spec = pl.BlockSpec((queries, TILE), lambda t: (0, t))
    row_spec = pl.BlockSpec((PER_TILE, 8, queries), lambda t: (t, 0, 0))
    out_spec = pl.BlockSpec((2, count, TILE), lambda t: (0, 0, t))
    in_specs = [t_spec, n_spec, t_spec, n_spec, row_spec, t_spec] + chunk_specs(count, tiles, parts)
    state = ()
    if not first:
        in_specs.append(t_spec)
        state = (dq,)
    return pl.pallas_call(
        functools.partial(attend_back_kernel, first, parts),
        grid=(tiles,),
        in_specs=in_specs,
        out_specs=(t_spec,) + (out_spec,) * parts,
        out_shape=(jax.ShapeDtypeStruct((channels, queries), f32),)
        + tuple(jax.ShapeDtypeStruct((2, count, channels), kind) for kind in out_types),
        scratch_shapes=[pltpu.VMEM((parts * count, TILE), f32)] * 2,
        compiler_params=pltpu.CompilerParams(vmem_limit_bytes=58 << 20),
        cost_estimate=pl.CostEstimate(
            flops=80 * parts * channels * queries * count,
            bytes_accessed=12 * channels * (queries + count),
            transcendentals=parts * channels // HEAD_DIM * queries * count,
        ),
        name="attend_back",
    )(query_t, query, grad_t, grad, logs, heads_t, *chunks, *chunks, aug, *state)


def swap(value, bit, axis="narrow"):
    count = lax.axis_size(axis)
    return lax.ppermute(value, axis, [(i, i ^ bit) for i in range(count)])


def low_bit(index):
    return index & -index


def axis_bits(axis):
    return [1 << level for level in range(lax.axis_size(axis).bit_length() - 1)]


def my_bit(bit, axis="narrow"):
    return (lax.axis_index(axis) // bit) % 2


def narrow_sum(value):
    for bit in axis_bits("narrow"):
        value = value + swap(value, bit)
    return value


def key_aug(keep_chunk):
    lane = lax.broadcasted_iota(jnp.int32, (keep_chunk.shape[0], TILE), 1)
    bias = jnp.where(keep_chunk[:, None] > 0, 0.0, MASKED)
    return jnp.where(lane == 0, bias, 0.0).astype(bf16)


def halve_step(held, bit, axis):
    halves = held.reshape((held.shape[0] // 2, 2) + held.shape[1:])
    mine = my_bit(bit, axis)
    kept = lax.dynamic_index_in_dim(halves, mine, 1, keepdims=False)
    sent = lax.dynamic_index_in_dim(halves, 1 - mine, 1, keepdims=False)
    return (kept.astype(f32) + swap(sent, bit, axis).astype(f32)).astype(bf16)


def halve(held, axis):
    for bit in axis_bits(axis):
        held = halve_step(held, bit, axis)
    return held[0]


def double(value, axis):
    whole = value[None]
    for bit in reversed(axis_bits(axis)):
        other = swap(whole, bit, axis)
        pair = jnp.where(
            my_bit(bit, axis) == 0,
            jnp.stack([whole, other], axis=1),
            jnp.stack([other, whole], axis=1),
        )
        whole = pair.reshape((-1,) + value.shape)
    return whole


def wide_split(share):
    wide = lax.axis_size("wide")
    return share.reshape(wide, share.shape[0] // wide, share.shape[1])


def narrow_gather(share):
    count = lax.axis_size("narrow")
    spot = lax.axis_index("narrow")
    near = jnp.stack([share] + [swap(share, index) for index in range(1, count)])
    pick = lambda index: lax.dynamic_index_in_dim(near, spot ^ index, 0, keepdims=False)
    return jnp.stack([pick(index) for index in range(count)])


def conv_finish(whole, rows):
    return jnp.transpose(whole, (0, 2, 1)).reshape(-1, whole.shape[1])[:rows].astype(f32)


def by_owner(grad_t, width):
    wide = lax.axis_size("wide")
    groups = grad_t.shape[0] // wide // width
    split = grad_t.reshape(wide, groups, width, grad_t.shape[1])
    return jnp.transpose(split, (0, 2, 1, 3)).reshape(wide * width, -1)


def narrow_finish(share):
    share = share.astype(bf16)
    for bit in axis_bits("narrow"):
        share = (share.astype(f32) + swap(share, bit).astype(f32)).astype(bf16)
    return share.astype(f32)


def own_columns(value):
    width = value.shape[-1] // lax.axis_size("wide")
    start = lax.axis_index("wide") * width
    return lax.dynamic_slice_in_dim(value, start, width, value.ndim - 1)


CONV_LIMIT = 50 << 20
NT = (((1,), (1,)), ((), ()))


def lanes_of(meta_ref, index, start, count, channels):
    return jnp.concatenate([meta_ref[index, start : start + count]] * (channels // TILE), axis=1)


def store_shifts(field, meta_ref, stack_ref):
    total, channels = field.shape
    low = jnp.where(
        lanes_of(meta_ref, 1, 0, total, channels) > 0, pltpu.roll(field, 1, 0), 0.0
    )
    high = jnp.where(
        lanes_of(meta_ref, 2, 0, total, channels) > 0, pltpu.roll(field, total - 1, 0), 0.0
    )
    stack_ref[:, :channels] = low.astype(bf16)
    stack_ref[:, channels : 2 * channels] = field.astype(bf16)
    stack_ref[:, 2 * channels :] = high.astype(bf16)


def with_halo(low_ref, own_ref, high_ref):
    parts = [low_ref[...].astype(f32), own_ref[...].astype(f32), high_ref[...].astype(f32)]
    return jnp.concatenate(parts, axis=0)


def conv_kernel(width_ref, x_ref, low_ref, high_ref, meta_ref, rows_ref, w_ref, add_ref, y_ref, sum_ref, stack_ref):
    local, channels = x_ref.shape
    total = stack_ref.shape[0]
    width = width_ref[0]
    field = with_halo(low_ref, x_ref, high_ref)
    keep = lanes_of(meta_ref, 0, 0, total, channels)
    pre = keep * (field - rows_ref[0:1]) * (rows_ref[1:2] * rows_ref[2:3])
    store_shifts(pre / (1.0 + jnp.exp(-pre)), meta_ref, stack_ref)
    block = local // 2
    sum_ref[...] = jnp.zeros_like(sum_ref)

    def block_step(step, carry):
        start = step * block
        taps = []
        for shift in (-1, 0, 1):
            offset = pl.multiple_of(LONG + start + shift * width, 16)
            taps.append(stack_ref[pl.ds(offset, block), :])
        out = jnp.dot(jnp.concatenate(taps, axis=1), w_ref[...], preferred_element_type=f32)
        own = pl.ds(pl.multiple_of(start, 16), block)
        if add_ref.shape[0] == local:
            out = out + add_ref[own, :].astype(f32)
        else:
            out = out + add_ref[0:1]
        y_ref[own, :] = out
        kept = meta_ref[0, pl.ds(pl.multiple_of(LONG + start, 16), block), :]
        kept = out * jnp.concatenate([kept] * (channels // TILE), axis=1)
        sum_ref[0:1] += jnp.sum(kept, axis=0, keepdims=True)
        sum_ref[1:2] += jnp.sum(kept * out, axis=0, keepdims=True)
        return carry

    lax.fori_loop(0, 2, block_step, 0)


def conv_forward(width, field, halo, meta, rows, weight, add):
    local, channels = field.shape
    vmem = pl.BlockSpec(memory_space=pltpu.VMEM)
    return pl.pallas_call(
        conv_kernel,
        in_specs=[pl.BlockSpec(memory_space=pltpu.SMEM)] + [vmem] * 7,
        out_specs=(vmem, vmem),
        out_shape=(
            jax.ShapeDtypeStruct((local, channels), f32),
            jax.ShapeDtypeStruct((8, channels), f32),
        ),
        scratch_shapes=[pltpu.VMEM((local + 2 * LONG, 3 * channels), bf16)],
        compiler_params=pltpu.CompilerParams(vmem_limit_bytes=CONV_LIMIT),
        cost_estimate=pl.CostEstimate(
            flops=2 * local * weight.size,
            bytes_accessed=4 * weight.size,
            transcendentals=2 * local * channels,
        ),
        name="conv_forward",
    )(width, field, halo[0], halo[1], meta, rows, weight, add)


def conv_build(with_skip, refs, meta_ref, rows_ref, stack_ref):
    d_ref, d_low, d_high, v_ref, v_low, v_high = refs[:6]
    local, channels = d_ref.shape
    total = stack_ref.shape[0]
    keep = lanes_of(meta_ref, 0, 0, total, channels)
    normed = (with_halo(v_low, v_ref, v_high) - rows_ref[0:1]) * rows_ref[1:2]
    inner = with_halo(d_low, d_ref, d_high) * keep * rows_ref[2:3] - rows_ref[3:4]
    field = keep * rows_ref[1:2] * (inner - normed * rows_ref[4:5])
    if with_skip:
        c_ref, c_low, c_high = refs[6:9]
        field = field + with_halo(c_low, c_ref, c_high)
    store_shifts(field, meta_ref, stack_ref)
    return field[LONG : LONG + local]


def conv_pull(width, x_ref, meta_ref, rows_ref, w_ref, stack_ref, pre_ref, sum_ref):
    local, channels = x_ref.shape
    block = local // 2

    def block_step(step, carry):
        start = step * block
        own = pl.ds(pl.multiple_of(start, 16), block)
        out = jnp.zeros((block, channels), f32)
        for row in range(3):
            offset = pl.multiple_of(LONG + start + (row - 1) * width, 16)
            for col in range(3):
                tap = 8 - (3 * row + col)
                out = out + lax.dot_general(
                    stack_ref[pl.ds(offset, block), col * channels : (col + 1) * channels],
                    w_ref[tap * channels : (tap + 1) * channels, :],
                    NT,
                    preferred_element_type=f32,
                )
        kept = meta_ref[0, pl.ds(pl.multiple_of(LONG + start, 16), block), :]
        kept = jnp.concatenate([kept] * (channels // TILE), axis=1)
        xhat = (x_ref[own, :].astype(f32) - rows_ref[5:6]) * rows_ref[6:7]
        pre = kept * xhat * rows_ref[7:8]
        gate = 1.0 / (1.0 + jnp.exp(-pre))
        grad = out * (gate * (1.0 + pre * (1.0 - gate)))
        pre_ref[own, :] = grad
        grad = grad * kept
        sum_ref[0:1] += jnp.sum(grad, axis=0, keepdims=True)
        sum_ref[1:2] += jnp.sum(grad * xhat, axis=0, keepdims=True)
        return carry

    lax.fori_loop(0, 2, block_step, 0)


def conv_weight(width, x_ref, meta_ref, rows_ref, stack_ref, pack_ref, extra_ref):
    local, channels = x_ref.shape
    kept = lanes_of(meta_ref, 0, LONG, local, channels)
    pre = kept * (x_ref[...].astype(f32) - rows_ref[5:6]) * (rows_ref[6:7] * rows_ref[7:8])
    act_t = jnp.transpose((pre / (1.0 + jnp.exp(-pre))).astype(bf16), (1, 0))
    extra = 0 if extra_ref is None else extra_ref.shape[2]
    groups = (pack_ref.shape[2] - extra) // TILE
    tiles = channels // TILE
    for row in range(3):
        offset = pl.multiple_of(LONG + (row - 1) * width, 16)
        for col in range(3):
            tap = 8 - (3 * row + col)
            grad = jnp.dot(
                act_t,
                stack_ref[pl.ds(offset, local), col * channels : (col + 1) * channels],
                preferred_element_type=f32,
            )
            grad = jnp.transpose(grad.astype(bf16), (1, 0))
            for tile in range(tiles):
                spot = tap * tiles + tile
                lane = (spot % groups) * TILE
                pack_ref[spot // groups, :, lane : lane + TILE] = grad[
                    :, tile * TILE : (tile + 1) * TILE
                ]
    for spot in range(9 * tiles, pack_ref.shape[0] * groups):
        lane = (spot % groups) * TILE
        pack_ref[spot // groups, :, lane : lane + TILE] = jnp.zeros((channels, TILE), bf16)
    if extra:
        pack_ref[:, :, groups * TILE :] = extra_ref[...]


def pull_first_kernel(width_ref, *refs):
    x_ref, meta_ref, rows_ref, w_ref, e_ref, stack_ref, pre_ref, sum_ref = refs[9:]
    e_ref[...] = conv_build(True, refs, meta_ref, rows_ref, stack_ref)
    sum_ref[...] = jnp.zeros_like(sum_ref)
    conv_pull(width_ref[0], x_ref, meta_ref, rows_ref, w_ref, stack_ref, pre_ref, sum_ref)


def weight_after_kernel(width_ref, stack_ref, x_ref, meta_ref, rows_ref, extra_ref, pack_ref):
    conv_weight(width_ref[0], x_ref, meta_ref, rows_ref, stack_ref, pack_ref, extra_ref)


def weight_first_kernel(width_ref, *refs):
    x_ref, meta_ref, rows_ref, stack_ref, pack_ref, sum_ref = refs[6:]
    field = conv_build(False, refs, meta_ref, rows_ref, stack_ref)
    sum_ref[...] = jnp.broadcast_to(jnp.sum(field, axis=0, keepdims=True), sum_ref.shape)
    conv_weight(width_ref[0], x_ref, meta_ref, rows_ref, stack_ref, pack_ref, None)


def pull_after_kernel(width_ref, stack_ref, x_ref, meta_ref, rows_ref, w_ref, pre_ref, sum_ref):
    sum_ref[...] = jnp.zeros_like(sum_ref)
    conv_pull(width_ref[0], x_ref, meta_ref, rows_ref, w_ref, stack_ref, pre_ref, sum_ref)


def conv_call(kernel, name, width, operands, shapes, flops):
    vmem = pl.BlockSpec(memory_space=pltpu.VMEM)
    return pl.pallas_call(
        kernel,
        in_specs=[pl.BlockSpec(memory_space=pltpu.SMEM)] + [vmem] * len(operands),
        out_specs=(vmem,) * len(shapes),
        out_shape=tuple(jax.ShapeDtypeStruct(shape, kind) for shape, kind in shapes),
        compiler_params=pltpu.CompilerParams(vmem_limit_bytes=CONV_LIMIT),
        cost_estimate=pl.CostEstimate(flops=flops, bytes_accessed=1 << 24, transcendentals=0),
        name=name,
    )(width, *operands)


def pack_width(weight):
    count = lax.axis_size("narrow")
    return (weight.shape[0] + (-weight.shape[0] % (count * TILE))) // count


def edge_rows(*fields):
    count = lax.axis_size("narrow")
    forward = [(i, i + 1) for i in range(count - 1)]
    backward = [(i + 1, i) for i in range(count - 1)]
    tails = jnp.concatenate([field[-LONG:] for field in fields], axis=0)
    heads = jnp.concatenate([field[:LONG] for field in fields], axis=0)
    low = lax.ppermute(tails, "narrow", forward)
    high = lax.ppermute(heads, "narrow", backward)
    cut = lambda rim, index: rim[index * LONG : (index + 1) * LONG]
    return [(cut(low, index), cut(high, index)) for index in range(len(fields))]


def pixel_meta(keep_image, row_start, local, row_width):
    rim = jnp.pad(keep_image, (LONG, LONG))
    keep = lax.dynamic_slice_in_dim(rim, row_start, local + 2 * LONG, 0)
    spot = jnp.arange(local + 2 * LONG, dtype=jnp.int32)
    column = (spot + 2 * LONG * SHORT - LONG) % row_width
    rows = jnp.stack([keep, (column > 0).astype(f32), (column < row_width - 1).astype(f32)])
    return jnp.broadcast_to(rows[:, :, None], rows.shape + (TILE,))


def row_table(*rows):
    table = jnp.stack([jnp.broadcast_to(row.reshape(-1), rows[0].reshape(-1).shape) for row in rows])
    return jnp.pad(table, ((0, 8 - len(rows)), (0, 0)))


MID_BLOCKS = 4


def dot_nt(left, right):
    return lax.dot_general(left, right, NT, preferred_element_type=f32)


def mid_kernel(
    owned,
    heads_ref,
    stream_ref,
    residual_ref,
    cot_ref,
    row_ref,
    attn_out_ref,
    geglu_in_ref,
    geglu_out_ref,
    proj_out_ref,
    out_ref,
    grad_mid_ref,
    grad_ref,
    grad_t_ref,
    top_ref,
    gate_ref,
    sum_ref,
    heads_low,
    normed_low,
    mixed_low,
    end_low,
    ffo_low,
    gates_low,
    mid_low,
):
    local, channels = stream_ref.shape
    hidden = geglu_out_ref.shape[0]
    block = local // MID_BLOCKS
    heads_low[...] = jnp.transpose(heads_ref[...].astype(bf16), (1, 0))[:local]
    sum_ref[...] = jnp.zeros_like(sum_ref)

    def block_step(step, carry):
        own = pl.ds(pl.multiple_of(step * block, 16), block)
        mid = stream_ref[own, :] + row_ref[0:1]
        mid = mid + jnp.dot(heads_low[own, :], attn_out_ref[...], preferred_element_type=f32)
        center = jnp.mean(mid, axis=1, keepdims=True)
        inv_std = lax.rsqrt(jnp.mean(jnp.square(mid - center), axis=1, keepdims=True) + EPS_LAYER)
        xhat = (mid - center) * inv_std
        normed = (xhat * row_ref[1:2]).astype(bf16)
        normed_low[own, :] = normed
        gates = jnp.dot(normed, geglu_in_ref[...], preferred_element_type=f32)
        value, gate = gates[:, :hidden], gates[:, hidden:]
        half = 0.5 * (1.0 + lax.erf(gate * math.sqrt(0.5)))
        gelu = gate * half
        slope = half + gate * jnp.exp(-0.5 * gate * gate) * (1.0 / math.sqrt(2.0 * math.pi))
        mixed = (value * gelu).astype(bf16)
        mixed_low[own, :] = mixed
        end = mid + jnp.dot(mixed, geglu_out_ref[...], preferred_element_type=f32)
        end = end.astype(bf16)
        end_low[own, :] = end
        out = residual_ref[own, :] + jnp.dot(end, proj_out_ref[...], preferred_element_type=f32)
        out_ref[own, :] = out.astype(bf16)
        grad_end = dot_nt(cot_ref[own, :], proj_out_ref[...])
        grad_ffo = grad_end.astype(bf16)
        ffo_low[own, :] = grad_ffo
        grad_mixed = dot_nt(grad_ffo, geglu_out_ref[...])
        grad_gates = jnp.concatenate(
            [(grad_mixed * gelu).astype(bf16), (grad_mixed * value * slope).astype(bf16)], axis=1
        )
        gates_low[own, :] = grad_gates
        grad_normed = dot_nt(grad_gates, geglu_in_ref[...])
        grad_hat = grad_normed * row_ref[1:2]
        mean_one = jnp.mean(grad_hat, axis=1, keepdims=True)
        mean_two = jnp.mean(grad_hat * xhat, axis=1, keepdims=True)
        grad_mid = grad_end + inv_std * (grad_hat - mean_one - xhat * mean_two)
        grad_mid_ref[own, :] = grad_mid
        sum_ref[0:1] += jnp.sum(grad_mid, axis=0, keepdims=True)
        sum_ref[1:2] += jnp.sum(grad_normed * xhat, axis=0, keepdims=True)
        grad_mid = grad_mid.astype(bf16)
        mid_low[own, :] = grad_mid
        grad_ref[own, :] = dot_nt(grad_mid, attn_out_ref[...]).astype(bf16)
        return carry

    lax.fori_loop(0, MID_BLOCKS, block_step, 0)
    pad = grad_ref.shape[0] - local
    if pad:
        grad_ref[local:, :] = jnp.zeros((pad, channels), bf16)
    grad_t_ref[...] = jnp.transpose(grad_ref[...], (1, 0))

    def put(index, grad):
        if owned:
            for owner in range(channels // owned):
                rows = grad[owner * owned : (owner + 1) * owned]
                top_ref[owner, index * owned : (index + 1) * owned, :] = rows
        else:
            top_ref[:, index * channels : (index + 1) * channels] = grad

    put(
        0,
        jnp.dot(
            jnp.transpose(cot_ref[...], (1, 0)), end_low[...], preferred_element_type=f32
        ),
    )
    put(
        1,
        jnp.dot(
            jnp.transpose(mid_low[...], (1, 0)), heads_low[...], preferred_element_type=f32
        ),
    )
    ffo_t = jnp.transpose(ffo_low[...], (1, 0))
    pieces = hidden // channels
    for piece in range(pieces):
        mixed = mixed_low[:, piece * channels : (piece + 1) * channels]
        put(2 + piece, jnp.dot(ffo_t, mixed, preferred_element_type=f32))
    normed_t = jnp.transpose(normed_low[...], (1, 0))
    for piece in range(2 * pieces):
        grads = gates_low[:, piece * channels : (piece + 1) * channels]
        grad = jnp.dot(normed_t, grads, preferred_element_type=f32)
        if owned:
            top_ref[piece, (2 + pieces) * owned :, :] = grad
        else:
            gate_ref[:, piece * channels : (piece + 1) * channels] = grad


def mid_layer(heads_t, stream, residual, cotangent, rows, attn_out, geglu_in, geglu_out, proj_out):
    local, channels = stream.shape
    queries = heads_t.shape[1]
    hidden = geglu_out.shape[0]
    wide = lax.axis_size("wide")
    pieces = 2 + hidden // channels
    aligned = 2 * hidden == wide * channels
    owned = channels // wide if aligned else 0
    if aligned:
        top_shape = jax.ShapeDtypeStruct((wide, pieces * owned + channels, channels), f32)
        gate_shape = jax.ShapeDtypeStruct((8, channels), f32)
    else:
        top_shape = jax.ShapeDtypeStruct((channels, pieces * channels), f32)
        gate_shape = jax.ShapeDtypeStruct((channels, 2 * hidden), f32)
    vmem = pl.BlockSpec(memory_space=pltpu.VMEM)
    low = lambda width: pltpu.VMEM((local, width), bf16)
    return pl.pallas_call(
        functools.partial(mid_kernel, owned),
        in_specs=[vmem] * 9,
        out_specs=(vmem,) * 7,
        out_shape=(
            jax.ShapeDtypeStruct((local, channels), bf16),
            jax.ShapeDtypeStruct((local, channels), f32),
            jax.ShapeDtypeStruct((queries, channels), bf16),
            jax.ShapeDtypeStruct((channels, queries), bf16),
            top_shape,
            gate_shape,
            jax.ShapeDtypeStruct((8, channels), f32),
        ),
        scratch_shapes=[
            low(channels),
            low(channels),
            low(hidden),
            low(channels),
            low(channels),
            low(2 * hidden),
            low(channels),
        ],
        compiler_params=pltpu.CompilerParams(vmem_limit_bytes=57 << 20),
        cost_estimate=pl.CostEstimate(
            flops=6 * local * channels * (3 * hidden + 2 * channels),
            bytes_accessed=24 * channels * hidden,
            transcendentals=2 * local * hidden,
        ),
        name="mid_layer",
    )(heads_t, stream, residual, cotangent, rows, attn_out, geglu_in, geglu_out, proj_out)


def top_shares(top, gates):
    wide = lax.axis_size("wide")
    if top.ndim == 3:
        share = lax.psum_scatter(top, "wide", scatter_dimension=0, tiled=True)[0]
        return (share,)
    channels = top.shape[0]
    split = top.reshape(wide, channels // wide, -1, channels)
    split = jnp.transpose(split, (0, 2, 1, 3)).reshape(wide, -1, channels)
    share = lax.psum_scatter(split, "wide", scatter_dimension=0, tiled=True)[0]
    gates = jnp.transpose(gates.reshape(channels, wide, -1), (1, 0, 2))
    return share, lax.psum_scatter(gates, "wide", scatter_dimension=0, tiled=True)[0]


def split_top(shares, owned, channels):
    if len(shares) == 1:
        count = shares[0].shape[0] - channels
        gates = shares[0][count:]
    else:
        count = shares[0].shape[0]
        gates = shares[1]
    pieces = shares[0][:count].reshape(-1, owned, channels)
    pieces = jnp.transpose(pieces, (0, 2, 1))
    return pieces[0], pieces[1], pieces[2:].reshape(-1, owned), gates


def per_device(
    latents,
    cotangent,
    bucket,
    pixel_mask,
    labels,
    timesteps,
    gain_first,
    conv_first,
    time_proj,
    gain_second,
    conv_second,
    gain_spatial,
    proj_in,
    gain_attn,
    attn_qkv,
    attn_out,
    class_table,
    cross_value,
    cross_out,
    gain_ff,
    geglu_in,
    geglu_out,
    proj_out,
):
    images, local_pix, channels = latents.shape
    row_start = lax.axis_index("narrow") * local_pix
    keep_all = pixel_mask.astype(jnp.float32)
    pixel_keep = lax.dynamic_slice_in_dim(keep_all, row_start, local_pix, 1)[0, :, None]
    counts = jnp.sum(keep_all, axis=1) * (channels // GROUPS)
    row_width = jnp.where(bucket[0] == 0, LONG, SHORT).astype(jnp.int32)
    width = row_width[None]
    meta = pixel_meta(keep_all[0], row_start, local_pix, row_width)
    pixels = latents[0]
    skip = cotangent[0]
    pixel_halo, skip_halo = edge_rows(pixels, skip)
    half_dim = time_proj.shape[0] // 2
    frequency = jnp.exp(-math.log(10000.0) * jnp.arange(half_dim, dtype=jnp.float32) / half_dim)
    angles = timesteps.astype(jnp.float32)[:, None] * frequency[None, :]
    time_act = jax.nn.silu(jnp.concatenate([jnp.cos(angles), jnp.sin(angles)], axis=1))
    time_term = jnp.dot(time_act, time_proj.astype(jnp.float32), precision=HIGH)
    label_hot = (
        labels[:, None] == jnp.arange(class_table.shape[0], dtype=jnp.int32)[None, :]
    ).astype(jnp.float32)
    context = jnp.dot(label_hot, class_table.astype(jnp.float32), precision=HIGH)
    value_weight = cross_value.astype(jnp.float32)
    cross_weight = cross_out.astype(jnp.float32)
    value_term = jnp.dot(context, value_weight, precision=HIGH)
    cross_term = jnp.dot(value_term, cross_weight, precision=HIGH)
    gain_one = gain_first.astype(jnp.float32)
    gain_two = gain_second.astype(jnp.float32)
    gain_three = gain_spatial.astype(jnp.float32)
    image_in = pixels.astype(jnp.float32)
    kept = image_in * pixel_keep
    sums_one = jnp.stack([jnp.sum(kept, axis=0), jnp.sum(kept * image_in, axis=0)])
    center_one, scale_one = group_moments(sums_one, counts)
    hidden, sums_two = conv_forward(
        width,
        pixels,
        pixel_halo,
        meta,
        row_table(center_one, scale_one, gain_one),
        conv_first,
        row_table(time_term[0]),
    )
    (hidden_halo,) = edge_rows(hidden)
    center_two, scale_two = group_moments(sums_two[:2], counts)
    residual, sums_three = conv_forward(
        width,
        hidden,
        hidden_halo,
        meta,
        row_table(center_two, scale_two, gain_two),
        conv_second,
        pixels,
    )
    center_three, scale_three = group_moments(sums_three[:2], counts)
    residual_hat = (residual - center_three) * scale_three
    spatial = (pixel_keep * residual_hat * gain_three).astype(jnp.bfloat16)[None]
    stream = jnp.einsum("npc,cd->npd", spatial, proj_in, preferred_element_type=jnp.float32)
    normed_attn, attn_pull = jax.vjp(layer_norm, stream, gain_attn.astype(jnp.float32))
    normed_attn = normed_attn.astype(jnp.bfloat16)
    packed_f = jnp.einsum("npc,cd->npd", normed_attn, attn_qkv, preferred_element_type=jnp.float32)
    query_pix = (packed_f[0, :, :channels] * (1.0 / (math.sqrt(HEAD_DIM) * LN2))).astype(bf16)
    pad_pix = -local_pix % QB
    query_pix = jnp.pad(query_pix, ((0, pad_pix), (0, 0)))
    query_t = query_pix.T
    key_value = packed_f[0, :, channels:].astype(bf16)
    count = lax.axis_size("narrow")
    position = lax.axis_index("narrow")
    chunks = [key_value] + [None] * (count - 1)
    for bit in axis_bits("narrow"):
        chunks[bit] = swap(key_value, bit)
    keep_chunk = lambda index: lax.dynamic_slice_in_dim(
        keep_all[0], (position ^ index) * local_pix, local_pix, 0
    )
    keeps = [keep_chunk(index) for index in range(count)]
    aug_of = lambda indices: key_aug(jnp.concatenate([keeps[index] for index in indices]))
    state = attend_some(True, count == 2, query_t, chunks[:2], aug_of([0, 1]), ())
    for index in range(2, count):
        bit = low_bit(index)
        if index != bit:
            chunks[index] = swap(chunks[index ^ bit], bit)
        elif index < count - 1:
            chunks[index], state = lax.optimization_barrier((chunks[index], state))
    for index in range(2, count):
        state = attend_some(
            False, index == count - 1, query_t, [chunks[index]], aug_of([index]), state
        )
    heads_t, log_rows = state
    output, grad_mid, grad_rows, grad_t, top_grads, gate_grads, mid_sums = mid_layer(
        heads_t,
        stream[0],
        residual,
        skip,
        row_table(cross_term[0], gain_ff.astype(jnp.float32)),
        attn_out,
        geglu_in,
        geglu_out,
        proj_out,
    )
    owned = channels // lax.axis_size("wide")
    shares = top_shares(top_grads, gate_grads)
    grad_query_t = None
    totals = [None] * count
    arrived = [None] * count
    calls = [[count - 1]] + [[last - 1, last] for last in range(count - 2, 0, -2)] + [[0]]
    for call in calls:
        grad_query_t, *parts = attend_back_some(
            call[0] == count - 1,
            [bf16 if index % 2 else f32 for index in call],
            query_t,
            query_pix,
            grad_t,
            grad_rows,
            log_rows,
            heads_t,
            [chunks[index] for index in call],
            aug_of(call),
            grad_query_t,
        )
        for index, total in zip(call, parts):
            for source in range(index + 1, count):
                if source ^ low_bit(source) == index:
                    total = total + arrived[source].astype(f32)
            if index:
                arrived[index] = swap(total.astype(bf16), low_bit(index))
            totals[index] = total
    total = totals[0]
    grad_packed = jnp.concatenate(
        [
            grad_query_t.T[:local_pix].astype(bf16),
            total[0].astype(bf16),
            total[1].astype(bf16),
        ],
        axis=1,
    )[None]
    shares, grad_packed = lax.optimization_barrier((shares, grad_packed))
    grad_attn_whole = jnp.einsum(
        "npc,npd->dc", normed_attn, grad_packed, preferred_element_type=jnp.float32
    )
    grad_normed_attn = jnp.einsum(
        "npd,cd->npc", grad_packed, attn_qkv, preferred_element_type=jnp.float32
    )
    grad_from_attn, grad_gain_attn = attn_pull(grad_normed_attn)
    grad_stream = (grad_mid[None] + grad_from_attn).astype(jnp.bfloat16)
    grad_proj_in = jnp.einsum(
        "npc,npd->dc", spatial, grad_stream, preferred_element_type=jnp.float32
    )
    grad_spatial = jnp.einsum(
        "npd,cd->npc", grad_stream, proj_in, preferred_element_type=jnp.float32
    )
    grad_spatial = grad_spatial[0]
    query_key = by_owner(grad_attn_whole[: 2 * channels], owned)
    low_parts = jnp.stack(
        [
            grad_proj_in,
            query_key[:, :channels],
            query_key[:, channels:],
            grad_attn_whole[2 * channels :],
        ]
    ).astype(bf16)
    grad_halo, residual_halo = edge_rows(grad_spatial, residual)
    kept = grad_spatial * pixel_keep
    sums = jnp.stack([jnp.sum(kept, axis=0), jnp.sum(kept * residual_hat, axis=0)])
    means, early_rows = group_means(
        sums, gain_three, counts, [mid_sums[0], mid_sums[1], grad_gain_attn]
    )
    pixel_shape = (local_pix, channels)
    stack_shape = ((local_pix + 2 * LONG, 3 * channels), bf16)
    sum_shape = ((8, channels), f32)
    lanes = pack_width(conv_second)
    flops = 2 * local_pix * conv_second.size
    rows_back = row_table(
        center_three,
        scale_three,
        gain_three,
        means[0],
        means[1],
        center_two,
        scale_two,
        gain_two,
    )
    grad_res, stack_second, grad_pre, sums = conv_call(
        pull_first_kernel,
        "conv_pull",
        width,
        [grad_spatial, *grad_halo, residual, *residual_halo, skip, *skip_halo]
        + [hidden, meta, rows_back, conv_second],
        [(pixel_shape, f32), stack_shape, (pixel_shape, f32), sum_shape],
        flops,
    )
    (grad_halo,) = edge_rows(grad_pre)
    means, middle_rows = group_means(sums[:2], gain_two, counts)
    shares = [narrow_finish(share) for share in shares]
    shares, stack_second = lax.optimization_barrier((shares, stack_second))
    (pack_second,) = conv_call(
        weight_after_kernel,
        "conv_weight",
        width,
        [stack_second, hidden, meta, rows_back, low_parts],
        [((count, channels, lanes + channels), bf16)],
        flops,
    )
    rows_back = row_table(
        center_two,
        scale_two,
        gain_two,
        means[0],
        means[1],
        center_one,
        scale_one,
        gain_one,
    )
    bits = axis_bits("narrow")
    held_second = pack_second
    for bit in bits[:-1]:
        held_second = halve_step(held_second, bit, "narrow")
    stack_first, pack_first, hidden_sums = conv_call(
        weight_first_kernel,
        "conv_weight",
        width,
        [grad_pre, *grad_halo, hidden, *hidden_halo, pixels, meta, rows_back],
        [stack_shape, ((count, channels, lanes), bf16), sum_shape],
        flops,
    )
    held_first = pack_first
    for bit in bits[:-1]:
        held_first = halve_step(held_first, bit, "narrow")
    held_second, stack_first = lax.optimization_barrier((held_second, stack_first))
    held_second = halve_step(held_second, bits[-1], "narrow")
    grad_pre, sums = conv_call(
        pull_after_kernel,
        "conv_pull",
        width,
        [stack_first, pixels, meta, rows_back, conv_first],
        [(pixel_shape, f32), sum_shape],
        flops,
    )
    held_second, held_first, sums = lax.optimization_barrier((held_second, held_first, sums))
    held_first = halve_step(held_first, bits[-1], "narrow")
    means, late_rows = group_means(sums[:2], gain_one, counts, [hidden_sums[0]])
    image_hat = (image_in - center_one) * scale_one
    grad_image = grad_pre * pixel_keep * gain_one - means[0] - image_hat * means[1]
    grad_latents = (grad_res + pixel_keep * scale_one * grad_image).astype(jnp.bfloat16)[None]
    conv_rows = conv_first.shape[0]
    wide_bits = axis_bits("wide")
    part_first = halve_step(wide_split(held_first[0]), wide_bits[0], "wide")
    part_second = wide_split(held_second[0])
    part_first, late_rows, part_second = lax.optimization_barrier(
        (part_first, late_rows, part_second)
    )
    for bit in wide_bits[1:]:
        part_first = halve_step(part_first, bit, "wide")
    part_second = halve(part_second, "wide")
    whole_second = narrow_gather(part_second)
    sum_conv_second = conv_finish(whole_second[:, :, :lanes], conv_rows)
    low_whole = jnp.transpose(whole_second[:, :, lanes:], (0, 2, 1)).astype(f32)
    sum_proj_out, sum_attn_out, sum_geglu_out, sum_geglu_in = split_top(shares, owned, channels)
    sum_conv_first = conv_finish(narrow_gather(part_first[0]), conv_rows)
    stamp_row = jnp.pad(
        jnp.concatenate([labels, timesteps]).astype(f32), (0, channels - 2 * images)
    )
    spread = double(
        jnp.stack(
            [
                early_rows[2],
                late_rows[2],
                early_rows[3],
                early_rows[4],
                early_rows[1],
                middle_rows[1],
                late_rows[1],
                stamp_row,
            ]
        ),
        "wide",
    )
    labels_all = spread[:, 7, 0].astype(jnp.int32)
    steps_all = spread[:, 7, 1].astype(jnp.int32)
    angles_all = steps_all.astype(jnp.float32)[:, None] * frequency[None, :]
    time_all = jax.nn.silu(jnp.concatenate([jnp.cos(angles_all), jnp.sin(angles_all)], axis=1))
    hot_all = (
        labels_all[:, None] == jnp.arange(class_table.shape[0], dtype=jnp.int32)[None, :]
    ).astype(jnp.float32)
    context_all = jnp.dot(hot_all, class_table.astype(jnp.float32), precision=HIGH)
    value_all = jnp.dot(context_all, value_weight, precision=HIGH)
    cross_all = spread[:, 0]
    grad_value_all = jnp.dot(cross_all, cross_weight.T, precision=HIGH)
    grad_context_all = jnp.dot(grad_value_all, value_weight.T, precision=HIGH)
    sum_cross_out = jnp.dot(value_all.T, own_columns(cross_all), precision=HIGH)
    sum_cross_value = jnp.dot(context_all.T, own_columns(grad_value_all), precision=HIGH)
    sum_class_table = jnp.dot(hot_all.T, own_columns(grad_context_all), precision=HIGH)
    sum_time_proj = jnp.dot(time_all.T, own_columns(spread[:, 1]), precision=HIGH)
    gain_sums = own_columns(jnp.sum(spread[:, 2:7], axis=0))
    return (
        output[None],
        grad_latents,
        gain_sums[4],
        sum_conv_first,
        sum_time_proj,
        gain_sums[3],
        sum_conv_second,
        gain_sums[2],
        low_whole[0],
        gain_sums[1],
        jnp.concatenate([low_whole[1], low_whole[2]], axis=1),
        low_whole[3],
        sum_attn_out,
        sum_class_table,
        sum_cross_value,
        sum_cross_out,
        gain_sums[0],
        sum_geglu_in,
        sum_geglu_out,
        sum_proj_out,
    )


def solution(mesh):
    placed = (
        P("wide", "narrow", None),
        P("wide", "narrow", None),
        P("wide"),
        P("wide", None),
        P("wide"),
        P("wide"),
        P(),
        P(),
        P(),
        P(),
        P(),
        P(),
        P(),
        P(),
        P(),
        P(),
        P(),
        P(),
        P(),
        P(),
        P(),
        P(),
        P(),
    )
    return jax.shard_map(
        per_device,
        mesh=mesh,
        in_specs=placed,
        out_specs=(
            P("wide", "narrow", None),
            P("wide", "narrow", None),
            P("wide"),
            P(None, "wide"),
            P(None, "wide"),
            P("wide"),
            P(None, "wide"),
            P("wide"),
            P(None, "wide"),
            P("wide"),
            P(None, "wide"),
            P(None, "wide"),
            P(None, "wide"),
            P(None, "wide"),
            P(None, "wide"),
            P(None, "wide"),
            P("wide"),
            P(None, "wide"),
            P(None, "wide"),
            P(None, "wide"),
        ),
        check_vma=False,
    )
```
